32 devices in a mesh: dp: 16 (over z, y, x), tensor: 2 (over core).
Axes of the slice: x: 2, y: 2, z: 4, core: 2. Of those that a mesh axis runs over, the one named last changes fastest.
Arguments:
- layer_in: bfloat16 [32, 584, 1024], P('dp', 'tensor'), may hold values from -6 to 6
- out_grad: bfloat16 [32, 584, 1024], P('dp', 'tensor'), may hold values from -6 to 6
- key_valid: int32 [32, 584], P('dp'), may hold values from 0 to 1, as said below
- image_live: int32 [32], P('dp'), may hold values 0 or 1
- w_qkv: bfloat16 [3, 1024, 1024], P(None, 'dp', 'tensor'), may hold values from -0.1875 to 0.1875
- w_out: bfloat16 [1024, 1024], P('tensor', 'dp'), may hold values from -2 to 2
- w_fc1: bfloat16 [1024, 4096], P('dp', 'tensor'), may hold values from -0.1875 to 0.1875
- w_fc2: bfloat16 [4096, 1024], P('tensor', 'dp'), may hold values from -0.09375 to 0.09375
- norm_gains: bfloat16 [2, 1024], P(None, 'dp'), may hold values from 0.5 to 1.5
- bias_rows: bfloat16 [6, 1024], P(None, 'dp'), may hold values from -1.1953125 to 1.1953125
- fc_bias: bfloat16 [4096], P('dp'), may hold values from -1.796875 to 1.796875
Outputs:
- layer_out: bfloat16 [32, 584, 1024], P('dp', 'tensor')
- input_grad: bfloat16 [32, 584, 1024], P('dp', 'tensor')
- grad_w_qkv: float32 [3, 1024, 1024], P(None, 'dp', 'tensor')
- grad_w_out: float32 [1024, 1024], P('tensor', 'dp')
- grad_w_fc1: float32 [1024, 4096], P('dp', 'tensor')
- grad_w_fc2: float32 [4096, 1024], P('tensor', 'dp')
- grad_vectors: float32 [8, 1024], P(None, ('dp', 'tensor'))
- grad_fc_bias: float32 [4096], P(('dp', 'tensor'))
The draws below stay inside these ranges and needn't reach their ends.
Inputs may be any that keep to these rules, and one draw needn't show every extreme that they name: `key_valid`: key 0 of every image is 1, and every key at a position of 577 or more is 0.
All inputs are finite; a program needn't handle non-finite values. No bound on the sum of `image_live` on one device may be relied on, other than what follows from the above.
Results may differ from the reference program's by a relative error of at most 0.015.
Values may be sent and summed in bfloat16 or wider, within the bound.
A program may use at most 256 MiB of HBM per device.

```python
import jax
import jax.numpy as jnp
from jax import lax

D = 1024
HEADS = 16
HEAD_DIM = 64
FF = 4096
SEQ = 584
REAL_TOK = 577
IMAGES = 32


def draw_key_valid(key, part):
    position = lax.broadcasted_iota(jnp.int32, (IMAGES, SEQ), 1)
    kept = jax.random.randint(key, (IMAGES, SEQ), 0, 8) < 7
    usable = (position < REAL_TOK) & ((position == 0) | kept)
    return jnp.where(usable, 1, 0).astype(jnp.int32)


def set_ends(values, stream_key, smallest, top_value):
    dims = values.shape
    spot = [jax.random.randint(jax.random.fold_in(stream_key, axis), (), 0, dims[axis]) for axis in range(len(dims))]
    values = values.at[tuple(spot)].set(smallest)
    longest = dims.index(max(dims))
    spot[longest] = (spot[longest] + 1) % dims[longest]
    return values.at[tuple(spot)].set(top_value)


def strengthened(values, own_key, source, target, parts, factor):
    def block_of(axis_at):
        return (jnp.arange(values.shape[axis_at]) // (values.shape[axis_at] // parts)).reshape((-1,) + (1,) * (values.ndim - 1 - axis_at))

    one_side = jax.random.permutation(own_key, parts)[block_of(target)]
    other_side = (block_of(target) + parts // 2) % parts
    return jnp.where((block_of(source) == one_side) | (block_of(source) == other_side), factor * values, values)


def shard_levels(rng, dims, split, least, top_value):
    def one(axis_at, blocks):
        draws = jax.random.uniform(jax.random.fold_in(jax.random.fold_in(rng, 6), axis_at), (blocks,), jnp.float32, least / len(split), top_value / len(split))
        return jnp.repeat(jnp.exp(draws), dims[axis_at] // blocks).reshape((-1,) + (1,) * (len(dims) - axis_at - 1))

    level = one(*split[0])
    for cut in split[1:]:
        level = level * one(*cut)
    return level


def gaussian(rng, extent, width, most, shards=(), dtype=jnp.bfloat16):
    array = width * jax.random.normal(rng, extent, jnp.float32)
    if shards:
        array = array * shard_levels(rng, extent, shards, -0.22, 0.18)
    return jnp.clip(array, -most, most).astype(dtype)


def noise_with(stream_key, dims, deviation, most, pieces, heavy, kind=jnp.bfloat16):
    entries = deviation * jax.random.normal(stream_key, dims, jnp.float32)
    if pieces:
        entries = entries * shard_levels(stream_key, dims, pieces, -0.22, 0.18)
    return jnp.clip(strengthened(entries, jax.random.fold_in(stream_key, 3), *heavy), -most, most).astype(kind)


def setup_inputs(seed: int = 0) -> dict:
    seeds = jax.random.split(jax.random.key(seed), 12)
    layer_in = gaussian(seeds[0], (IMAGES, SEQ, D), 1.0, 6.0, ((0, 16), (1, 2)))
    out_grad = noise_with(seeds[1], (IMAGES, SEQ, D), 1.0, 6.0, ((0, 16), (1, 2)), (0, 2, 16, 2.0))
    key_valid = draw_key_valid(jax.random.fold_in(seeds[11], 71), 0)
    image_live = set_ends((jax.random.randint(seeds[3], (IMAGES,), 0, 4) < 3).astype(jnp.int32), jax.random.fold_in(seeds[3], 1), 0, 1)
    w_qkv = gaussian(seeds[4], (3, D, D), D ** -0.5, 0.1875, ((1, 16), (2, 2)))
    w_out = gaussian(seeds[5], (D, D), (max(4 * D // REAL_TOK, 1)) ** -0.5, 2.0, ((0, 2), (1, 16)))
    w_fc1 = gaussian(seeds[6], (D, FF), D ** -0.5, 0.1875, ((0, 16), (1, 2)))
    w_fc2 = gaussian(seeds[7], (FF, D), FF ** -0.5, 0.09375, ((0, 2), (1, 16)))
    norm_gains = jnp.clip(1.0 + 0.1 * jax.random.normal(seeds[8], (2, D), jnp.float32), 0.5, 1.5).astype(jnp.bfloat16)
    bias_rows = gaussian(seeds[9], (6, D), 0.2, 1.1953125, ((1, 16),))
    fc_bias = gaussian(seeds[10], (FF,), 0.3, 1.796875, ((0, 16),))
    return dict(layer_in=layer_in, out_grad=out_grad, key_valid=key_valid, image_live=image_live, w_qkv=w_qkv, w_out=w_out, w_fc1=w_fc1, w_fc2=w_fc2, norm_gains=norm_gains, bias_rows=bias_rows, fc_bias=fc_bias)


@jax.custom_vjp
def low(v):
    return lax.optimization_barrier(v.astype(jnp.bfloat16)).astype(jnp.float32)

@jax.custom_vjp
def low_back(v):
    return v

def low_keep(v):
    return (low(v), None)

def low_pass(kept, grad):
    return (grad,)

def back_keep(v):
    return (v, None)

def back_low(kept, grad):
    return (low(grad),)
low.defvjp(low_keep, low_pass)
low_back.defvjp(back_keep, back_low)

def layer_norm(values, gain_row, shift_row):
    centred = values - lax.optimization_barrier(jnp.mean(values, axis=-1, keepdims=True))
    spread = lax.optimization_barrier(jnp.mean(centred * centred, axis=-1, keepdims=True))
    return centred * lax.rsqrt(spread + 1e-05) * gain_row + shift_row

def rounded_both(values):
    return low_back(low(values))

def one_layer(tokens, w_qkv, w_out, w_fc1, w_fc2, norm_gains, bias_rows, fc_bias, valid_row):
    highest = lax.Precision.HIGHEST
    first = low(layer_norm(tokens, norm_gains[0], bias_rows[0]))
    mixed_rows = jnp.einsum('sd,cde->cse', first, w_qkv, precision=highest)
    queries = rounded_both(mixed_rows[0] + bias_rows[1]).reshape(SEQ, HEADS, HEAD_DIM)
    key_rows = rounded_both(mixed_rows[1]).reshape(SEQ, HEADS, HEAD_DIM)
    value_rows = rounded_both(mixed_rows[2] + bias_rows[2]).reshape(SEQ, HEADS, HEAD_DIM)
    raw_scores = low_back(jnp.einsum('qhd,khd->hqk', queries, key_rows, precision=highest))
    scores = jnp.where(valid_row[None, None, :] > 0, raw_scores * HEAD_DIM ** (-0.5), -1000000000.0)
    attn_probs = jax.nn.softmax(scores, axis=-1)
    attended = jnp.einsum('hqk,khd->qhd', low(attn_probs), value_rows, precision=highest).reshape(SEQ, D)
    attended = rounded_both(attended)
    middle = tokens + low_back(jnp.dot(attended, w_out, precision=highest) + bias_rows[3])
    second = low(layer_norm(middle, norm_gains[1], bias_rows[4]))
    hidden = low_back(jnp.dot(second, w_fc1, precision=highest) + fc_bias)
    activated = low(hidden * jax.nn.sigmoid(1.702 * hidden))
    return middle + low_back(jnp.dot(activated, w_fc2, precision=highest) + bias_rows[5])

def reference(layer_in, out_grad, key_valid, image_live, w_qkv, w_out, w_fc1, w_fc2, norm_gains, bias_rows, fc_bias):
    weights = tuple((source.astype(jnp.float32) for source in (w_qkv, w_out, w_fc1, w_fc2, norm_gains, bias_rows, fc_bias)))

    def image_step(running, sample):
        tokens, grad_rows, valid_row, live_flag = sample

        def forward(token_rows, *weight_args):
            return one_layer(token_rows, *weight_args, valid_row)
        result, pullback = jax.vjp(forward, tokens.astype(jnp.float32), *weights)
        gradients = pullback(grad_rows.astype(jnp.float32) * live_flag.astype(jnp.float32))
        running = tuple((before + added for before, added in zip(running, gradients[1:])))
        return (running, (result.astype(jnp.bfloat16), gradients[0].astype(jnp.bfloat16)))
    initial = tuple((jnp.zeros_like(source) for source in weights))
    totals, (layer_out, input_grad) = lax.scan(image_step, initial, (layer_in, out_grad, key_valid, image_live))
    qkv_total, out_total, fc1_total, fc2_total, gain_total, shift_total, fcb_total = totals
    vectors = jnp.stack([gain_total[0], shift_total[0], shift_total[1], shift_total[2], shift_total[3], gain_total[1], shift_total[4], shift_total[5]])
    return (layer_out, input_grad, qkv_total, out_total, fc1_total, fc2_total, vectors, fcb_total)
```

```python
import functools

import jax
import jax.numpy as jnp
from jax import lax
from jax.experimental import pallas as pl
from jax.experimental.pallas import tpu as pltpu
from jax.sharding import PartitionSpec as P

MESH = pl.DeviceIdType.MESH

D = 1024
HEAD_DIM = 64
FF = 4096


EPSILON = 1e-05


def norm_forward(values, gain_row, shift_row):
    centred = values - jnp.mean(values, axis=-1, keepdims=True)
    inverse = lax.rsqrt(jnp.mean(centred * centred, axis=-1, keepdims=True) + EPSILON)
    normed = centred * inverse
    return (normed * gain_row + shift_row, normed, inverse)


def norm_backward(upstream, normed, inverse, gain_row):
    scaled = upstream * gain_row
    return inverse * (
        scaled
        - jnp.mean(scaled, axis=-1, keepdims=True)
        - normed * jnp.mean(scaled * normed, axis=-1, keepdims=True)
    )


def pair_slice(source, pair_index):
    pair_width = 2 * HEAD_DIM
    sliced = lax.dynamic_slice_in_dim(source, pair_index * pair_width, pair_width, 2)
    return sliced.reshape(sliced.shape[0], sliced.shape[1], 2, HEAD_DIM)


def pair_scores(query_block, key_block, valid_keys, score_scale):
    scores = (
        jnp.einsum("bqhd,bkhd->bhqk", query_block, key_block, preferred_element_type=jnp.float32)
        * score_scale
    )
    return jnp.where(valid_keys[:, None, None, :], scores, -1000000000.0)


def join_pairs(stacked):
    pair_count, batch_size, seq_length, pair_width = stacked.shape
    return jnp.transpose(stacked, (1, 2, 0, 3)).reshape(
        batch_size, seq_length, pair_count * pair_width
    )


def attend_forward(queries, key_rows, value_rows, valid_keys, score_scale):
    batch_size, seq_length, local_cols = queries.shape
    pair_count = local_cols // (2 * HEAD_DIM)

    def one_pair(pair_index):
        scores = pair_scores(
            pair_slice(queries, pair_index),
            pair_slice(key_rows, pair_index),
            valid_keys,
            score_scale,
        )
        row_max = jnp.max(scores, axis=-1, keepdims=True)
        expons = jnp.exp(scores - row_max)
        row_total = jnp.sum(expons, axis=-1, keepdims=True)
        attn_probs = (expons / row_total).astype(jnp.bfloat16)
        mixed_rows = jnp.einsum(
            "bhqk,bkhd->bqhd",
            attn_probs,
            pair_slice(value_rows, pair_index),
            preferred_element_type=jnp.float32,
        )
        mixed_rows = mixed_rows.reshape(batch_size, seq_length, 2 * HEAD_DIM).astype(jnp.bfloat16)
        return (mixed_rows, (row_max + jnp.log(row_total))[..., 0])

    blocks, log_totals = lax.map(one_pair, jnp.arange(pair_count))
    return (join_pairs(blocks), log_totals)


def attend_backward(
    queries, key_rows, value_rows, attended_grad, log_totals, valid_keys, score_scale
):
    batch_size, seq_length, local_cols = queries.shape
    pair_count = local_cols // (2 * HEAD_DIM)

    def one_pair(inputs):
        pair_index, pair_totals = inputs
        query_block = pair_slice(queries, pair_index)
        key_block = pair_slice(key_rows, pair_index)
        value_block = pair_slice(value_rows, pair_index)
        grad_block = pair_slice(attended_grad, pair_index)
        scores = pair_scores(query_block, key_block, valid_keys, score_scale)
        attn_probs = jnp.exp(scores - pair_totals[..., None])
        prob_grad = jnp.einsum(
            "bqhd,bkhd->bhqk", grad_block, value_block, preferred_element_type=jnp.float32
        )
        centre = jnp.sum(attn_probs * prob_grad, axis=-1, keepdims=True)
        score_grad = (attn_probs * (prob_grad - centre) * score_scale).astype(jnp.bfloat16)
        query_grad = jnp.einsum(
            "bhqk,bkhd->bqhd", score_grad, key_block, preferred_element_type=jnp.float32
        )
        key_grad = jnp.einsum(
            "bhqk,bqhd->bkhd", score_grad, query_block, preferred_element_type=jnp.float32
        )
        value_grad = jnp.einsum(
            "bhqk,bqhd->bkhd",
            attn_probs.astype(jnp.bfloat16),
            grad_block,
            preferred_element_type=jnp.float32,
        )
        return tuple(
            (
                member.reshape(batch_size, seq_length, 2 * HEAD_DIM).astype(jnp.bfloat16)
                for member in (query_grad, key_grad, value_grad)
            )
        )

    grad_parts = lax.map(one_pair, (jnp.arange(pair_count), log_totals))
    return tuple((join_pairs(member) for member in grad_parts))


class Place:
    def __init__(self):
        dp=lax.axis_index("dp"); self.c=lax.axis_index("tensor")
        self.dp=dp; self.z=dp//4; self.y=(dp//2)%2; self.x=dp%2
    def dev(self, d):
        if d=="x": t=self.dp+1-2*self.x
        elif d=="y": t=self.dp+2-4*self.y
        elif d=="u": t=self.dp+4
        elif d=="d": t=self.dp-4
        return (t,self.c)
    def greet(self):
        bar=pltpu.get_barrier_semaphore()
        for d in "xy": pl.semaphore_signal(bar,inc=1,device_id=self.dev(d),device_id_type=MESH)
        pl.semaphore_signal(bar,inc=1,device_id=(self.dp,1-self.c),device_id_type=MESH)
        @pl.when(self.z<3)
        def _(): pl.semaphore_signal(bar,inc=1,device_id=self.dev("u"),device_id_type=MESH)
        @pl.when(self.z>0)
        def _(): pl.semaphore_signal(bar,inc=1,device_id=self.dev("d"),device_id_type=MESH)
        @pl.when((self.z==0)|(self.z==3))
        def _(): pl.semaphore_wait(bar,4)
        @pl.when((self.z>0)&(self.z<3))
        def _(): pl.semaphore_wait(bar,5)

class Scatter:
    def __init__(self, pc, G, R1, R2, RZ, R3, out, s1, s2, sz, s3, ss):
        self.pc=pc; self.G,self.R1,self.R2,self.RZ,self.R3,self.out=G,R1,R2,RZ,R3,out
        self.s1,self.s2,self.sz,self.s3,self.ss=s1,s2,sz,s3,ss
    def order(self, s): return ("x","y") if s%2==0 else ("y","x")
    def kinds(self, s):
        return (3*s+1,"y","x"),(3*s+2,"x","y")
    def copy(self, src, dst, d, rsem):
        si={"x":0,"y":1,"u":2,"d":3}[d]
        return pltpu.make_async_remote_copy(src_ref=src,dst_ref=dst,send_sem=self.ss.at[si],recv_sem=rsem,device_id=self.pc.dev(d),device_id_type=MESH)
    def wait(self, ref, sem): pltpu.make_async_copy(ref,ref,sem).wait()
    def pair(self, p, t, d, other):
        pc=self.pc
        if d=="y": return self.G.at[p,t,(1-pc.y) if other else pc.y]
        return self.G.at[p,t,:,(1-pc.x) if other else pc.x]
    def one(self, p, t, flip=None):
        pc=self.pc
        return self.G.at[p,t,(1-pc.y) if flip=="y" else pc.y,(1-pc.x) if flip=="x" else pc.x]
    def each(self, dist, fn):
        z=self.pc.z
        if dist==0: fn(z,None); return
        @pl.when(z+dist<=3)
        def _(): fn(z+dist,"u")
        @pl.when(z-dist>=0)
        def _(): fn(z-dist,"d")
    def r0(self, s):
        for p,d in [(3*s,self.order(s)[1])]+[(p,a) for p,a,b in self.kinds(s)]:
            for dist in (3,2,1,0):
                self.each(dist, lambda t,_: self.copy(self.pair(p,t,d,True),self.R1.at[p,t],d,self.s1.at[p,t]).start())
    def acc(self, dst, *others):
        v=dst[...].astype(jnp.float32)
        for o in others: v=v+o[...].astype(jnp.float32)
        dst[...]=v.astype(jnp.bfloat16)
    def r1(self, s, dists=(3,2,1,0)):
        p=3*s; d1,d2=self.order(s)
        for dist in dists:
            def go(t,_):
                self.wait(self.R1.at[p,t],self.s1.at[p,t])
                self.acc(self.pair(p,t,d2,False),self.R1.at[p,t])
                self.copy(self.one(p,t,d1),self.R2.at[s,t],d1,self.s2.at[s,t]).start()
            self.each(dist,go)
    def line(self, p, view, slot, pre, dist, own):
        z=self.pc.z
        def go(t,way):
            pre(t)
            if way=="u":
                @pl.when(z>0)
                def _():
                    self.wait(slot(t+1),self.sz.at[p,t+1]); self.acc(view(t),slot(t+1))
                self.copy(view(t),slot(t+1),"u",self.sz.at[p,t+1]).start()
            elif way=="d":
                @pl.when(z<3)
                def _():
                    self.wait(slot(t),self.sz.at[p,t]); self.acc(view(t),slot(t))
                self.copy(view(t),slot(t),"d",self.sz.at[p,t]).start()
            else:
                @pl.when(z>0)
                def _():
                    self.wait(slot(z+1),self.sz.at[p,z+1]); self.acc(view(z),slot(z+1))
                @pl.when(z<3)
                def _():
                    self.wait(slot(z),self.sz.at[p,z]); self.acc(view(z),slot(z))
                own()
        self.each(dist,go)
    def rxy(self, s, dist):
        for p,a,b in self.kinds(s):
            view=lambda t: self.pair(p,t,a,False)
            def pre(t):
                self.wait(self.R1.at[p,t],self.s1.at[p,t]); self.acc(view(t),self.R1.at[p,t])
            def own(): self.copy(self.one(p,self.pc.z,b),self.R3.at[p],b,self.s3.at[p]).start()
            self.line(p,view,lambda i: self.RZ.at[p,i],pre,dist,own)
    def rz(self, s, dist):
        p=3*s
        def pre(t):
            self.wait(self.R2.at[s,t],self.s2.at[s,t]); self.acc(self.one(p,t),self.R2.at[s,t])
        def own():
            self.out[p]=self.one(p,self.pc.z)[...].astype(jnp.float32)
        self.line(p,lambda t: self.one(p,t),lambda i: self.RZ.at[p,i,0],pre,dist,own)
    def last(self, s):
        for p,a,b in self.kinds(s):
            self.wait(self.R3.at[p],self.s3.at[p])
            self.out[p]=self.one(p,self.pc.z)[...].astype(jnp.float32)+self.R3[p].astype(jnp.float32)
    def blocks(self,n,sem):
        while n>=16: self.wait(self.G.at[0],sem); n-=16
        while n>=4: self.wait(self.G.at[0,0],sem); n-=4
        while n: self.wait(self.G.at[0,0,0,0],sem); n-=1
    def finish(self):
        self.blocks(60,self.ss.at[0]); self.blocks(60,self.ss.at[1])
        for k in range(3):
            @pl.when(self.pc.z==k)
            def _(): self.blocks(20*(3-k),self.ss.at[2])
            @pl.when(self.pc.z==k+1)
            def _(): self.blocks(20*(k+1),self.ss.at[3])
    EVENTS=["r0","r1","xy3","xy2","z3","xy1","z2","xy0","z1","last","z0"]
    def run(self,s,e):
        if e[0]=="r": getattr(self,e)(s)
        elif e=="last": self.last(s)
        elif e[0]=="z": self.rz(s,int(e[1]))
        else: self.rxy(s,int(e[2]))

def scatter_order(off,pre):
    ev=[]
    for s in range(4):
        for i,e in enumerate(Scatter.EVENTS):
            ev.append((i+off*s-(pre if e=="r0" else 0),s,i,e))
    return [(s,e) for _,s,_,e in sorted(ev)]

def rs_kernel(order, g_ref, o_ref, G, R1,R2,RZ,R3, OUT, lsem,s1,s2,sz,s3,ss):
    pc=Place()
    cps=[pltpu.make_async_copy(g_ref.at[pl.ds(3*i,3)],G.at[pl.ds(3*i,3)],lsem.at[i]) for i in range(4)]
    for c in cps: c.start()
    pc.greet()
    sc=Scatter(pc,G,R1,R2,RZ,R3,OUT,s1,s2,sz,s3,ss)
    for s,e in order:
        if e=="r0": cps[s].wait()
        sc.run(s,e)
    cp=pltpu.make_async_copy(OUT,o_ref,lsem.at[0]); cp.start();
    sc.finish(); cp.wait()

def rs_scratch():
    B=lambda *s: pltpu.VMEM(s+(64,512),jnp.bfloat16)
    D=lambda *s: pltpu.SemaphoreType.DMA(s)
    return [B(12,4,2,2),B(12,4,2),B(4,4),B(12,5,2),B(12),pltpu.VMEM((12,64,512),jnp.float32),D(4),D(12,4),D(4,4),D(12,5),D(12),D(4)]

def rs_call(g, order, name="rs"):
    return pl.pallas_call(functools.partial(rs_kernel,order), out_shape=jax.ShapeDtypeStruct((12,64,512),jnp.float32),
        in_specs=[pl.BlockSpec(memory_space=pl.ANY)], out_specs=pl.BlockSpec(memory_space=pl.ANY),
        scratch_shapes=rs_scratch(), name=name,
        compiler_params=pltpu.CompilerParams(collective_id=1,has_side_effects=True,vmem_limit_bytes=60*2**20))(g)

class Gather:
    NS=4
    def __init__(self, wloc, wall, zs, fs, ts, ss):
        self.wloc, self.wall, self.zs, self.fs, self.ts, self.ss = wloc, wall, zs, fs, ts, ss
        dp=lax.axis_index("dp"); self.c=lax.axis_index("tensor")
        self.z=dp//4; self.y=(dp//2)%2; self.x=dp%2
        self.dp=dp
    def dev(self, d):
        if d=="x": t=self.z*4+self.y*2+(1-self.x)
        elif d=="y": t=self.z*4+(1-self.y)*2+self.x
        elif d=="u": t=self.dp+4
        else: t=self.dp-4
        return (t,self.c)
    def greet(self, bar):
        n=jnp.where((self.z==0)|(self.z==3),3,4)
        for d in "xy": pl.semaphore_signal(bar,inc=1,device_id=self.dev(d),device_id_type=MESH)
        @pl.when(self.z<3)
        def _(): pl.semaphore_signal(bar,inc=1,device_id=self.dev("u"),device_id_type=MESH)
        @pl.when(self.z>0)
        def _(): pl.semaphore_signal(bar,inc=1,device_id=self.dev("d"),device_id_type=MESH)
        return n
    def copy(self, ref, d, rsem):
        si={"x":0,"y":1,"u":2,"d":3}[d]
        return pltpu.make_async_remote_copy(src_ref=ref,dst_ref=ref,send_sem=self.ss.at[si],recv_sem=rsem,device_id=self.dev(d),device_id_type=MESH)
    def zsend(self, ref_of, p, zsrc, up, cond):
        ref=ref_of(zsrc)
        @pl.when(cond)
        def _(): self.copy(ref, "u" if up else "d", self.zs.at[p,zsrc]).start()
    def vZ(self,p): return lambda zz: self.wall.at[p,zz,self.y,self.x]
    def vXZY(self,p): return lambda zz: self.wall.at[p,zz,self.y]
    def vYZX(self,p): return lambda zz: self.wall.at[p,zz,:,self.x]
    def wait(self, ref, sem):
        pltpu.make_async_copy(ref,ref,sem).wait()
    def pieces(self, s):
        return 3*s, 3*s+1, 3*s+2
    def order(self, s):
        return ("x","y") if s%2==0 else ("y","x")
    def nb(self, d, p):
        if d=="x": return lambda zz: self.wall.at[p,zz,self.y,1-self.x]
        return lambda zz: self.wall.at[p,zz,1-self.y,self.x]
    def pair(self, d1, p):
        return self.vXZY(p) if d1=="x" else self.vYZX(p)
    def e0(self, s):
        pz,px,py=self.pieces(s); d1,d2=self.order(s); z=self.z
        self.zsend(self.vZ(pz),pz,z,True,z<3)
        self.zsend(self.vZ(pz),pz,z,False,z>0)
        self.copy(self.vZ(px)(z),"x",self.fs.at[px,0]).start()
        self.copy(self.vZ(py)(z),"y",self.fs.at[py,0]).start()
        self.copy(self.vZ(pz)(z),d1,self.fs.at[pz,z]).start()
    def e1(self, s):
        pz,px,py=self.pieces(s); z=self.z
        for p,v,d,e in ((px,self.vXZY(px),"x","y"),(py,self.vYZX(py),"y","x")):
            self.wait(self.nb(d,p)(z),self.fs.at[p,0])
            self.zsend(v,p,z,True,z<3)
            self.zsend(v,p,z,False,z>0)
            self.copy(v(z),e,self.ts.at[p]).start()
    def zarr(self, p, v, dist, then):
        z=self.z
        @pl.when(z-dist>=0)
        def _():
            src=z-dist
            self.wait(v(src),self.zs.at[p,src])
            self.zsend(v,p,src,True,z<3)
            then(src)
        @pl.when(z+dist<=3)
        def _():
            src=z+dist
            self.wait(v(src),self.zs.at[p,src])
            self.zsend(v,p,src,False,z>0)
            then(src)
    def ez(self, s, dist):
        pz,px,py=self.pieces(s); d1,d2=self.order(s); z=self.z
        if dist<=3:
            self.zarr(pz,self.vZ(pz),dist,lambda src: self.copy(self.vZ(pz)(src),d1,self.fs.at[pz,src]).start())
        def d1arr(src):
            self.wait(self.nb(d1,pz)(src),self.fs.at[pz,src])
            self.copy(self.pair(d1,pz)(src),d2,self.ts.at[pz]).start()
        if dist==1: d1arr(z)
        else:
            @pl.when(z-(dist-1)>=0)
            def _(): d1arr(z-(dist-1))
            @pl.when(z+(dist-1)<=3)
            def _(): d1arr(z+(dist-1))
    def exy(self, s, dist):
        pz,px,py=self.pieces(s)
        for p,v,e in ((px,self.vXZY(px),"y"),(py,self.vYZX(py),"x")):
            self.zarr(p,v,dist,lambda src: self.copy(v(src),e,self.ts.at[p]).start())
    def term(self, s):
        pz,px,py=self.pieces(s); d1,d2=self.order(s)
        for p,d in ((pz,d2),(px,"y"),(py,"x")):
            ref=self.wall.at[p,:,1-self.y] if d=="y" else self.wall.at[p,:,:,1-self.x]
            self.wait(ref,self.ts.at[p])
    def finish(self):
        flat=lambda n: self.wall.at[0:n//16] if n%16==0 else None
        for si in (0,1):
            self.wait(self.wall.at[0:3],self.ss.at[si]); self.wait(self.wall.at[0,0:3],self.ss.at[si])
        for k in range(3):
            @pl.when(self.z==k)
            def _():
                for _i in range(k+1):
                    self.wait(self.wall.at[0],self.ss.at[2]); self.wait(self.wall.at[0,0],self.ss.at[2])
            @pl.when(self.z==k+1)
            def _():
                for _i in range(3-k):
                    self.wait(self.wall.at[0],self.ss.at[3]); self.wait(self.wall.at[0,0],self.ss.at[3])
    EVENTS=["e0","e1","z1","xy1","z2","xy2","z3","xy3","z4","term"]
    def run(self, s, e):
        if e=="e0": self.e0(s)
        elif e=="e1": self.e1(s)
        elif e=="term": self.term(s)
        elif e[0]=="z": self.ez(s,int(e[1]))
        else: self.exy(s,int(e[2]))

def gather_order(off, pre):
    ev=[]
    for s in range(4):
        for i,e in enumerate(Gather.EVENTS):
            k = i+off*s
            if e=="e0": k=off*s-pre
            ev.append((k,s,i,e))
    ev.sort()
    return [(s,e) for k,s,i,e in ev]


def ag_kernel(order, wloc, wall, held, lsem, zs, fs, ts, ss):
    pc = Place()
    pc.greet()
    cp = pltpu.make_async_copy(wloc, held, lsem)
    cp.start()
    cp.wait()
    cp = pltpu.make_async_copy(held, wall.at[:, pc.z, pc.y, pc.x], lsem)
    cp.start()
    cp.wait()
    g = Gather(wloc, wall, zs, fs, ts, ss)
    for s, e in order:
        g.run(s, e)
    g.finish()


def ag_call(wloc, order):
    D = lambda *s: pltpu.SemaphoreType.DMA(s)
    return pl.pallas_call(
        functools.partial(ag_kernel, order),
        out_shape=jax.ShapeDtypeStruct((12, 4, 2, 2, 64, 512), jnp.bfloat16),
        in_specs=[pl.BlockSpec(memory_space=pl.ANY)],
        out_specs=pl.BlockSpec(memory_space=pl.ANY),
        scratch_shapes=[pltpu.VMEM((12, 64, 512), jnp.bfloat16), pltpu.SemaphoreType.DMA, D(12, 4), D(12, 4), D(12), D(4)],
        name="gather",
        compiler_params=pltpu.CompilerParams(collective_id=0, has_side_effects=True),
    )(wloc)

def gather_all(w_qkv, w_out, w_fc1, w_fc2, norm_gains, bias_rows, fc_bias):
    count = lax.axis_size("dp")
    local = jnp.concatenate([w_qkv, w_out.T[None], split_cols(w_fc1), split_cols(w_fc2.T)], axis=0)
    if count == 16:
        whole = ag_call(local, gather_order(2, 8)).reshape(12, D, 512)
    else:
        whole = lax.all_gather(local, "dp", axis=1, tiled=True)
    small = (
        lax.all_gather(norm_gains, "dp", axis=1, tiled=True),
        lax.all_gather(bias_rows, "dp", axis=1, tiled=True),
        lax.all_gather(fc_bias, "dp", axis=0, tiled=True),
    )
    return (whole[:3], whole[3].T, join_cols(whole[4:8]), join_cols(whole[8:12]).T), small


def split_cols(m):
    return jnp.transpose(m.reshape(m.shape[0], m.shape[1] // 512, 512), (1, 0, 2))


def join_cols(m):
    return jnp.transpose(m, (1, 0, 2)).reshape(m.shape[1], m.shape[0] * 512)


def scatter_all(grads):
    qkv, out, up, down = grads
    parts = jnp.concatenate([qkv, out.T[None], split_cols(up), split_cols(down.T)], axis=0).astype(jnp.bfloat16)
    if lax.axis_size("dp") == 16:
        mine = rs_call(parts.reshape(12, 4, 2, 2, 64, 512), scatter_order(2, 0))
    else:
        mine = lax.psum_scatter(parts, "dp", scatter_dimension=1, tiled=True).astype(jnp.float32)
    return (mine[:3], mine[3].T, join_cols(mine[4:8]), join_cols(mine[8:12]).T)


def shards(
    layer_in,
    out_grad,
    key_valid,
    image_live,
    w_qkv,
    w_out,
    w_fc1,
    w_fc2,
    norm_gains,
    bias_rows,
    fc_bias,
):
    tensor_index = lax.axis_index("tensor")
    local_width = w_qkv.shape[2]
    hidden_local = w_fc1.shape[1]
    score_scale = HEAD_DIM ** (-0.5)
    gathered = gather_all(w_qkv, w_out, w_fc1, w_fc2, norm_gains, bias_rows, fc_bias)
    outputs = []
    input_grads = []
    weight_totals = None
    vector_total = jnp.zeros((8, D), jnp.float32)
    fc_total = jnp.zeros((FF,), jnp.float32)
    zero_row = jnp.zeros((D,), jnp.float32)
    zero_hidden = jnp.zeros((FF,), jnp.float32)
    IMG_MB = layer_in.shape[0]
    for micro_step in range(1):
        first_img = 0
        tokens = layer_in[first_img : first_img + IMG_MB].astype(jnp.float32)
        live_rows = image_live[first_img : first_img + IMG_MB].astype(jnp.float32)[:, None, None]
        grad_local = out_grad[first_img : first_img + IMG_MB].astype(jnp.float32) * live_rows
        grad_low = grad_local.astype(jnp.bfloat16)
        valid_keys = key_valid[first_img : first_img + IMG_MB] > 0
        (qkv_weight, out_weight, up_weight, down_weight), (gain_rows, shift_rows, hidden_shift) = gathered
        gain_rows = gain_rows.astype(jnp.float32)
        shift_rows = shift_rows.astype(jnp.float32)
        query_bias = lax.dynamic_slice_in_dim(
            shift_rows[1], tensor_index * local_width, local_width
        )
        value_bias = lax.dynamic_slice_in_dim(
            shift_rows[2], tensor_index * local_width, local_width
        )
        hidden_bias = lax.dynamic_slice_in_dim(
            hidden_shift.astype(jnp.float32), tensor_index * hidden_local, hidden_local
        )
        first, first_normed, first_inverse = norm_forward(tokens, gain_rows[0], shift_rows[0])
        first_full = lax.all_gather(first.astype(jnp.bfloat16), "tensor", axis=1, tiled=True)
        projected = jnp.einsum(
            "bsd,cde->cbse", first_full, qkv_weight, preferred_element_type=jnp.float32
        )
        queries = (projected[0] + query_bias).astype(jnp.bfloat16)
        key_rows = projected[1].astype(jnp.bfloat16)
        value_rows = (projected[2] + value_bias).astype(jnp.bfloat16)
        attended, log_totals = attend_forward(
            queries, key_rows, value_rows, valid_keys, score_scale
        )
        attn_terms = jnp.einsum(
            "bsl,ld->bsd", attended, out_weight, preferred_element_type=jnp.float32
        )
        middle = (
            tokens
            + lax.psum_scatter(
                attn_terms.astype(jnp.bfloat16), "tensor", scatter_dimension=1, tiled=True
            ).astype(jnp.float32)
            + shift_rows[3]
        )
        second, second_normed, second_inverse = norm_forward(middle, gain_rows[1], shift_rows[4])
        second_full = lax.all_gather(second.astype(jnp.bfloat16), "tensor", axis=1, tiled=True)
        hidden = (
            jnp.einsum("bsd,df->bsf", second_full, up_weight, preferred_element_type=jnp.float32)
            + hidden_bias
        )
        gate_sig = jax.nn.sigmoid(1.702 * hidden)
        activated = (hidden * gate_sig).astype(jnp.bfloat16)
        mlp_terms = jnp.einsum(
            "bsf,fd->bsd", activated, down_weight, preferred_element_type=jnp.float32
        )
        layer_rows = (
            middle
            + lax.psum_scatter(
                mlp_terms.astype(jnp.bfloat16), "tensor", scatter_dimension=1, tiled=True
            ).astype(jnp.float32)
            + shift_rows[5]
        )
        outputs.append(layer_rows.astype(jnp.bfloat16))
        grad_full = lax.all_gather(grad_low, "tensor", axis=1, tiled=True)
        down_grad = jnp.einsum(
            "bsf,bsd->fd", activated, grad_full, preferred_element_type=jnp.float32
        )
        act_grad = jnp.einsum(
            "bsd,fd->bsf", grad_full, down_weight, preferred_element_type=jnp.float32
        )
        hidden_grad = (act_grad * (gate_sig + 1.702 * hidden * gate_sig * (1.0 - gate_sig))).astype(
            jnp.bfloat16
        )
        up_grad = jnp.einsum(
            "bsd,bsf->df", second_full, hidden_grad, preferred_element_type=jnp.float32
        )
        second_terms = jnp.einsum(
            "bsf,df->bsd", hidden_grad, up_weight, preferred_element_type=jnp.float32
        )
        second_grad = lax.psum_scatter(
            second_terms.astype(jnp.bfloat16), "tensor", scatter_dimension=1, tiled=True
        ).astype(jnp.float32)
        middle_grad = grad_local + norm_backward(
            second_grad, second_normed, second_inverse, gain_rows[1]
        )
        middle_low = middle_grad.astype(jnp.bfloat16)
        middle_full = lax.all_gather(middle_low, "tensor", axis=1, tiled=True)
        out_w_grad = jnp.einsum(
            "bsl,bsd->ld", attended, middle_full, preferred_element_type=jnp.float32
        )
        attended_grad = jnp.einsum(
            "bsd,ld->bsl", middle_full, out_weight, preferred_element_type=jnp.float32
        ).astype(jnp.bfloat16)
        query_grad, key_grad, value_grad = attend_backward(
            queries, key_rows, value_rows, attended_grad, log_totals, valid_keys, score_scale
        )
        stacked_grad = jnp.stack([query_grad, key_grad, value_grad])
        qkv_grad = jnp.einsum(
            "bsd,cbse->cde", first_full, stacked_grad, preferred_element_type=jnp.float32
        )
        first_terms = jnp.einsum(
            "cbse,cde->bsd", stacked_grad, qkv_weight, preferred_element_type=jnp.float32
        )
        first_grad = lax.psum_scatter(
            first_terms.astype(jnp.bfloat16), "tensor", scatter_dimension=1, tiled=True
        ).astype(jnp.float32)
        input_rows = middle_grad + norm_backward(
            first_grad, first_normed, first_inverse, gain_rows[0]
        )
        input_grads.append(input_rows.astype(jnp.bfloat16))
        micro_vectors = jnp.stack(
            [
                jnp.sum(first_grad * first_normed, axis=(0, 1)),
                jnp.sum(first_grad, axis=(0, 1)),
                lax.dynamic_update_slice_in_dim(
                    zero_row,
                    jnp.sum(query_grad, axis=(0, 1), dtype=jnp.float32),
                    tensor_index * local_width,
                    0,
                ),
                lax.dynamic_update_slice_in_dim(
                    zero_row,
                    jnp.sum(value_grad, axis=(0, 1), dtype=jnp.float32),
                    tensor_index * local_width,
                    0,
                ),
                jnp.sum(middle_low, axis=(0, 1), dtype=jnp.float32),
                jnp.sum(second_grad * second_normed, axis=(0, 1)),
                jnp.sum(second_grad, axis=(0, 1)),
                jnp.sum(grad_local, axis=(0, 1)),
            ]
        )
        vector_total = vector_total + micro_vectors
        fc_total = fc_total + lax.dynamic_update_slice_in_dim(
            zero_hidden,
            jnp.sum(hidden_grad, axis=(0, 1), dtype=jnp.float32),
            tensor_index * hidden_local,
            0,
        )
        micro_grads = (qkv_grad, out_w_grad, up_grad, down_grad)
        if weight_totals is None:
            weight_totals = micro_grads
        else:
            weight_totals = tuple(
                (before + added for before, added in zip(weight_totals, micro_grads))
            )
    weight_totals = scatter_all(weight_totals)
    summed_vectors, summed_hidden = (
        lax.psum_scatter(vector_total, ("dp", "tensor"), scatter_dimension=1, tiled=True),
        lax.psum_scatter(fc_total, ("dp", "tensor"), scatter_dimension=0, tiled=True),
    )
    return (
        jnp.concatenate(outputs, axis=0),
        jnp.concatenate(input_grads, axis=0),
        weight_totals[0],
        weight_totals[1],
        weight_totals[2],
        weight_totals[3],
        summed_vectors,
        summed_hidden,
    )


def solution(mesh):
    return jax.shard_map(
        shards,
        mesh=mesh,
        in_specs=(
            P("dp", "tensor", None),
            P("dp", "tensor", None),
            P("dp", None),
            P("dp"),
            P(None, "dp", "tensor"),
            P("tensor", "dp"),
            P("dp", "tensor"),
            P("tensor", "dp"),
            P(None, "dp"),
            P(None, "dp"),
            P("dp"),
        ),
        out_specs=(
            P("dp", "tensor", None),
            P("dp", "tensor", None),
            P(None, "dp", "tensor"),
            P("tensor", "dp"),
            P("dp", "tensor"),
            P("tensor", "dp"),
            P(None, ("dp", "tensor")),
            P(("dp", "tensor")),
        ),
        check_vma=False,
    )
```

```python
import functools

import jax
import jax.numpy as jnp
from jax import lax
from jax.experimental import pallas as pl
from jax.experimental.pallas import tpu as pltpu
from jax.sharding import PartitionSpec as P

D = 1024
HEAD_DIM = 64
FF = 4096
EPSILON = 1e-05
MESH = pl.DeviceIdType.MESH
bf16 = jnp.bfloat16
f32 = jnp.float32

PIECES = 12
COLS = 512
HALF = 292
PAD = 304
SEQ = 2 * PAD
ROWS = 4 * PAD
GROUP = 16


def matmul(a, b):
    return lax.dot_general(a, b, (((1,), (0,)), ((), ())), preferred_element_type=f32)


def matmul_nt(a, b):
    return lax.dot_general(a, b, (((1,), (1,)), ((), ())), preferred_element_type=f32)


def matmul_tn(a, b):
    return lax.dot_general(a, b, (((0,), (0,)), ((), ())), preferred_element_type=f32)


def normalize(values):
    centred = values - jnp.mean(values, axis=-1, keepdims=True)
    inverse = lax.rsqrt(jnp.mean(centred * centred, axis=-1, keepdims=True) + EPSILON)
    return centred * inverse, inverse


def norm_backward(upstream, normed, inverse, gain_row):
    scaled = upstream * gain_row
    return inverse * (
        scaled
        - jnp.mean(scaled, axis=-1, keepdims=True)
        - normed * jnp.mean(scaled * normed, axis=-1, keepdims=True)
    )


class Place:
    def __init__(self, comm):
        self.comm = comm
        self.dp = lax.axis_index("dp")
        self.c = lax.axis_index("tensor")
        self.z = self.dp // 4
        self.y = (self.dp // 2) % 2
        self.x = self.dp % 2

    def dev(self, d):
        if d == "x":
            t = self.dp + 1 - 2 * self.x
        elif d == "y":
            t = self.dp + 2 - 4 * self.y
        elif d == "u":
            t = self.dp + 4
        elif d == "d":
            t = self.dp - 4
        else:
            return (self.dp, 1 - self.c)
        return (t, self.c)

    def greet(self):
        bar = pltpu.get_barrier_semaphore()

        def hail(d):
            pl.semaphore_signal(bar, inc=1, device_id=self.dev(d), device_id_type=MESH)

        hail("c")
        if not self.comm:
            pl.semaphore_wait(bar, 1)
            return
        hail("x")
        hail("y")
        pl.when(self.z < 3)(lambda: hail("u"))
        pl.when(self.z > 0)(lambda: hail("d"))
        pl.when((self.z == 0) | (self.z == 3))(lambda: pl.semaphore_wait(bar, 4))
        pl.when((self.z > 0) & (self.z < 3))(lambda: pl.semaphore_wait(bar, 5))


def wait_bytes(ref, sem):
    pltpu.make_async_copy(ref, ref, sem).wait()


class Gather:
    def __init__(self, pc, wall, routes, zs, fs, ts, ss):
        self.pc, self.wall, self.routes = pc, wall, routes
        self.zs, self.fs, self.ts, self.ss = zs, fs, ts, ss

    def copy(self, ref, d, rsem):
        return pltpu.make_async_remote_copy(
            src_ref=ref,
            dst_ref=ref,
            send_sem=self.ss.at["xyud".index(d)],
            recv_sem=rsem,
            device_id=self.pc.dev(d),
            device_id_type=MESH,
        )

    def block(self, p, zz):
        return self.wall.at[p, zz, self.pc.y, self.pc.x]

    def pair(self, p, zz, d1):
        if d1 == "x":
            return self.wall.at[p, zz, self.pc.y]
        return self.wall.at[p, zz, :, self.pc.x]

    def beside(self, p, zz, d):
        if d == "x":
            return self.wall.at[p, zz, self.pc.y, 1 - self.pc.x]
        return self.wall.at[p, zz, 1 - self.pc.y, self.pc.x]

    def part(self, p, zz):
        kind, d1, _ = self.routes[p]
        return self.block(p, zz) if kind == "Z" else self.pair(p, zz, d1)

    def pass_on(self, p, zz, way):
        cond = self.pc.z < 3 if way == "u" else self.pc.z > 0
        pl.when(cond)(lambda: self.copy(self.part(p, zz), way, self.zs.at[p, zz]).start())

    def to_second(self, p, zz):
        _, d1, d2 = self.routes[p]
        self.copy(self.pair(p, zz, d1), d2, self.ts.at[p]).start()

    def open(self, p):
        kind, d1, d2 = self.routes[p]
        z = self.pc.z
        if kind == "Z":
            self.pass_on(p, z, "u")
            self.pass_on(p, z, "d")
            self.copy(self.block(p, z), d1, self.fs.at[p, z]).start()
        else:
            self.copy(self.block(p, z), d1, self.fs.at[p, 0]).start()

    def first(self, p, zz):
        _, d1, _ = self.routes[p]
        sem = self.fs.at[p, zz] if self.routes[p][0] == "Z" else self.fs.at[p, 0]
        wait_bytes(self.beside(p, zz, d1), sem)

    def step(self, p, dist):
        kind, d1, d2 = self.routes[p]
        z = self.pc.z

        def along(src, way):
            wait_bytes(self.part(p, src), self.zs.at[p, src])
            self.pass_on(p, src, way)
            if kind == "Z":
                self.copy(self.block(p, src), d1, self.fs.at[p, src]).start()
            else:
                self.to_second(p, src)

        def arrived(src):
            self.first(p, src)
            self.to_second(p, src)

        if kind == "P" and dist == 0:
            self.first(p, z)
            self.pass_on(p, z, "u")
            self.pass_on(p, z, "d")
            self.to_second(p, z)
            return
        if 1 <= dist <= 3:
            pl.when(z - dist >= 0)(lambda: along(z - dist, "u"))
            pl.when(z + dist <= 3)(lambda: along(z + dist, "d"))
        if kind == "Z":
            if dist == 1:
                arrived(z)
            elif dist > 1:
                pl.when(z - dist + 1 >= 0)(lambda: arrived(z - dist + 1))
                pl.when(z + dist - 1 <= 3)(lambda: arrived(z + dist - 1))

    def close(self, p):
        d2 = self.routes[p][2]
        if d2 == "y":
            wait_bytes(self.wall.at[p, :, 1 - self.pc.y], self.ts.at[p])
        else:
            wait_bytes(self.wall.at[p, :, :, 1 - self.pc.x], self.ts.at[p])

    def drain(self, n, sem):
        while n >= 16:
            wait_bytes(self.wall.at[0], sem)
            n -= 16
        while n >= 4:
            wait_bytes(self.wall.at[0, 0], sem)
            n -= 4
        while n:
            wait_bytes(self.wall.at[0, 0, 0, 0], sem)
            n -= 1

    def finish(self):
        sent = {"x": 0, "y": 0, "z": 0}
        for kind, d1, d2 in self.routes:
            sent[d1] += 4 if kind == "Z" else 1
            sent[d2] += 8
            sent["z"] += 1 if kind == "Z" else 2
        self.drain(sent["x"], self.ss.at[0])
        self.drain(sent["y"], self.ss.at[1])
        for k in range(3):
            pl.when(self.pc.z == k)(lambda: self.drain(sent["z"] * (k + 1), self.ss.at[2]))
            pl.when(self.pc.z == k + 1)(lambda: self.drain(sent["z"] * (3 - k), self.ss.at[3]))


def gather_routes():
    routes = []
    for s in range(PIECES // 3):
        d1, d2 = ("x", "y") if s % 2 == 0 else ("y", "x")
        routes += [("Z", d1, d2), ("P", "x", "y"), ("P", "y", "x")]
    return routes


class Scatter:
    def __init__(self, pc, sums, routes, first, second, line, last, s1, s2, sz, s3, ss):
        self.pc, self.sums, self.routes = pc, sums, routes
        self.r1, self.r2, self.rz, self.r3 = first, second, line, last
        self.s1, self.s2, self.sz, self.s3, self.ss = s1, s2, sz, s3, ss

    def copy(self, src, dst, d, rsem):
        return pltpu.make_async_remote_copy(
            src_ref=src,
            dst_ref=dst,
            send_sem=self.ss.at["xyud".index(d)],
            recv_sem=rsem,
            device_id=self.pc.dev(d),
            device_id_type=MESH,
        )

    def pair(self, p, t, d, other):
        pc = self.pc
        if d == "y":
            return self.sums.at[p, t, (1 - pc.y) if other else pc.y]
        return self.sums.at[p, t, :, (1 - pc.x) if other else pc.x]

    def one(self, p, t, flip=None):
        pc = self.pc
        return self.sums.at[p, t, (1 - pc.y) if flip == "y" else pc.y, (1 - pc.x) if flip == "x" else pc.x]

    def each(self, dist, fn):
        z = self.pc.z
        if dist == 0:
            fn(z, None)
            return
        pl.when(z + dist <= 3)(lambda: fn(z + dist, "u"))
        pl.when(z - dist >= 0)(lambda: fn(z - dist, "d"))

    def add(self, dst, *others):
        total = dst[...].astype(f32)
        for o in others:
            total = total + o[...].astype(f32)
        dst[...] = total.astype(dst.dtype)

    def open(self, p):
        d2 = self.routes[p][2]
        for dist in (3, 2, 1, 0):
            self.each(
                dist,
                lambda t, _: self.copy(self.pair(p, t, d2, True), self.r1.at[p, t], d2, self.s1.at[p, t]).start(),
            )

    def across(self, p):
        _, d1, d2 = self.routes[p]

        def go(t, _):
            wait_bytes(self.r1.at[p, t], self.s1.at[p, t])
            self.add(self.pair(p, t, d2, False), self.r1.at[p, t])
            self.copy(self.one(p, t, d1), self.r2.at[p // 3, t], d1, self.s2.at[p // 3, t]).start()

        for dist in (3, 2, 1, 0):
            self.each(dist, go)

    def step(self, p, dist, done):
        kind, d1, d2 = self.routes[p]
        z = self.pc.z
        if kind == "Z":
            view = lambda t: self.one(p, t)
            slot = lambda i: self.rz.at[p, i, 0]
        else:
            view = lambda t: self.pair(p, t, d2, False)
            slot = lambda i: self.rz.at[p, i]

        def go(t, way):
            if kind == "Z":
                wait_bytes(self.r2.at[p // 3, t], self.s2.at[p // 3, t])
                mine = self.r2.at[p // 3, t]
            else:
                wait_bytes(self.r1.at[p, t], self.s1.at[p, t])
                mine = self.r1.at[p, t]

            def arrival(i):
                wait_bytes(slot(i), self.sz.at[p, i])
                return slot(i)

            if way == "u":
                pl.when(z > 0)(lambda: self.add(view(t), mine, arrival(t + 1)))
                pl.when(z == 0)(lambda: self.add(view(t), mine))
                self.copy(view(t), slot(t + 1), "u", self.sz.at[p, t + 1]).start()
            elif way == "d":
                pl.when(z < 3)(lambda: self.add(view(t), mine, arrival(t)))
                pl.when(z == 3)(lambda: self.add(view(t), mine))
                self.copy(view(t), slot(t), "d", self.sz.at[p, t]).start()
            else:
                pl.when(z == 0)(lambda: self.add(view(z), mine, arrival(z)))
                pl.when(z == 3)(lambda: self.add(view(z), mine, arrival(z + 1)))
                pl.when((z > 0) & (z < 3))(lambda: self.add(view(z), mine, arrival(z), arrival(z + 1)))
                if kind == "Z":
                    done(p, self.one(p, z)[...].astype(f32))
                else:
                    self.copy(self.one(p, z, d1), self.r3.at[p], d1, self.s3.at[p]).start()

        self.each(dist, go)

    def close(self, p, done):
        if self.routes[p][0] == "P":
            wait_bytes(self.r3.at[p], self.s3.at[p])
            done(p, self.one(p, self.pc.z)[...].astype(f32) + self.r3[p].astype(f32))

    def drain(self, n, sem):
        while n >= 16:
            wait_bytes(self.sums.at[0], sem)
            n -= 16
        while n >= 4:
            wait_bytes(self.sums.at[0, 0], sem)
            n -= 4
        while n:
            wait_bytes(self.sums.at[0, 0, 0, 0], sem)
            n -= 1

    def finish(self):
        sent = {"x": 0, "y": 0, "z": 0}
        for kind, d1, d2 in self.routes:
            sent[d1] += 4 if kind == "Z" else 1
            sent[d2] += 8
            sent["z"] += 1 if kind == "Z" else 2
        self.drain(sent["x"], self.ss.at[0])
        self.drain(sent["y"], self.ss.at[1])
        for k in range(3):
            pl.when(self.pc.z == k)(lambda: self.drain(sent["z"] * (3 - k), self.ss.at[2]))
            pl.when(self.pc.z == k + 1)(lambda: self.drain(sent["z"] * (k + 1), self.ss.at[3]))


def scatter_routes():
    routes = []
    for s in range(PIECES // 3):
        d1, d2 = ("x", "y") if s % 2 == 0 else ("y", "x")
        routes += [("P", "x", "y"), ("P", "y", "x"), ("Z", d1, d2)]
    return routes


def row_tile(i):
    return pl.ds(pl.multiple_of(i * PAD, 16), PAD)


def loop(count, body):
    def run(i, carry):
        body(i)
        return carry

    lax.fori_loop(0, count, run, 0)


def tensor_copy(pc, src, dst, send, recv):
    return pltpu.make_async_remote_copy(
        src_ref=src, dst_ref=dst, send_sem=send, recv_sem=recv, device_id=pc.dev("c"), device_id_type=MESH
    )


def forward_kernel(comm, *refs):
    if comm:
        x_ref, go_ref, live, mask, wq, wo, w1, w2, sml = refs[:9]
        refs = refs[9:]
        wall = refs[0]
        refs = refs[1:]
    else:
        x_ref, go_ref, live, mask, wall, smalls_in = refs[:6]
        refs = refs[6:]
    (
        h1t_o, h2t_o, g_o, gt_o, q_o, k_o, v_o, o_o, lse_o, x2_o, act_o, fac_o, outp_o, vec,
        held, smalls, hb, xp, h1, h2, g, hT, q, k, v, o, lse, x2, wbuf, proj, precv, act, fac, acc,
        lsem, wsem, osem, tsem, zs, fs, ts, ss, vzs, vfs, vts, vss,
    ) = refs
    pc = Place(comm)
    c = pc.c
    pc.greet()
    events = []
    if comm:
        for i in range(3):
            held[i] = wq[i]
        held[3] = wo[...].T
        for i in range(4):
            held[4 + i] = w1[:, i * COLS : (i + 1) * COLS]
            held[8 + i] = w2[i * COLS : (i + 1) * COLS, :].T
        own = pltpu.make_async_copy(held, wall.at[:, pc.z, pc.y, pc.x], lsem)
        own.start()
        smalls[0, pc.z, pc.y, pc.x] = sml[...]
        small = Gather(pc, smalls, [("P", "x", "y")], vzs, vfs, vts, vss)
        small.open(0)
        own.wait()
        big = Gather(pc, wall, gather_routes(), zs, fs, ts, ss)
        for p in range(PIECES):
            big.open(p)
        for p in range(PIECES):
            for dist in range(5):
                key = 2 * dist + 2 * (p // 3) + (1 if p % 3 else 0)
                events.append((key, p, dist))
        events.sort()

    todo = list(events)

    def advance(n):
        for _ in range(min(n, len(todo))):
            _, p, dist = todo.pop(0)
            big.step(p, dist)

    def advance_for(p):
        if comm:
            while any(e[1] == p for e in todo):
                advance(1)
            big.close(p)

    for i in range(2):
        rows = go_ref[i].astype(f32) * live[i].astype(f32)
        at = pl.multiple_of((2 * i + c) * PAD, 16)
        g[pl.ds(at + HALF - 4, PAD - HALF + 4)] = jnp.zeros((PAD - HALF + 4, D), bf16)
        g[pl.ds(at, HALF)] = rows.astype(bf16)
        xp[i, pl.ds(HALF - 4, PAD - HALF + 4)] = jnp.zeros((PAD - HALF + 4, D), bf16)
        xp[i, pl.ds(0, HALF)] = x_ref[i]
    gcopies = []
    for i in range(2):
        part = g.at[row_tile(2 * i + c)]
        cp = tensor_copy(pc, part, part, tsem.at[0, i], tsem.at[1, i])
        cp.start()
        gcopies.append(cp)

    if comm:
        for dist in range(4):
            advance(1)
            small.step(0, dist)
        small.close(0)
        small.finish()
        blocks = [smalls[0, r // 4, (r // 2) % 2, r % 2] for r in range(GROUP)]
    else:
        blocks = [smalls_in[r] for r in range(GROUP)]
    for r in range(GROUP):
        vec[:, r * 64 : (r + 1) * 64] = blocks[r][0:8, 0:64].astype(f32)
    for r in range(GROUP // 2):
        both = jnp.where(c == 0, blocks[r][8:10].astype(f32), blocks[r + GROUP // 2][8:10].astype(f32))
        for i in range(2):
            hb[:, r * 256 + i * 128 : r * 256 + (i + 1) * 128] = both[i : i + 1]

    advance(2)
    for i in range(2):
        normed, _ = normalize(xp[i].astype(f32))
        h1[row_tile(2 * i + c)] = (normed * vec[0:1] + vec[2:3]).astype(bf16)
    hcopies = []
    for i in range(2):
        part = h1.at[row_tile(2 * i + c)]
        cp = tensor_copy(pc, part, part, tsem.at[2, i], tsem.at[3, i])
        cp.start()
        hcopies.append(cp)
    advance(2)
    for cp in gcopies:
        cp.wait()
    outs = []

    def emit(src, dst, i):
        cp = pltpu.make_async_copy(src, dst, osem.at[i])
        cp.start()
        outs.append(cp)

    emit(g, g_o, 0)

    def transpose_into(src):
        def body(i):
            cols = pl.ds(pl.multiple_of(i * 128, 128), 128)
            hT[cols, :] = src[:, cols].T

        loop(D // 128, body)

    transpose_into(g)
    emit(hT, gt_o, 1)
    for cp in hcopies:
        cp.wait()

    def load(p, slot):
        cp = pltpu.make_async_copy(wall.at[p], wbuf.at[slot], wsem.at[slot])
        cp.start()
        return cp

    def weight(slot):
        return wbuf[slot].reshape(D, COLS)

    qcol = pl.ds(pl.multiple_of(c * COLS, COLS), COLS)
    for p in range(3):
        advance_for(p)
        load(p, p).wait()
        dst = (q, k, v)[p]

        def project(i):
            out = matmul(h1[row_tile(i)], weight(p))
            if p == 0:
                out = (out + vec[3:4, qcol]) * (HEAD_DIM**-0.5)
            elif p == 2:
                out = out + vec[4:5, qcol]
            dst[row_tile(i)] = out.astype(bf16)

        loop(4, project)
    emit(q, q_o, 2)
    emit(k, k_o, 3)
    emit(v, v_o, 4)
    outs[1].wait()
    transpose_into(h1)
    outs[1] = pltpu.make_async_copy(hT, h1t_o, osem.at[1])
    outs[1].start()

    lane = lax.broadcasted_iota(jnp.int32, (1, 128), 1)
    share = -(-len(todo) // 10)

    def attend(n):
        img, pair = n // 4, n % 4
        rows = pl.ds(pl.multiple_of(img * SEQ, 16), SEQ)
        cols = pl.ds(pl.multiple_of(pair * 128, 128), 128)
        qb, kb, vb = q[rows, cols], k[rows, cols], v[rows, cols]
        bias = mask[img, 0:1, :]
        mixed = []
        totals = lse[rows]
        for h in range(2):
            mine = (lane >= 64 * h) & (lane < 64 * h + 64)
            s = matmul_nt(jnp.where(mine, qb, jnp.zeros_like(qb)), kb) + bias
            top = jnp.max(s, axis=-1, keepdims=True)
            e = jnp.exp(s - top)
            total = jnp.sum(e, axis=-1, keepdims=True)
            mixed.append(matmul(e.astype(bf16), vb) / total)
            totals = jnp.where(lane == 2 * pair + h, top + jnp.log(total), totals)
        lse[rows] = totals
        o[rows, cols] = jnp.where(lane < 64, mixed[0], mixed[1]).astype(bf16)
        if comm:
            for j in range(8):
                pl.when(n == j)(lambda: advance(share))

    lse[...] = jnp.zeros_like(lse)
    loop(8, attend)
    emit(o, o_o, 5)
    for i in range(2):
        turned = lse[pl.ds(i * SEQ, SEQ)].T
        for h in range(8):
            lse_o[i, h] = turned[h : h + 1]

    advance_for(3)
    load(3, 3).wait()

    def out_project(i):
        proj[row_tile(i)] = matmul_nt(o[row_tile(i)], weight(3)).astype(bf16)

    loop(4, out_project)
    pcopies = []
    for i in range(2):
        cp = tensor_copy(
            pc, proj.at[row_tile(2 * i + 1 - c)], precv.at[row_tile(i)], tsem.at[4, i], tsem.at[5, i]
        )
        cp.start()
        pcopies.append(cp)
    fc1 = []
    for j in range(4):
        advance_for(4 + j)
        fc1.append(load(4 + j, j) if j < 3 else None)
        if j == 0:
            for i in range(2):
                pcopies[i].wait()
                mid = (
                    xp[i].astype(f32)
                    + proj[row_tile(2 * i + c)].astype(f32)
                    + precv[row_tile(i)].astype(f32)
                    + vec[5:6]
                )
                x2[row_tile(i)] = mid
                normed, _ = normalize(mid)
                h2[row_tile(2 * i + c)] = (normed * vec[1:2] + vec[6:7]).astype(bf16)
                part = h2.at[row_tile(2 * i + c)]
                cp = tensor_copy(pc, part, part, tsem.at[6, i], tsem.at[7, i])
                cp.start()
                hcopies[i] = cp
            emit(x2, x2_o, 6)
            for cp in hcopies:
                cp.wait()
    fc1[3] = load(7, 3)
    for j in range(4):
        fc1[j].wait()

        def up(i):
            u = matmul(h2[row_tile(i)], weight(j)) + hb[:, j * COLS : (j + 1) * COLS]
            gate = 1.0 / (1.0 + jnp.exp(-1.702 * u))
            act[j, row_tile(i)] = (u * gate).astype(bf16)
            fac[j, row_tile(i)] = (gate + 1.702 * u * gate * (1.0 - gate)).astype(bf16)

        loop(4, up)
        emit(act.at[j], act_o.at[j], 7 + j)
        emit(fac.at[j], fac_o.at[j], 11 + j)
        advance(2)
    outs[1].wait()
    transpose_into(h2)
    outs[1] = pltpu.make_async_copy(hT, h2t_o, osem.at[1])
    outs[1].start()
    for j in range(4):
        advance_for(8 + j)
        load(8 + j, j).wait()

        def down(i):
            out = matmul_nt(act[j, row_tile(i)], weight(j))
            if j > 0:
                out = out + acc[row_tile(i)]
            if j < 3:
                acc[row_tile(i)] = out
            else:
                proj[row_tile(i)] = out.astype(bf16)

        loop(4, down)
    emit(proj, outp_o, 15)
    for cp in outs:
        cp.wait()
    if comm:
        big.finish()


def forward_call(comm, args):
    B = lambda *s: pltpu.VMEM(s, bf16)
    F = lambda *s: pltpu.VMEM(s, f32)
    S = lambda *s: pltpu.SemaphoreType.DMA(s)
    A = pl.BlockSpec(memory_space=pl.ANY)
    V = pl.BlockSpec(memory_space=pltpu.VMEM)
    M = pl.BlockSpec(memory_space=pltpu.SMEM)
    sh = jax.ShapeDtypeStruct
    outs = [
        sh((D, ROWS), bf16), sh((D, ROWS), bf16), sh((ROWS, D), bf16), sh((D, ROWS), bf16),
        sh((ROWS, COLS), bf16), sh((ROWS, COLS), bf16), sh((ROWS, COLS), bf16), sh((ROWS, COLS), bf16),
        sh((2, 8, 1, SEQ), f32), sh((2 * PAD, D), f32), sh((4, ROWS, COLS), bf16), sh((4, ROWS, COLS), bf16),
        sh((ROWS, D), bf16), sh((8, D), f32),
    ]
    ospecs = [A] * 8 + [V] + [A] * 4 + [V]
    if comm:
        outs = [sh((PIECES, 4, 2, 2, 64, COLS), bf16)] + outs
        ospecs = [A] + ospecs
        ispecs = [V, V, M, V, V, V, V, V, V]
    else:
        ispecs = [V, V, M, V, A, V]
    scratch = [
        B(PIECES, 64, COLS), B(1, 4, 2, 2, 16, 128), F(1, 4 * COLS), B(2, PAD, D), B(ROWS, D), B(ROWS, D), B(ROWS, D),
        B(D, ROWS), B(ROWS, COLS), B(ROWS, COLS), B(ROWS, COLS), B(ROWS, COLS), F(2 * SEQ, 128), F(2 * PAD, D),
        B(4, 4, 2, 2, 64, COLS), B(ROWS, D), B(2 * PAD, D), B(4, ROWS, COLS), B(4, ROWS, COLS), F(ROWS, D),
        pltpu.SemaphoreType.DMA, S(4), S(16), S(8, 2), S(PIECES, 4), S(PIECES, 4), S(PIECES), S(4),
        S(1, 4), S(1, 4), S(1), S(4),
    ]
    return pl.pallas_call(
        functools.partial(forward_kernel, comm),
        out_shape=outs,
        in_specs=ispecs,
        out_specs=ospecs,
        scratch_shapes=scratch,
        name="forward",
        compiler_params=pltpu.CompilerParams(
            collective_id=0, has_side_effects=True, vmem_limit_bytes=62 * 2**20
        ),
    )(*args)


def slots_of(j):
    return 2 * j, 2 * j + 1


HOOKS = (0.4, 0.9, 1.3, 1.8, 2.2, 2.7, 3.1, 3.5, 4.0, 4.4, 5.0)
LOOP_KEYS = tuple(5.4 + 0.4 * i for i in range(8))


def backward_kernel(comm, *refs):
    x_ref, mask, vec, lse, wall, h1t_i, h2t_i, g_i, gt_i, q_i, k_i, v_i, o_i, x2_i, act_i, fac_i, outp_i = refs[:17]
    refs = refs[17:]
    layer_o, input_o = refs[:2]
    refs = refs[2:]
    if comm:
        gqkv, gout, gfc1, gfc2, gvec, gfc = refs[:6]
        refs = refs[6:]
    else:
        sums_o, vs_o, fcs_o = refs[:3]
        refs = refs[3:]
    (
        sums, r1, r2, rz, r3, x2, orecv, drecv, dx, stage, delta, vs, fcs, vsum, v1, vz, v3, vpart,
        lsem, osem, tsem, s1, s2, sz, s3, ss, t1, tz, t3, tt,
    ) = refs
    pc = Place(comm)
    c = pc.c
    pc.greet()
    events = []
    big = Scatter(pc, sums, scatter_routes(), r1, r2, rz, r3, s1, s2, sz, s3, ss)
    if comm:
        for p in range(PIECES):
            if big.routes[p][0] == "Z":
                events.append((p + 1.3, p, "across"))
                events += [(p + 2.0 + 0.6 * i, p, 3 - i) for i in range(4)]
            else:
                events += [(p + 1.3 + 0.6 * i, p, 3 - i) for i in range(4)]
                events.append((p + 4.0, p, "close"))
    todo = sorted(events, key=lambda e: e[0])

    def done(p, value):
        if p < 8:
            j = p // 2
            if p % 2 == 0:
                gfc2[j * COLS : (j + 1) * COLS, :] = value.T
            else:
                gfc1[:, j * COLS : (j + 1) * COLS] = value
        elif p == 8:
            gout[...] = value.T
        else:
            gqkv[p - 9] = value

    def advance(key):
        while todo and todo[0][0] <= key:
            _, p, what = todo.pop(0)
            if what == "across":
                big.across(p)
            elif what == "close":
                big.close(p, done)
            else:
                big.step(p, what, done)

    def opened(p):
        if comm:
            big.open(p)

    def fetch(src, dst, i):
        cp = pltpu.make_async_copy(src, dst, lsem.at[i])
        cp.start()
        return cp

    ocopies = []
    for i in range(2):
        cp = tensor_copy(
            pc, outp_i.at[row_tile(2 * i + 1 - c)], orecv.at[row_tile(i)], tsem.at[0, i], tsem.at[1, i]
        )
        cp.start()
        ocopies.append(cp)
    x2copy = fetch(x2_i, x2, 0)
    ocopy = [fetch(outp_i.at[row_tile(2 * i + c)], dx.at[row_tile(2 * i + c)], 1 + i) for i in range(2)]
    vs[...] = jnp.zeros_like(vs)

    def weight_grad(p, left, right):
        def body(i):
            rows = pl.ds(pl.multiple_of(i * 256, 256), 256)
            sums[p, i] = matmul(left[rows, :], right[...]).astype(bf16).reshape(2, 2, 64, COLS)

        loop(4, body)
        opened(p)

    hooks = list(HOOKS)

    def feed_forward(h2t, gt, g, dh2, act, fac, du, w):
        cps = [
            fetch(gt_i, gt, 3),
            fetch(act_i.at[0], act, 4),
            fetch(g_i, g, 5),
            fetch(fac_i.at[0], fac, 6),
            fetch(wall.at[8], w.at[0], 7),
            fetch(wall.at[4], w.at[1], 8),
            fetch(h2t_i, h2t, 9),
        ]
        for j in range(4):
            first, second = slots_of(j)
            if j == 0:
                cps[0].wait()
            cps[1].wait()
            weight_grad(first, gt, act)
            if j < 3:
                cps[1] = fetch(act_i.at[j + 1], act, 4)
            advance(hooks.pop(0))
            if j == 0:
                cps[2].wait()
            for i in (3, 4, 5):
                cps[i].wait()

            def tile(i):
                rows = row_tile(i)
                da = matmul(g[rows], w[0].reshape(D, COLS))
                du[rows] = (da * fac[rows].astype(f32)).astype(bf16)
                part = matmul_nt(du[rows], w[1].reshape(D, COLS))
                if j == 0:
                    dh2[rows] = part
                else:
                    dh2[rows] += part

            loop(4, tile)
            fcs[:, j * COLS : (j + 1) * COLS] = jnp.sum(du[...].astype(f32), axis=0, keepdims=True)
            if j < 3:
                cps[3] = fetch(fac_i.at[j + 1], fac, 6)
                cps[4] = fetch(wall.at[9 + j], w.at[0], 7)
                cps[5] = fetch(wall.at[5 + j], w.at[1], 8)
            if j == 0:
                cps[6].wait()
            weight_grad(second, h2t, du)
            advance(hooks.pop(0))
            if j == 0:
                x2copy.wait()
                for i in range(2):
                    ocopy[i].wait()
                    ocopies[i].wait()
                    total = (
                        x2[row_tile(i)]
                        + dx[row_tile(2 * i + c)].astype(f32)
                        + orecv[row_tile(i)].astype(f32)
                        + vec[7:8]
                    )
                    stage[i] = total[0:HALF].astype(bf16)
                lcopy = pltpu.make_async_copy(stage, layer_o, osem.at[0])
                lcopy.start()

        sent = []
        for i in range(2):
            orecv[row_tile(i)] = dh2[row_tile(2 * i + 1 - c)].astype(bf16)
            cp = tensor_copy(pc, orecv.at[row_tile(i)], drecv.at[row_tile(i)], tsem.at[2, i], tsem.at[3, i])
            cp.start()
            sent.append(cp)
        lcopy.wait()
        copies = []
        for i in range(2):
            sent[i].wait()
            own = row_tile(2 * i + c)
            up = dh2[own] + drecv[row_tile(i)].astype(f32)
            normed, inverse = normalize(x2[row_tile(i)])
            grad = g[own].astype(f32)
            total = grad + norm_backward(up, normed, inverse, vec[1:2])
            low = total.astype(bf16)
            x2[row_tile(i)] = total
            dx[own] = low
            vs[5:6] += jnp.sum(up * normed, axis=0, keepdims=True)
            vs[6:7] += jnp.sum(up, axis=0, keepdims=True)
            vs[4:5] += jnp.sum(low.astype(f32), axis=0, keepdims=True)
            vs[7:8] += jnp.sum(grad, axis=0, keepdims=True)
        for i in range(2):
            own = row_tile(2 * i + c)
            cp = tensor_copy(pc, dx.at[own], dx.at[own], tsem.at[4, i], tsem.at[5, i])
            cp.start()
            copies.append(cp)
        advance(hooks.pop(0))
        for cp in copies:
            cp.wait()

    B = lambda *s: pltpu.VMEM(s, bf16)
    F = lambda *s: pltpu.VMEM(s, f32)
    pl.run_scoped(
        feed_forward, B(D, ROWS), B(D, ROWS), B(ROWS, D), F(ROWS, D), B(ROWS, COLS), B(ROWS, COLS), B(ROWS, COLS),
        B(2, 4, 2, 2, 64, COLS),
    )

    def attention(q, k, v, o, do, w, hT, mcol):
        cps = [fetch(a, b, i) for i, (a, b) in enumerate(((o_i, o), (wall.at[3], w.at[3]), (q_i, q), (k_i, k), (v_i, v)))]
        cps += [fetch(wall.at[i], w.at[i], 5 + i) for i in range(3)]

        def turn(i):
            cols = pl.ds(pl.multiple_of(i * 128, 128), 128)
            hT[cols, :] = dx[:, cols].T

        loop(D // 128, turn)
        cps[0].wait()
        weight_grad(8, hT, o)
        cps.append(fetch(h1t_i, hT, 8))
        cps[1].wait()

        def out_back(i):
            do[row_tile(i)] = matmul(dx[row_tile(i)], w[3].reshape(D, COLS)).astype(bf16)

        loop(4, out_back)
        pick = lax.broadcasted_iota(jnp.int32, (8, COLS), 0) == lax.broadcasted_iota(jnp.int32, (8, COLS), 1) // HEAD_DIM
        pick = pick.astype(f32).astype(bf16)
        for i in range(2):
            rows = pl.ds(i * SEQ, SEQ)
            prod = do[rows].astype(f32) * o[rows].astype(f32)
            high = prod.astype(bf16)
            low = (prod - high.astype(f32)).astype(bf16)
            part = matmul_nt(pick, high) + matmul_nt(pick, low)
            for h in range(8):
                delta[i, h] = part[h : h + 1]
            mcol[rows] = jnp.broadcast_to(mask[i, 0:1], (128, SEQ)).T
        advance(hooks.pop(0))
        for i in range(2, 5):
            cps[i].wait()
        lane = lax.broadcasted_iota(jnp.int32, (1, 128), 1)

        def attend(n):
            img, pair = n // 4, n % 4
            rows = pl.ds(pl.multiple_of(img * SEQ, 16), SEQ)
            cols = pl.ds(pl.multiple_of(pair * 128, 128), 128)
            qb, kb, vb, gb = q[rows, cols], k[rows, cols], v[rows, cols], do[rows, cols]
            bias = mcol[rows, 0:1]
            dq, dk, dv = [], None, None
            for h in range(2):
                mine = (lane >= 64 * h) & (lane < 64 * h + 64)
                qm = jnp.where(mine, qb, jnp.zeros_like(qb))
                gm = jnp.where(mine, gb, jnp.zeros_like(gb))
                p = jnp.exp(matmul_nt(kb, qm) + bias - lse[img, 2 * pair + h])
                dp = matmul_nt(vb, gm)
                ds = (p * (dp - delta[img, 2 * pair + h])).astype(bf16)
                dvh = matmul(p.astype(bf16), gm)
                dkh = matmul(ds, qm)
                dq.append(matmul_tn(ds, kb) * (HEAD_DIM**-0.5))
                dk = dkh if dk is None else dk + dkh
                dv = dvh if dv is None else dv + dvh
            q[rows, cols] = jnp.where(lane < 64, dq[0], dq[1]).astype(bf16)
            k[rows, cols] = dk.astype(bf16)
            v[rows, cols] = dv.astype(bf16)
            for j in range(8):
                pl.when(n == j)(lambda: advance(LOOP_KEYS[j]))

        loop(8, attend)
        cps[8].wait()
        for i, part in enumerate((q, k, v)):
            weight_grad(9 + i, hT, part)
        advance(LOOP_KEYS[-1] + 0.4)
        for i in range(3):
            cps[5 + i].wait()

        def back(t):
            rows = row_tile(t)
            total = matmul_nt(q[rows], w[0].reshape(D, COLS))
            total += matmul_nt(k[rows], w[1].reshape(D, COLS))
            total += matmul_nt(v[rows], w[2].reshape(D, COLS))
            return total

        sent = []
        for i in range(2):
            dx[row_tile(2 * i + 1 - c)] = back(2 * i + 1 - c).astype(bf16)
            cp = tensor_copy(
                pc, dx.at[row_tile(2 * i + 1 - c)], drecv.at[row_tile(i)], tsem.at[6, i], tsem.at[7, i]
            )
            cp.start()
            sent.append(cp)
        xcopy = fetch(x_ref, stage, 0)
        xcopy.wait()
        advance(LOOP_KEYS[-1] + 0.8)
        for i in range(2):
            up = back(2 * i + c)
            sent[i].wait()
            up = (up + drecv[row_tile(i)].astype(f32))[0:HALF]
            normed, inverse = normalize(stage[i].astype(f32))
            total = x2[row_tile(i)][0:HALF] + norm_backward(up, normed, inverse, vec[0:1])
            stage[i] = total.astype(bf16)
            vs[0:1] += jnp.sum(up * normed, axis=0, keepdims=True)
            vs[1:2] += jnp.sum(up, axis=0, keepdims=True)
        icopy = pltpu.make_async_copy(stage, input_o, osem.at[1])
        icopy.start()
        here = pl.ds(pl.multiple_of(c * COLS, COLS), COLS)
        vs[2:3, here] = jnp.sum(q[...].astype(f32), axis=0, keepdims=True)
        vs[3:4, here] = jnp.sum(v[...].astype(f32), axis=0, keepdims=True)
        if comm:
            vsum[...] = jnp.zeros_like(vsum)
            for r in range(GROUP):
                vsum[0, r // 4, (r // 2) % 2, r % 2, 0:8, 0:64] = vs[:, r * 64 : (r + 1) * 64]
            for r in range(GROUP // 2):
                for half in range(2):
                    row = fcs[:, (2 * r + half) * 128 : (2 * r + half + 1) * 128]
                    for side in range(2):
                        at = r + side * (GROUP // 2)
                        value = jnp.where(c == side, row, jnp.zeros_like(row))
                        vsum[0, at // 4, (at // 2) % 2, at % 2, 8 + half : 9 + half, :] = value
            small = Scatter(pc, vsum, [("P", "x", "y")], v1, None, vz, v3, t1, None, tz, t3, tt)
            small.open(0)
            advance(LOOP_KEYS[-1] + 1.6)
            for dist in (3, 2, 1, 0):
                small.step(0, dist, None)
                advance(LOOP_KEYS[-1] + 2.2 + 0.4 * (3 - dist))

            def keep(p, value):
                vpart[0] = value

            small.close(0, keep)
            cp = tensor_copy(pc, vpart.at[0], vpart.at[1], tsem.at[8, 0], tsem.at[9, 0])
            cp.start()
            advance(1e9)
            cp.wait()
            total = vpart[0] + vpart[1]
            gvec[...] = jnp.where(c == 0, total[0:8, 0:32], total[0:8, 32:64])
            gfc[...] = jnp.where(c == 0, total[8:9], total[9:10])
            small.finish()
            big.finish()
        else:
            cps2 = [pltpu.make_async_copy(a, b, osem.at[2 + i]) for i, (a, b) in enumerate(((sums, sums_o), (vs, vs_o), (fcs, fcs_o)))]
            for cp in cps2:
                cp.start()
            for cp in cps2:
                cp.wait()
        icopy.wait()

    pl.run_scoped(
        attention, B(ROWS, COLS), B(ROWS, COLS), B(ROWS, COLS), B(ROWS, COLS), B(ROWS, COLS), B(4, 4, 2, 2, 64, COLS),
        B(D, ROWS), F(ROWS, 128),
    )


def backward_call(comm, args):
    B = lambda *s: pltpu.VMEM(s, bf16)
    F = lambda *s: pltpu.VMEM(s, f32)
    S = lambda *s: pltpu.SemaphoreType.DMA(s)
    A = pl.BlockSpec(memory_space=pl.ANY)
    V = pl.BlockSpec(memory_space=pltpu.VMEM)
    sh = jax.ShapeDtypeStruct
    outs = [sh((2, HALF, D), bf16), sh((2, HALF, D), bf16)]
    ospecs = [A, A]
    if comm:
        outs += [
            sh((3, 64, COLS), f32), sh((COLS, 64), f32), sh((64, 4 * COLS), f32), sh((4 * COLS, 64), f32),
            sh((8, 32), f32), sh((1, 128), f32),
        ]
        ospecs += [V] * 6
    else:
        outs += [sh((PIECES, 4, 2, 2, 64, COLS), bf16), sh((8, D), f32), sh((1, 4 * COLS), f32)]
        ospecs += [A] * 3
    ispecs = [A, V, V, V] + [A] * 13
    one = (4, 2, 2, 64, COLS)
    scratch = [
        B(PIECES, *one), B(PIECES, 4, 2, 64, COLS), B(4, 4, 64, COLS), B(PIECES, 5, 2, 64, COLS), B(PIECES, 64, COLS),
        F(2 * PAD, D), B(2 * PAD, D), B(2 * PAD, D), B(ROWS, D), B(2, HALF, D), F(2, 8, 1, SEQ), F(8, D), F(1, 4 * COLS),
        F(1, 4, 2, 2, 16, 128), F(1, 4, 2, 16, 128), F(1, 5, 2, 16, 128), F(1, 16, 128), F(2, 16, 128),
        S(10), S(5), S(10, 2), S(PIECES, 4), S(4, 4), S(PIECES, 5), S(PIECES), S(4), S(1, 4), S(1, 5), S(1), S(4),
    ]
    return pl.pallas_call(
        functools.partial(backward_kernel, comm),
        out_shape=outs,
        in_specs=ispecs,
        out_specs=ospecs,
        scratch_shapes=scratch,
        name="backward",
        compiler_params=pltpu.CompilerParams(
            collective_id=1, has_side_effects=True, vmem_limit_bytes=62 * 2**20
        ),
    )(*args)


def split_cols(m):
    return jnp.transpose(m.reshape(m.shape[0], m.shape[1] // COLS, COLS), (1, 0, 2))


def shards(layer_in, out_grad, key_valid, image_live, w_qkv, w_out, w_fc1, w_fc2, norm_gains, bias_rows, fc_bias):
    comm = lax.axis_size("dp") == GROUP
    valid = jnp.pad(key_valid.reshape(2, 2, HALF), ((0, 0), (0, 0), (0, PAD - HALF))).reshape(2, 1, SEQ)
    mask = jnp.broadcast_to(jnp.where(valid > 0, 0.0, -1e9).astype(f32), (2, 8, SEQ))
    rows = jnp.concatenate([norm_gains, bias_rows], axis=0)
    if comm:
        low = jnp.pad(rows, ((0, 8), (0, 64)))
        small = lax.dynamic_update_slice(low, fc_bias.reshape(2, 128), (8, 0))
        made = forward_call(True, (layer_in, out_grad, image_live, mask, w_qkv, w_out, w_fc1, w_fc2, small))
        wall, made = made[0], made[1:]
    else:
        local = jnp.concatenate([w_qkv, w_out.T[None], split_cols(w_fc1), split_cols(w_fc2.T)], axis=0)
        wall = lax.all_gather(local, "dp", axis=1, tiled=True).reshape(PIECES, 4, 2, 2, 64, COLS)
        rows = lax.all_gather(rows, "dp", axis=1, tiled=True)
        hidden = lax.all_gather(fc_bias, "dp", axis=0, tiled=True)
        small = jnp.pad(jnp.transpose(rows.reshape(8, GROUP, 64), (1, 0, 2)), ((0, 0), (0, 8), (0, 64)))
        small = lax.dynamic_update_slice(small, hidden.reshape(GROUP, 2, 128), (0, 8, 0))
        made = forward_call(False, (layer_in, out_grad, image_live, mask, wall, small))
    h1t, h2t, g, gt, q, k, v, o, lse, x2, act, fac, outp, vec = made
    back = backward_call(
        comm, (layer_in, mask, vec, lse, wall, h1t, h2t, g, gt, q, k, v, o, x2, act, fac, outp)
    )
    layer_out, input_grad = back[:2]
    if comm:
        gqkv, gout, gfc1, gfc2, gvec, gfc = back[2:]
        return (layer_out, input_grad, gqkv, gout, gfc1, gfc2, gvec, gfc.reshape(128))
    sums, vs, fcs = back[2:]
    mine = lax.psum_scatter(sums.reshape(PIECES, D, COLS), "dp", scatter_dimension=1, tiled=True).astype(f32)
    down = jnp.transpose(mine[0:8:2], (0, 2, 1)).reshape(4 * COLS, -1)
    up = jnp.transpose(mine[1:8:2], (1, 0, 2)).reshape(-1, 4 * COLS)
    vector = lax.psum_scatter(vs, ("dp", "tensor"), scatter_dimension=1, tiled=True)
    whole = lax.dynamic_update_slice(jnp.zeros((FF,), f32), fcs[0], (lax.axis_index("tensor") * 4 * COLS,))
    hidden = lax.psum_scatter(whole, ("dp", "tensor"), scatter_dimension=0, tiled=True)
    return (layer_out, input_grad, mine[9:12], mine[8].T, up, down, vector, hidden)


def solution(mesh):
    return jax.shard_map(
        shards,
        mesh=mesh,
        in_specs=(
            P("dp", "tensor", None),
            P("dp", "tensor", None),
            P("dp", None),
            P("dp"),
            P(None, "dp", "tensor"),
            P("tensor", "dp"),
            P("dp", "tensor"),
            P("tensor", "dp"),
            P(None, "dp"),
            P(None, "dp"),
            P("dp"),
        ),
        out_specs=(
            P("dp", "tensor", None),
            P("dp", "tensor", None),
            P(None, "dp", "tensor"),
            P("tensor", "dp"),
            P("dp", "tensor"),
            P("tensor", "dp"),
            P(None, ("dp", "tensor")),
            P(("dp", "tensor")),
        ),
        check_vma=False,
    )
```

```python
import functools

import jax
import jax.numpy as jnp
from jax import lax
from jax.experimental import pallas as pl
from jax.experimental.pallas import tpu as pltpu
from jax.sharding import PartitionSpec as P

D = 1024
HEAD_DIM = 64
FF = 4096
EPSILON = 1e-05
MESH = pl.DeviceIdType.MESH
bf16 = jnp.bfloat16
f32 = jnp.float32

PIECES = 12
COLS = 512
HALF = 292
PAD = 304
SEQ = 2 * PAD
ROWS = 4 * PAD
GROUP = 16


def matmul(a, b):
    return lax.dot_general(a, b, (((1,), (0,)), ((), ())), preferred_element_type=f32)


def matmul_nt(a, b):
    return lax.dot_general(a, b, (((1,), (1,)), ((), ())), preferred_element_type=f32)


def matmul_tn(a, b):
    return lax.dot_general(a, b, (((0,), (0,)), ((), ())), preferred_element_type=f32)


def column_sums(ref):
    return matmul(jnp.ones((8, ref.shape[0]), bf16), ref[...])[0:1]


def normalize(values):
    centred = values - jnp.mean(values, axis=-1, keepdims=True)
    inverse = lax.rsqrt(jnp.mean(centred * centred, axis=-1, keepdims=True) + EPSILON)
    return centred * inverse, inverse


def norm_backward(upstream, normed, inverse, gain_row):
    scaled = upstream * gain_row
    return inverse * (
        scaled
        - jnp.mean(scaled, axis=-1, keepdims=True)
        - normed * jnp.mean(scaled * normed, axis=-1, keepdims=True)
    )


class Place:
    def __init__(self, comm):
        self.comm = comm
        self.dp = lax.axis_index("dp")
        self.c = lax.axis_index("tensor")
        self.z = self.dp // 4
        self.y = (self.dp // 2) % 2
        self.x = self.dp % 2

    def dev(self, d):
        if d == "x":
            t = self.dp + 1 - 2 * self.x
        elif d == "y":
            t = self.dp + 2 - 4 * self.y
        elif d == "u":
            t = self.dp + 4
        elif d == "d":
            t = self.dp - 4
        else:
            return (self.dp, 1 - self.c)
        return (t, self.c)

    def greet(self):
        bar = pltpu.get_barrier_semaphore()

        def hail(d):
            pl.semaphore_signal(bar, inc=1, device_id=self.dev(d), device_id_type=MESH)

        hail("c")
        if not self.comm:
            pl.semaphore_wait(bar, 1)
            return
        hail("x")
        hail("y")
        pl.when(self.z < 3)(lambda: hail("u"))
        pl.when(self.z > 0)(lambda: hail("d"))
        pl.when((self.z == 0) | (self.z == 3))(lambda: pl.semaphore_wait(bar, 4))
        pl.when((self.z > 0) & (self.z < 3))(lambda: pl.semaphore_wait(bar, 5))


def wait_bytes(ref, sem):
    pltpu.make_async_copy(ref, ref, sem).wait()


class Gather:
    def __init__(self, pc, wall, routes, zs, fs, ts, ss):
        self.pc, self.wall, self.routes = pc, wall, routes
        self.zs, self.fs, self.ts, self.ss = zs, fs, ts, ss

    def copy(self, ref, d, rsem):
        return pltpu.make_async_remote_copy(
            src_ref=ref,
            dst_ref=ref,
            send_sem=self.ss.at["xyud".index(d)],
            recv_sem=rsem,
            device_id=self.pc.dev(d),
            device_id_type=MESH,
        )

    def block(self, p, zz):
        return self.wall.at[p, zz, self.pc.y, self.pc.x]

    def pair(self, p, zz, d1):
        if d1 == "x":
            return self.wall.at[p, zz, self.pc.y]
        return self.wall.at[p, zz, :, self.pc.x]

    def beside(self, p, zz, d):
        if d == "x":
            return self.wall.at[p, zz, self.pc.y, 1 - self.pc.x]
        return self.wall.at[p, zz, 1 - self.pc.y, self.pc.x]

    def part(self, p, zz):
        kind, d1, _ = self.routes[p]
        return self.block(p, zz) if kind == "Z" else self.pair(p, zz, d1)

    def pass_on(self, p, zz, way):
        cond = self.pc.z < 3 if way == "u" else self.pc.z > 0
        pl.when(cond)(lambda: self.copy(self.part(p, zz), way, self.zs.at[p, zz]).start())

    def to_second(self, p, zz):
        _, d1, d2 = self.routes[p]
        self.copy(self.pair(p, zz, d1), d2, self.ts.at[p]).start()

    def open(self, p):
        kind, d1, d2 = self.routes[p]
        z = self.pc.z
        if kind == "Z":
            self.pass_on(p, z, "u")
            self.pass_on(p, z, "d")
            self.copy(self.block(p, z), d1, self.fs.at[p, z]).start()
        else:
            self.copy(self.block(p, z), d1, self.fs.at[p, 0]).start()

    def first(self, p, zz):
        _, d1, _ = self.routes[p]
        sem = self.fs.at[p, zz] if self.routes[p][0] == "Z" else self.fs.at[p, 0]
        wait_bytes(self.beside(p, zz, d1), sem)

    def step(self, p, dist):
        kind, d1, d2 = self.routes[p]
        z = self.pc.z

        def along(src, way):
            wait_bytes(self.part(p, src), self.zs.at[p, src])
            self.pass_on(p, src, way)
            if kind == "Z":
                self.copy(self.block(p, src), d1, self.fs.at[p, src]).start()
            else:
                self.to_second(p, src)

        def arrived(src):
            self.first(p, src)
            self.to_second(p, src)

        if kind == "P" and dist == 0:
            self.first(p, z)
            self.pass_on(p, z, "u")
            self.pass_on(p, z, "d")
            self.to_second(p, z)
            return
        if 1 <= dist <= 3:
            pl.when(z - dist >= 0)(lambda: along(z - dist, "u"))
            pl.when(z + dist <= 3)(lambda: along(z + dist, "d"))
        if kind == "Z":
            if dist == 1:
                arrived(z)
            elif dist > 1:
                pl.when(z - dist + 1 >= 0)(lambda: arrived(z - dist + 1))
                pl.when(z + dist - 1 <= 3)(lambda: arrived(z + dist - 1))

    def close(self, p):
        d2 = self.routes[p][2]
        if d2 == "y":
            wait_bytes(self.wall.at[p, :, 1 - self.pc.y], self.ts.at[p])
        else:
            wait_bytes(self.wall.at[p, :, :, 1 - self.pc.x], self.ts.at[p])

    def drain(self, n, sem):
        while n >= 16:
            wait_bytes(self.wall.at[0], sem)
            n -= 16
        while n >= 4:
            wait_bytes(self.wall.at[0, 0], sem)
            n -= 4
        while n:
            wait_bytes(self.wall.at[0, 0, 0, 0], sem)
            n -= 1

    def finish(self):
        sent = {"x": 0, "y": 0, "z": 0}
        for kind, d1, d2 in self.routes:
            sent[d1] += 4 if kind == "Z" else 1
            sent[d2] += 8
            sent["z"] += 1 if kind == "Z" else 2
        self.drain(sent["x"], self.ss.at[0])
        self.drain(sent["y"], self.ss.at[1])
        for k in range(3):
            pl.when(self.pc.z == k)(lambda: self.drain(sent["z"] * (k + 1), self.ss.at[2]))
            pl.when(self.pc.z == k + 1)(lambda: self.drain(sent["z"] * (3 - k), self.ss.at[3]))


class Scatter:
    def __init__(self, pc, sums, routes, first, second, line, single, last, s1, s2, sz, s3, ss):
        self.pc, self.sums, self.routes = pc, sums, routes
        self.r1, self.r2, self.rz, self.rzz, self.r3 = first, second, line, single, last
        self.s1, self.s2, self.sz, self.s3, self.ss = s1, s2, sz, s3, ss
        self.rank = [sum(r[0] == "Z" for r in routes[:p]) for p in range(len(routes))]

    def copy(self, src, dst, d, rsem):
        return pltpu.make_async_remote_copy(
            src_ref=src,
            dst_ref=dst,
            send_sem=self.ss.at["xyud".index(d)],
            recv_sem=rsem,
            device_id=self.pc.dev(d),
            device_id_type=MESH,
        )

    def pair(self, p, t, d, other):
        pc = self.pc
        if d == "y":
            return self.sums.at[p, t, (1 - pc.y) if other else pc.y]
        return self.sums.at[p, t, :, (1 - pc.x) if other else pc.x]

    def one(self, p, t, flip=None):
        pc = self.pc
        return self.sums.at[p, t, (1 - pc.y) if flip == "y" else pc.y, (1 - pc.x) if flip == "x" else pc.x]

    def each(self, dist, fn):
        z = self.pc.z
        if dist == 0:
            fn(z, None)
            return
        pl.when(z + dist <= 3)(lambda: fn(z + dist, "u"))
        pl.when(z - dist >= 0)(lambda: fn(z - dist, "d"))

    def add(self, dst, *others):
        total = dst[...].astype(f32)
        for o in others:
            total = total + o[...].astype(f32)
        dst[...] = total.astype(dst.dtype)

    def open(self, p):
        d2 = self.routes[p][2]
        for dist in (3, 2, 1, 0):
            self.each(
                dist,
                lambda t, _: self.copy(self.pair(p, t, d2, True), self.r1.at[p, t], d2, self.s1.at[p, t]).start(),
            )

    def across(self, p):
        _, d1, d2 = self.routes[p]

        def go(t, _):
            wait_bytes(self.r1.at[p, t], self.s1.at[p, t])
            self.add(self.pair(p, t, d2, False), self.r1.at[p, t])
            self.copy(self.one(p, t, d1), self.r2.at[self.rank[p], t], d1, self.s2.at[self.rank[p], t]).start()

        for dist in (3, 2, 1, 0):
            self.each(dist, go)

    def step(self, p, dist, done):
        kind, d1, d2 = self.routes[p]
        z = self.pc.z
        if kind == "Z":
            view = lambda t: self.one(p, t)
            slot = lambda i: self.rzz.at[self.rank[p], i]
        else:
            view = lambda t: self.pair(p, t, d2, False)
            slot = lambda i: self.rz.at[p - self.rank[p], i]

        def go(t, way):
            if kind == "Z":
                wait_bytes(self.r2.at[self.rank[p], t], self.s2.at[self.rank[p], t])
                mine = self.r2.at[self.rank[p], t]
            else:
                wait_bytes(self.r1.at[p, t], self.s1.at[p, t])
                mine = self.r1.at[p, t]

            def arrival(i):
                wait_bytes(slot(i), self.sz.at[p, i])
                return slot(i)

            if way == "u":
                pl.when(z > 0)(lambda: self.add(view(t), mine, arrival(t + 1)))
                pl.when(z == 0)(lambda: self.add(view(t), mine))
                self.copy(view(t), slot(t + 1), "u", self.sz.at[p, t + 1]).start()
            elif way == "d":
                pl.when(z < 3)(lambda: self.add(view(t), mine, arrival(t)))
                pl.when(z == 3)(lambda: self.add(view(t), mine))
                self.copy(view(t), slot(t), "d", self.sz.at[p, t]).start()
            else:
                pl.when(z == 0)(lambda: self.add(view(z), mine, arrival(z)))
                pl.when(z == 3)(lambda: self.add(view(z), mine, arrival(z + 1)))
                pl.when((z > 0) & (z < 3))(lambda: self.add(view(z), mine, arrival(z), arrival(z + 1)))
                if kind == "Z":
                    done(p, self.one(p, z)[...].astype(f32))
                else:
                    self.copy(self.one(p, z, d1), self.r3.at[p - self.rank[p]], d1, self.s3.at[p]).start()

        self.each(dist, go)

    def close(self, p, done):
        if self.routes[p][0] == "P":
            wait_bytes(self.r3.at[p - self.rank[p]], self.s3.at[p])
            done(p, self.one(p, self.pc.z)[...].astype(f32) + self.r3[p - self.rank[p]].astype(f32))

    def drain(self, n, sem):
        while n >= 16:
            wait_bytes(self.sums.at[0], sem)
            n -= 16
        while n >= 4:
            wait_bytes(self.sums.at[0, 0], sem)
            n -= 4
        while n:
            wait_bytes(self.sums.at[0, 0, 0, 0], sem)
            n -= 1

    def finish(self):
        sent = {"x": 0, "y": 0, "z": 0}
        for kind, d1, d2 in self.routes:
            sent[d1] += 4 if kind == "Z" else 1
            sent[d2] += 8
            sent["z"] += 1 if kind == "Z" else 2
        self.drain(sent["x"], self.ss.at[0])
        self.drain(sent["y"], self.ss.at[1])
        for k in range(3):
            pl.when(self.pc.z == k)(lambda: self.drain(sent["z"] * (3 - k), self.ss.at[2]))
            pl.when(self.pc.z == k + 1)(lambda: self.drain(sent["z"] * (k + 1), self.ss.at[3]))


def row_tile(i):
    return pl.ds(pl.multiple_of(i * PAD, 16), PAD)


def loop(count, body):
    def run(i, carry):
        body(i)
        return carry

    lax.fori_loop(0, count, run, 0)


def tensor_copy(pc, src, dst, send, recv):
    return pltpu.make_async_remote_copy(
        src_ref=src, dst_ref=dst, send_sem=send, recv_sem=recv, device_id=pc.dev("c"), device_id_type=MESH
    )


FORWARD_ROUTES = (
    ("Z", "y", "x"),
    ("P", "x", "y"),
    ("Z", "y", "x"),
    ("P", "x", "y"),
    ("P", "y", "x"),
    ("Z", "x", "y"),
    ("P", "y", "x"),
    ("Z", "x", "y"),
    ("P", "y", "x"),
    ("P", "x", "y"),
    ("P", "x", "y"),
    ("P", "y", "x"),
)
FORWARD_PLAN = {
    "small0": (21,),
    "small1": (40, 1,),
    "small2": (10, 22, 2, 11, 30,),
    "small4": (51, 3, 12, 23, 31,),
    "norm0": (13, 100,),
    "norm1": (4, 90, 32,),
    "turn_g": (71,),
    "wait_h": (24,),
    "turn_h1": (52, 110, 60,),
    "attend2": (72,),
    "attend3": (41,),
    "attend4": (80, 33, 53,),
    "attend6": (42,),
    "attend7": (73, 61, 91,),
    "need3": (43,),
    "own3": (54, 74,),
    "mid1": (62, 101,),
    "need4": (63, 81,),
    "need5": (92,),
    "need7": (82,),
    "turn_h2": (111, 93, 102,),
    "grad1": (83,),
    "grad3": (112,),
    "need8": (103,),
    "need9": (113,),
}
BACKWARD_ROUTES = (
    ("P", "x", "y"),
    ("P", "y", "x"),
    ("Z", "x", "y"),
    ("Z", "y", "x"),
    ("P", "y", "x"),
    ("P", "y", "x"),
    ("P", "x", "y"),
    ("Z", "x", "y"),
    ("P", "y", "x"),
    ("P", "y", "x"),
    ("P", "x", "y"),
    ("Z", "y", "x"),
)
BACKWARD_PLAN = {
    "tile2": (3,),
    "tile8": (13,),
    "tile11": (2,),
    "tile12": (12,),
    "grad4": (1,),
    "grad6": (43, 11,),
    "out": (42, 24, 63,),
    "attend0": (53, 41,),
    "attend2": (34, 52, 62,),
    "attend6": (51, 83,),
    "attend10": (61,),
    "attend11": (33,),
    "attend12": (74, 82,),
    "attend13": (23,),
    "attend15": (81,),
    "grad10": (73, 32, 72, 10,),
    "grad11": (31, 22,),
    "back1": (40, 103, 93,),
    "back3": (50, 30, 102, 15,),
    "small3": (92,),
    "small2": (101,),
    "small0": (91, 80,),
    "small_end": (60, 114, 113, 71, 0, 100, 90, 65, 112, 21,),
    "end": (5, 70, 105, 111, 20, 55, 95, 85, 45, 110,),
}


def forward_kernel(comm, *refs):
    if comm:
        x_ref, go_ref, live, mask, wq, wo, w1, w2, sml = refs[:9]
        wall_o = refs[9]
        refs = refs[10:]
    else:
        x_ref, go_ref, live, mask, wall_i, smalls_in = refs[:6]
        refs = refs[6:]
    (
        h1t_o, h2t_o, g_o, q_o, k_o, v_o, o_o, lse_o, x2_o, fac_o, dw_o, outp_o, outc_o, vec,
        wall, smalls, hb, xp, h1, g, gT, hT, q, k, v, o, lse, x2, proj, precv, act, fac, dw, acc,
        lsem, osem, tsem, zs, fs, ts, ss, vzs, vfs, vts, vss,
    ) = refs
    pc = Place(comm)
    c = pc.c
    pc.greet()
    big = Gather(pc, wall, FORWARD_ROUTES, zs, fs, ts, ss)
    outs = {}

    def emit(src, dst, i):
        outs[i] = pltpu.make_async_copy(src, dst, osem.at[i])
        outs[i].start()

    def at(name):
        if comm:
            for code in FORWARD_PLAN.get(name, ()):
                big.step(code // 10, code % 10)

    def need(p):
        if comm:
            big.close(p)
            emit(wall.at[p], wall_o.at[p], 20 + p)

    def weight(p):
        return wall[p].reshape(D, COLS)

    if comm:
        smalls[0, pc.z, pc.y, pc.x] = sml[...]
        small = Gather(pc, smalls, [("P", "x", "y")], vzs, vfs, vts, vss)
        small.open(0)
        for i in range(3):
            wall[i, pc.z, pc.y, pc.x] = wq[i]
        wall[3, pc.z, pc.y, pc.x] = wo[...]
        for i in range(4):
            wall[4 + i, pc.z, pc.y, pc.x] = w1[:, i * COLS : (i + 1) * COLS]
            wall[8 + i, pc.z, pc.y, pc.x] = w2[:, i * COLS : (i + 1) * COLS]
        for p in range(PIECES):
            big.open(p)
    else:
        whole = pltpu.make_async_copy(wall_i, wall, lsem)
        whole.start()

    gcopies = []
    for i in range(2):
        rows = go_ref[i].astype(f32) * live[i].astype(f32)
        start = pl.multiple_of((2 * i + c) * PAD, 16)
        g[pl.ds(start + HALF - 4, PAD - HALF + 4)] = jnp.zeros((PAD - HALF + 4, D), bf16)
        g[pl.ds(start, HALF)] = rows.astype(bf16)
        part = g.at[row_tile(2 * i + c)]
        cp = tensor_copy(pc, part, part, tsem.at[0, i], tsem.at[1, i])
        cp.start()
        gcopies.append(cp)
        xp[i, pl.ds(HALF - 4, PAD - HALF + 4)] = jnp.zeros((PAD - HALF + 4, D), bf16)
        xp[i, pl.ds(0, HALF)] = x_ref[i]

    if comm:
        for dist in range(4):
            at(f"small{dist}")
            small.step(0, dist)
        at("small4")
        small.close(0)
        small.finish()
        blocks = [smalls[0, r // 4, (r // 2) % 2, r % 2] for r in range(GROUP)]
    else:
        blocks = [smalls_in[r] for r in range(GROUP)]
        whole.wait()
    for r in range(GROUP):
        vec[:, r * 64 : (r + 1) * 64] = blocks[r][0:8, 0:64].astype(f32)
    for r in range(GROUP // 2):
        both = jnp.where(c == 0, blocks[r][8:10].astype(f32), blocks[r + GROUP // 2][8:10].astype(f32))
        for i in range(2):
            hb[:, r * 256 + i * 128 : r * 256 + (i + 1) * 128] = both[i : i + 1]

    hcopies = []
    for i in range(2):
        at(f"norm{i}")
        normed, _ = normalize(xp[i].astype(f32))
        h1[row_tile(2 * i + c)] = (normed * vec[0:1] + vec[2:3]).astype(bf16)
        part = h1.at[row_tile(2 * i + c)]
        cp = tensor_copy(pc, part, part, tsem.at[2, i], tsem.at[3, i])
        cp.start()
        hcopies.append(cp)
    for cp in gcopies:
        cp.wait()
    emit(g, g_o, 0)

    def transpose_into(dst, src):
        def body(i):
            cols = pl.ds(pl.multiple_of(i * 128, 128), 128)
            dst[cols, :] = src[:, cols].T

        loop(D // 128, body)

    at("turn_g")
    transpose_into(gT, g)
    at("wait_h")
    for cp in hcopies:
        cp.wait()
    at("turn_h1")
    transpose_into(hT, h1)
    emit(hT, h1t_o, 1)

    qcol = pl.ds(pl.multiple_of(c * COLS, COLS), COLS)
    for p in range(3):
        at(f"need{p}")
        need(p)
        dst = (q, k, v)[p]

        def project(i):
            out = matmul(h1[row_tile(i)], weight(p))
            if p == 0:
                out = (out + vec[3:4, qcol]) * (HEAD_DIM**-0.5)
            elif p == 2:
                out = out + vec[4:5, qcol]
            dst[row_tile(i)] = out.astype(bf16)

        loop(4, project)
        emit(dst, (q_o, k_o, v_o)[p], 2 + p)

    lane = lax.broadcasted_iota(jnp.int32, (1, 128), 1)

    def attend(n):
        img, pair = n // 4, n % 4
        for j in range(8):
            pl.when(n == j)(lambda: at(f"attend{j}"))
        rows = pl.ds(pl.multiple_of(img * SEQ, 16), SEQ)
        cols = pl.ds(pl.multiple_of(pair * 128, 128), 128)
        qb, kb, vb = q[rows, cols], k[rows, cols], v[rows, cols]
        bias = mask[img, 0:1, :]
        mixed = []
        totals = lse[rows]
        for h in range(2):
            mine = (lane >= 64 * h) & (lane < 64 * h + 64)
            s = matmul_nt(jnp.where(mine, qb, jnp.zeros_like(qb)), kb) + bias
            top = jnp.max(s, axis=-1, keepdims=True)
            e = jnp.exp(s - top)
            total = jnp.sum(e, axis=-1, keepdims=True)
            mixed.append(matmul(e.astype(bf16), vb) / total)
            totals = jnp.where(lane == 2 * pair + h, top + jnp.log(total), totals)
        lse[rows] = totals
        o[rows, cols] = jnp.where(lane < 64, mixed[0], mixed[1]).astype(bf16)

    lse[...] = jnp.zeros_like(lse)
    loop(8, attend)
    emit(o, o_o, 5)

    h2 = h1
    at("need3")
    need(3)
    pcopies = []
    for i in range(2):
        other = row_tile(2 * i + 1 - c)
        proj[other] = matmul_nt(o[other], weight(3)).astype(bf16)
        cp = tensor_copy(pc, proj.at[other], precv.at[row_tile(i)], tsem.at[4, i], tsem.at[5, i])
        cp.start()
        pcopies.append(cp)
    at("own3")
    for i in range(2):
        own = row_tile(2 * i + c)
        proj[own] = matmul_nt(o[own], weight(3)).astype(bf16)
    for i in range(2):
        turned = lse[pl.ds(i * SEQ, SEQ)].T
        for h in range(8):
            lse_o[i, h] = turned[h : h + 1]
    for i in range(2):
        at(f"mid{i}")
        pcopies[i].wait()
        own = row_tile(2 * i + c)
        mid = xp[i].astype(f32) + proj[own].astype(f32) + precv[row_tile(i)].astype(f32) + vec[5:6]
        x2[row_tile(i)] = mid
        normed, _ = normalize(mid)
        h2[own] = (normed * vec[1:2] + vec[6:7]).astype(bf16)
        part = h2.at[own]
        cp = tensor_copy(pc, part, part, tsem.at[6, i], tsem.at[7, i])
        cp.start()
        hcopies[i] = cp
    emit(x2, x2_o, 6)

    def mine_first(i):
        return (i % 2) * 2 + jnp.where(i < 2, c, 1 - c)

    for j in range(4):
        at(f"need{4 + j}")
        need(4 + j)
        if j > 1:
            outs.pop(7 + j - 2).wait()

        def up(i):
            rows = row_tile(mine_first(i))
            u = matmul(h2[rows], weight(4 + j)) + hb[:, j * COLS : (j + 1) * COLS]
            gate = 1.0 / (1.0 + jnp.exp(-1.702 * u))
            act[j, rows] = (u * gate).astype(bf16)
            fac[j % 2, rows] = (gate + 1.702 * u * gate * (1.0 - gate)).astype(bf16)

        lax.fori_loop(0, 2, lambda i, z: (up(i), z)[1], 0)
        at(f"half{j}")
        if j == 0:
            for cp in hcopies:
                cp.wait()
        lax.fori_loop(2, 4, lambda i, z: (up(i), z)[1], 0)
        emit(fac.at[j % 2], fac_o.at[j], 7 + j)
    at("turn_h2")
    outs.pop(1).wait()
    transpose_into(hT, h2)
    emit(hT, h2t_o, 1)
    for j in range(4):
        at(f"grad{j}")
        if j > 1:
            outs.pop(11 + j - 2).wait()

        def weight_grad(i):
            rows = pl.ds(pl.multiple_of(i * 256, 256), 256)
            dw[j % 2, i] = matmul(gT[rows, :], act[j]).astype(bf16).reshape(2, 2, 64, COLS)

        loop(4, weight_grad)
        emit(dw.at[j % 2], dw_o.at[j], 11 + j)
    for j in range(4):
        at(f"need{8 + j}")
        need(8 + j)

        def down(i):
            rows = row_tile(i)
            out = matmul_nt(act[j, rows], weight(8 + j))
            if j > 0:
                out = out + acc[rows]
            acc[rows] = out

        if j < 3:
            loop(4, down)
            continue
        for i in range(2):
            down(2 * i + c)
            out = (acc[row_tile(2 * i + c)] + vec[7:8]).astype(bf16)
            for half in range(2):
                proj[pl.ds(half * SEQ + i * PAD, PAD), 0:COLS] = out[:, half * COLS : (half + 1) * COLS]
            down(2 * i + 1 - c)
            out = acc[row_tile(2 * i + 1 - c)].astype(bf16)
            for half in range(2):
                proj[pl.ds(half * SEQ + i * PAD, PAD), COLS:] = out[:, half * COLS : (half + 1) * COLS]
    emit(proj.at[:, pl.ds(0, COLS)], outc_o, 15)
    emit(proj.at[:, pl.ds(COLS, COLS)], outp_o, 16)
    for cp in outs.values():
        cp.wait()
    if comm:
        big.finish()


def forward_call(comm, args):
    B = lambda *s: pltpu.VMEM(s, bf16)
    F = lambda *s: pltpu.VMEM(s, f32)
    S = lambda *s: pltpu.SemaphoreType.DMA(s)
    A = pl.BlockSpec(memory_space=pl.ANY)
    V = pl.BlockSpec(memory_space=pltpu.VMEM)
    M = pl.BlockSpec(memory_space=pltpu.SMEM)
    sh = jax.ShapeDtypeStruct
    outs = [
        sh((D, ROWS), bf16), sh((D, ROWS), bf16), sh((ROWS, D), bf16),
        sh((ROWS, COLS), bf16), sh((ROWS, COLS), bf16), sh((ROWS, COLS), bf16), sh((ROWS, COLS), bf16),
        sh((2, 8, 1, SEQ), f32), sh((2 * PAD, D), f32), sh((4, ROWS, COLS), bf16), sh((4, 4, 2, 2, 64, COLS), bf16),
        sh((ROWS, COLS), bf16), sh((ROWS, COLS), bf16), sh((8, D), f32),
    ]
    ospecs = [A] * 7 + [V] + [A] * 5 + [V]
    if comm:
        outs = [sh((PIECES, 4, 2, 2, 64, COLS), bf16)] + outs
        ospecs = [A] + ospecs
        ispecs = [V, V, M, V, V, V, V, V, V]
    else:
        ispecs = [V, V, M, V, A, V]
    scratch = [
        B(PIECES, 4, 2, 2, 64, COLS), B(1, 4, 2, 2, 16, 128), F(1, 4 * COLS), B(2, PAD, D), B(ROWS, D), B(ROWS, D),
        B(D, ROWS), B(D, ROWS), B(ROWS, COLS), B(ROWS, COLS), B(ROWS, COLS), B(ROWS, COLS),
        F(2 * SEQ, 128), F(2 * PAD, D), B(ROWS, D), B(2 * PAD, D), B(4, ROWS, COLS), B(2, ROWS, COLS),
        B(2, 4, 2, 2, 64, COLS), F(ROWS, D),
        pltpu.SemaphoreType.DMA, S(32), S(8, 2), S(PIECES, 4), S(PIECES, 4), S(PIECES), S(4),
        S(1, 4), S(1, 4), S(1), S(4),
    ]
    return pl.pallas_call(
        functools.partial(forward_kernel, comm),
        out_shape=outs,
        in_specs=ispecs,
        out_specs=ospecs,
        scratch_shapes=scratch,
        name="forward",
        compiler_params=pltpu.CompilerParams(
            collective_id=0, has_side_effects=True, vmem_limit_bytes=62 * 2**20
        ),
    )(*args)


def backward_kernel(comm, *refs):
    x_ref, mask, vec, lse, wall, h1t_i, h2t_i, g_i, q_i, k_i, v_i, o_i, x2_i, fac_i, dw_i, outp_i, outc_i = refs[:17]
    layer_o, input_o = refs[17:19]
    refs = refs[19:]
    if comm:
        gqkv, gout, gfc1, gfc2, gvec, gfc = refs[:6]
        refs = refs[6:]
    else:
        sums_o, vs_o, fcs_o = refs[:3]
        refs = refs[3:]
    (
        sums, r1, r2, rz, rzz, r3, x2, drecv, dx, stage, delta, vs, fcs, vsum, v1, vz, v3, vpart,
        hT, dh2, fac, du, o, w, free,
        lsem, osem, tsem, s1, s2, sz, s3, ss, t1, tz, t3, tt,
    ) = refs
    pc = Place(comm)
    c = pc.c
    pc.greet()
    big = Scatter(pc, sums, BACKWARD_ROUTES, r1, r2, rz, rzz, r3, s1, s2, sz, s3, ss)

    def done(p, value):
        if p < 4:
            gfc2[:, p * COLS : (p + 1) * COLS] = value
        elif p < 8:
            gfc1[:, (p - 4) * COLS : (p - 3) * COLS] = value
        elif p == 8:
            gout[...] = value
        else:
            gqkv[p - 9] = value

    def at(name):
        if not comm:
            return
        for code in BACKWARD_PLAN.get(name, ()):
            p, what = code // 10, code % 10
            if what == 4:
                big.across(p)
            elif what == 5:
                big.close(p, done)
            else:
                big.step(p, what, done)

    def opened(p):
        if comm:
            big.open(p)

    def fetch(src, dst, i):
        cp = pltpu.make_async_copy(src, dst, lsem.at[i])
        cp.start()
        return cp

    def weight(slot):
        return w[slot].reshape(D, COLS)

    grads = fetch(dw_i, sums.at[pl.ds(0, 4)], 0)
    gcopy = fetch(g_i, dx, 1)
    fcopy = [fetch(fac_i.at[j], fac.at[j], 2 + j) for j in range(2)]
    wcopy = [fetch(wall.at[8], w.at[0], 4), fetch(wall.at[4], w.at[1], 5), fetch(wall.at[9], w.at[2], 6), fetch(wall.at[5], w.at[3], 7)]
    ocopies = []
    for i in range(2):
        cp = tensor_copy(pc, outp_i.at[:, row_tile(i)], drecv.at[:, row_tile(i)], tsem.at[0, i], tsem.at[1, i])
        cp.start()
        ocopies.append(cp)
    x2copy = fetch(x2_i, x2, 8)
    ocopy = fetch(outc_i, o, 9)
    hcopy = fetch(h2t_i, hT, 10)
    vs[...] = jnp.zeros_like(vs)

    def weight_grad(p, right):
        def body(i):
            rows = pl.ds(pl.multiple_of(i * 256, 256), 256)
            sums[p, i] = matmul(hT[rows, :], right[...].reshape(ROWS, COLS)).astype(bf16).reshape(2, 2, 64, COLS)

        loop(4, body)
        opened(p)

    grads.wait()
    for p in range(4):
        opened(p)
    gcopy.wait()
    sent = []
    for j in range(4):
        fcopy[j % 2].wait()
        wcopy[2 * (j % 2)].wait()
        wcopy[2 * (j % 2) + 1].wait()

        def tile(n, inner=True):
            if inner:
                for m in range(4):
                    pl.when(n == m)(lambda: at(f"tile{4 * j + m}"))
            i = (n % 2) * 2 + jnp.where(n < 2, 1 - c, c)
            rows = row_tile(i)
            da = matmul(dx[rows], weight(2 * (j % 2)))
            du[j, rows] = (da * fac[j % 2, rows].astype(f32)).astype(bf16)
            part = matmul_nt(du[j, rows], weight(2 * (j % 2) + 1))
            if j == 0:
                dh2[rows] = part
            else:
                dh2[rows] += part

        if j < 3:
            loop(4, tile)
        else:
            lax.fori_loop(0, 2, lambda n, z: (tile(n), z)[1], 0)
            pl.semaphore_wait(free, 1)
            for i in range(2):
                for half in range(2):
                    cols = slice(half * COLS, (half + 1) * COLS)
                    o[half, row_tile(i)] = dh2[row_tile(2 * i + 1 - c), cols].astype(bf16)
                cp = tensor_copy(pc, o.at[:, row_tile(i)], drecv.at[:, row_tile(i)], tsem.at[2, i], tsem.at[3, i])
                cp.start()
                sent.append(cp)
            lax.fori_loop(2, 4, lambda n, z: (tile(n), z)[1], 0)
        fcs[:, j * COLS : (j + 1) * COLS] = column_sums(du.at[j])
        if j < 2:
            fcopy[j] = fetch(fac_i.at[j + 2], fac.at[j], 2 + j)
            wcopy[2 * j] = fetch(wall.at[10 + j], w.at[2 * j], 4 + 2 * j)
            wcopy[2 * j + 1] = fetch(wall.at[6 + j], w.at[2 * j + 1], 5 + 2 * j)
        elif j == 2:
            wcopy[0] = fetch(wall.at[0], w.at[0], 4)
            wcopy[1] = fetch(wall.at[1], w.at[1], 5)
        else:
            wcopy[2] = fetch(wall.at[2], w.at[2], 6)
            wcopy[3] = fetch(wall.at[3], w.at[3], 7)
        if j == 0:
            at("layer")
            x2copy.wait()
            ocopy.wait()
            for i in range(2):
                ocopies[i].wait()
                for half in range(2):
                    cols = slice(half * COLS, (half + 1) * COLS)
                    total = (
                        x2[row_tile(i), cols]
                        + o[half, row_tile(i)].astype(f32)
                        + drecv[half, row_tile(i)].astype(f32)
                    )
                    stage[i, :, cols] = total[0:HALF].astype(bf16)
            lcopy = pltpu.make_async_copy(stage, layer_o, osem.at[0])
            lcopy.start()
            pl.semaphore_signal(free, inc=1, device_id=pc.dev("c"), device_id_type=MESH)

    def received(i):
        return jnp.concatenate([drecv[0, row_tile(i)], drecv[1, row_tile(i)]], axis=1).astype(f32)

    at("grad4")
    hcopy.wait()
    weight_grad(4, du.at[0])
    copies = []
    for i in range(2):
        at(f"mid{i}")
        sent[i].wait()
        own = row_tile(2 * i + c)
        up = dh2[own] + received(i)
        normed, inverse = normalize(x2[row_tile(i)])
        grad = dx[own].astype(f32)
        total = grad + norm_backward(up, normed, inverse, vec[1:2])
        low = total.astype(bf16)
        x2[row_tile(i)] = total
        dx[own] = low
        cp = tensor_copy(pc, dx.at[own], dx.at[own], tsem.at[4, i], tsem.at[5, i])
        cp.start()
        copies.append(cp)
        vs[5:6] += jnp.sum(up * normed, axis=0, keepdims=True)
        vs[6:7] += jnp.sum(up, axis=0, keepdims=True)
        vs[4:5] += jnp.sum(low.astype(f32), axis=0, keepdims=True)
        vs[7:8] += jnp.sum(grad, axis=0, keepdims=True)
    lcopy.wait()
    xcopy = fetch(x_ref, stage, 8)
    ocopy = fetch(o_i, o, 9)
    for j in range(1, 4):
        at(f"grad{4 + j}")
        weight_grad(4 + j, du.at[j])
        if j == 1:
            qcopy = fetch(q_i, du.at[0], 2)
            kcopy = fetch(k_i, du.at[1], 3)
        elif j == 2:
            vcopy = fetch(v_i, du.at[2], 10)
    q, k, v, do = (du.at[i] for i in range(4))
    at("turn")
    for cp in copies:
        cp.wait()

    def turn(i):
        cols = pl.ds(pl.multiple_of(i * 128, 128), 128)
        hT[cols, :] = dx[:, cols].T

    loop(D // 128, turn)
    ocopy.wait()
    weight_grad(8, o)
    hcopy = fetch(h1t_i, hT, 0)
    at("out")
    wcopy[3].wait()

    def out_back(i):
        do[row_tile(i)] = matmul(dx[row_tile(i)], weight(3)).astype(bf16)

    loop(4, out_back)
    at("delta")
    pick = lax.broadcasted_iota(jnp.int32, (8, COLS), 0) == lax.broadcasted_iota(jnp.int32, (8, COLS), 1) // HEAD_DIM
    pick = pick.astype(f32).astype(bf16)
    mcol = dh2.at[:, pl.ds(0, 128)]
    for i in range(2):
        rows = pl.ds(i * SEQ, SEQ)
        prod = do[rows].astype(f32) * o[i].astype(f32)
        high = prod.astype(bf16)
        low = (prod - high.astype(f32)).astype(bf16)
        part = matmul_nt(pick, high) + matmul_nt(pick, low)
        for h in range(8):
            delta[i, h] = part[h : h + 1]
        mcol[rows] = jnp.broadcast_to(mask[i, 0:1], (128, SEQ)).T
    for cp in (qcopy, kcopy, vcopy):
        cp.wait()
    lane = lax.broadcasted_iota(jnp.int32, (1, 128), 1)

    def attend(n):
        img, head = n // 8, n % 8
        for j in range(16):
            pl.when(n == j)(lambda: at(f"attend{j}"))
        rows = pl.ds(pl.multiple_of(img * SEQ, 16), SEQ)
        cols = pl.ds(pl.multiple_of(head // 2 * 128, 128), 128)
        first = 64 * (head % 2)
        mine = (lane >= first) & (lane < first + 64)
        qb, gb = q[rows, cols], do[rows, cols]
        qm = jnp.where(mine, qb, jnp.zeros_like(qb))
        gm = jnp.where(mine, gb, jnp.zeros_like(gb))
        dq = None
        for t in range(2):
            part = pl.ds(pl.multiple_of(img * SEQ + t * PAD, 16), PAD)
            kb, vb = k[part, cols], v[part, cols]
            p = jnp.exp(matmul_nt(kb, qm) + mcol[part, 0:1] - lse[img, head])
            dp = matmul_nt(vb, gm)
            ds = (p * (dp - delta[img, head])).astype(bf16)
            dv = matmul(p.astype(bf16), gm)
            dk = matmul(ds, qm)
            dqt = matmul_tn(ds, kb)
            dq = dqt if dq is None else dq + dqt
            k[part, cols] = jnp.where(mine, dk.astype(bf16), kb)
            v[part, cols] = jnp.where(mine, dv.astype(bf16), vb)
        q[rows, cols] = jnp.where(mine, (dq * (HEAD_DIM**-0.5)).astype(bf16), qb)

    loop(16, attend)
    hcopy.wait()
    for i, part in enumerate((q, k, v)):
        at(f"grad{9 + i}")
        weight_grad(9 + i, part)
    for i in range(3):
        wcopy[i].wait()

    def back(t):
        rows = row_tile(t)
        total = matmul_nt(q[rows], weight(0))
        total += matmul_nt(k[rows], weight(1))
        total += matmul_nt(v[rows], weight(2))
        return total

    sent = []
    for i in range(2):
        at(f"back{i}")
        part = back(2 * i + 1 - c).astype(bf16)
        for half in range(2):
            o[half, row_tile(i)] = part[:, half * COLS : (half + 1) * COLS]
        cp = tensor_copy(pc, o.at[:, row_tile(i)], drecv.at[:, row_tile(i)], tsem.at[6, i], tsem.at[7, i])
        cp.start()
        sent.append(cp)
    xcopy.wait()
    here = pl.ds(pl.multiple_of(c * COLS, COLS), COLS)
    vs[2:3, here] = column_sums(q)
    vs[3:4, here] = column_sums(v)
    for i in range(2):
        at(f"back{2 + i}")
        up = back(2 * i + c)
        sent[i].wait()
        up = (up + received(i))[0:HALF]
        normed, inverse = normalize(stage[i].astype(f32))
        total = x2[row_tile(i)][0:HALF] + norm_backward(up, normed, inverse, vec[0:1])
        stage[i] = total.astype(bf16)
        vs[0:1] += jnp.sum(up * normed, axis=0, keepdims=True)
        vs[1:2] += jnp.sum(up, axis=0, keepdims=True)
    icopy = pltpu.make_async_copy(stage, input_o, osem.at[1])
    icopy.start()
    if comm:
        at("vectors")
        vsum[...] = jnp.zeros_like(vsum)
        for r in range(GROUP):
            vsum[0, r // 4, (r // 2) % 2, r % 2, 0:8, 0:64] = vs[:, r * 64 : (r + 1) * 64]
        for r in range(GROUP // 2):
            for half in range(2):
                row = fcs[:, (2 * r + half) * 128 : (2 * r + half + 1) * 128]
                for side in range(2):
                    to = r + side * (GROUP // 2)
                    value = jnp.where(c == side, row, jnp.zeros_like(row))
                    vsum[0, to // 4, (to // 2) % 2, to % 2, 8 + half : 9 + half, :] = value
        small = Scatter(pc, vsum, [("P", "x", "y")], v1, None, vz, None, v3, t1, None, tz, t3, tt)
        small.open(0)
        for dist in (3, 2, 1, 0):
            at(f"small{dist}")
            small.step(0, dist, None)

        def keep(p, value):
            vpart[0] = value

        at("small_end")
        small.close(0, keep)
        cp = tensor_copy(pc, vpart.at[0], vpart.at[1], tsem.at[8, 0], tsem.at[9, 0])
        cp.start()
        at("end")
        cp.wait()
        total = vpart[0] + vpart[1]
        gvec[...] = jnp.where(c == 0, total[0:8, 0:32], total[0:8, 32:64])
        gfc[...] = jnp.where(c == 0, total[8:9], total[9:10])
        small.finish()
        big.finish()
    else:
        pairs = ((sums, sums_o), (vs, vs_o), (fcs, fcs_o))
        copies = [pltpu.make_async_copy(a, b, osem.at[2 + i]) for i, (a, b) in enumerate(pairs)]
        for cp in copies:
            cp.start()
        for cp in copies:
            cp.wait()
    icopy.wait()


def backward_call(comm, args):
    B = lambda *s: pltpu.VMEM(s, bf16)
    F = lambda *s: pltpu.VMEM(s, f32)
    S = lambda *s: pltpu.SemaphoreType.DMA(s)
    A = pl.BlockSpec(memory_space=pl.ANY)
    V = pl.BlockSpec(memory_space=pltpu.VMEM)
    sh = jax.ShapeDtypeStruct
    outs = [sh((2, HALF, D), bf16), sh((2, HALF, D), bf16)]
    ospecs = [A, A]
    if comm:
        outs += [
            sh((3, 64, COLS), f32), sh((64, COLS), f32), sh((64, 4 * COLS), f32), sh((64, 4 * COLS), f32),
            sh((8, 32), f32), sh((1, 128), f32),
        ]
        ospecs += [V] * 6
    else:
        outs += [sh((PIECES, 4, 2, 2, 64, COLS), bf16), sh((8, D), f32), sh((1, 4 * COLS), f32)]
        ospecs += [A] * 3
    ispecs = [A, V, V, V] + [A] * 13
    one = (4, 2, 2, 64, COLS)
    scratch = [
        B(PIECES, *one), B(PIECES, 4, 2, 64, COLS), B(4, 4, 64, COLS), B(8, 5, 2, 64, COLS), B(4, 5, 64, COLS),
        B(8, 64, COLS),
        F(2 * PAD, D), B(2, SEQ, COLS), B(ROWS, D), B(2, HALF, D), F(2, 8, 1, SEQ), F(8, D), F(1, 4 * COLS),
        F(1, 4, 2, 2, 16, 128), F(1, 4, 2, 16, 128), F(1, 5, 2, 16, 128), F(1, 16, 128), F(2, 16, 128),
        B(D, ROWS), F(ROWS, D), B(2, ROWS, COLS), B(4, ROWS, COLS), B(2, SEQ, COLS), B(4, *one),
        pltpu.SemaphoreType.REGULAR, S(11), S(5), S(10, 2), S(PIECES, 4), S(4, 4), S(PIECES, 5), S(PIECES), S(4), S(1, 4), S(1, 5), S(1), S(4),
    ]
    return pl.pallas_call(
        functools.partial(backward_kernel, comm),
        out_shape=outs,
        in_specs=ispecs,
        out_specs=ospecs,
        scratch_shapes=scratch,
        name="backward",
        compiler_params=pltpu.CompilerParams(
            collective_id=1, has_side_effects=True, vmem_limit_bytes=63 * 2**20
        ),
    )(*args)


def split_cols(m):
    return jnp.transpose(m.reshape(m.shape[0], m.shape[1] // COLS, COLS), (1, 0, 2))


def shards(layer_in, out_grad, key_valid, image_live, w_qkv, w_out, w_fc1, w_fc2, norm_gains, bias_rows, fc_bias):
    comm = lax.axis_size("dp") == GROUP
    valid = jnp.pad(key_valid.reshape(2, 2, HALF), ((0, 0), (0, 0), (0, PAD - HALF))).reshape(2, 1, SEQ)
    mask = jnp.broadcast_to(jnp.where(valid > 0, 0.0, -1e9).astype(f32), (2, 8, SEQ))
    rows = jnp.concatenate([norm_gains, bias_rows], axis=0)
    if comm:
        low = jnp.pad(rows, ((0, 8), (0, 64)))
        small = lax.dynamic_update_slice(low, fc_bias.reshape(2, 128), (8, 0))
        made = forward_call(True, (layer_in, out_grad, image_live, mask, w_qkv, w_out.T, w_fc1, w_fc2.T, small))
        wall, made = made[0], made[1:]
    else:
        local = jnp.concatenate([w_qkv, w_out.T[None], split_cols(w_fc1), split_cols(w_fc2.T)], axis=0)
        wall = lax.all_gather(local, "dp", axis=1, tiled=True).reshape(PIECES, 4, 2, 2, 64, COLS)
        rows = lax.all_gather(rows, "dp", axis=1, tiled=True)
        hidden = lax.all_gather(fc_bias, "dp", axis=0, tiled=True)
        small = jnp.pad(jnp.transpose(rows.reshape(8, GROUP, 64), (1, 0, 2)), ((0, 0), (0, 8), (0, 64)))
        small = lax.dynamic_update_slice(small, hidden.reshape(GROUP, 2, 128), (0, 8, 0))
        made = forward_call(False, (layer_in, out_grad, image_live, mask, wall, small))
    h1t, h2t, g, q, k, v, o, lse, x2, fac, dw, outp, outc, vec = made
    o, outp, outc = (m.reshape(2, SEQ, COLS) for m in (o, outp, outc))
    back = backward_call(
        comm, (layer_in, mask, vec, lse, wall, h1t, h2t, g, q, k, v, o, x2, fac, dw, outp, outc)
    )
    layer_out, input_grad = back[:2]
    if comm:
        gqkv, gout, gfc1, gfc2, gvec, gfc = back[2:]
        return (layer_out, input_grad, gqkv, gout.T, gfc1, gfc2.T, gvec, gfc.reshape(128))
    sums, vs, fcs = back[2:]
    mine = lax.psum_scatter(sums.reshape(PIECES, D, COLS), "dp", scatter_dimension=1, tiled=True).astype(f32)
    down = jnp.transpose(mine[0:4], (0, 2, 1)).reshape(4 * COLS, -1)
    up = jnp.transpose(mine[4:8], (1, 0, 2)).reshape(-1, 4 * COLS)
    vector = lax.psum_scatter(vs, ("dp", "tensor"), scatter_dimension=1, tiled=True)
    whole = lax.dynamic_update_slice(jnp.zeros((FF,), f32), fcs[0], (lax.axis_index("tensor") * 4 * COLS,))
    hidden = lax.psum_scatter(whole, ("dp", "tensor"), scatter_dimension=0, tiled=True)
    return (layer_out, input_grad, mine[9:12], mine[8].T, up, down, vector, hidden)


def solution(mesh):
    return jax.shard_map(
        shards,
        mesh=mesh,
        in_specs=(
            P("dp", "tensor", None),
            P("dp", "tensor", None),
            P("dp", None),
            P("dp"),
            P(None, "dp", "tensor"),
            P("tensor", "dp"),
            P("dp", "tensor"),
            P("tensor", "dp"),
            P(None, "dp"),
            P(None, "dp"),
            P("dp"),
        ),
        out_specs=(
            P("dp", "tensor", None),
            P("dp", "tensor", None),
            P(None, "dp", "tensor"),
            P("tensor", "dp"),
            P("dp", "tensor"),
            P("tensor", "dp"),
            P(None, ("dp", "tensor")),
            P(("dp", "tensor")),
        ),
        check_vma=False,
    )
```

```python
import functools

import jax
import jax.numpy as jnp
from jax import lax
from jax.experimental import pallas as pl
from jax.experimental.pallas import tpu as pltpu
from jax.sharding import PartitionSpec as P

D = 1024
HEAD_DIM = 64
FF = 4096
EPSILON = 1e-05
MESH = pl.DeviceIdType.MESH
bf16 = jnp.bfloat16
f32 = jnp.float32

PIECES = 12
COLS = 512
HALF = 292
PAD = 304
SEQ = 2 * PAD
ROWS = 4 * PAD
GROUP = 16


def matmul(a, b):
    return lax.dot_general(a, b, (((1,), (0,)), ((), ())), preferred_element_type=f32)


def matmul_nt(a, b):
    return lax.dot_general(a, b, (((1,), (1,)), ((), ())), preferred_element_type=f32)


def matmul_tn(a, b):
    return lax.dot_general(a, b, (((0,), (0,)), ((), ())), preferred_element_type=f32)


def column_sums(ref):
    return matmul(jnp.ones((8, ref.shape[0]), bf16), ref[...])[0:1]


def normalize(values):
    centred = values - jnp.mean(values, axis=-1, keepdims=True)
    inverse = lax.rsqrt(jnp.mean(centred * centred, axis=-1, keepdims=True) + EPSILON)
    return centred * inverse, inverse


def norm_backward(upstream, normed, inverse, gain_row):
    scaled = upstream * gain_row
    return inverse * (
        scaled
        - jnp.mean(scaled, axis=-1, keepdims=True)
        - normed * jnp.mean(scaled * normed, axis=-1, keepdims=True)
    )


class Place:
    def __init__(self, comm):
        self.comm = comm
        self.dp = lax.axis_index("dp")
        self.c = lax.axis_index("tensor")
        self.z = self.dp // 4
        self.y = (self.dp // 2) % 2
        self.x = self.dp % 2

    def dev(self, d):
        if d == "x":
            t = self.dp + 1 - 2 * self.x
        elif d == "y":
            t = self.dp + 2 - 4 * self.y
        elif d == "u":
            t = self.dp + 4
        elif d == "d":
            t = self.dp - 4
        else:
            return (self.dp, 1 - self.c)
        return (t, self.c)

    def greet(self):
        bar = pltpu.get_barrier_semaphore()

        def hail(d):
            pl.semaphore_signal(bar, inc=1, device_id=self.dev(d), device_id_type=MESH)

        hail("c")
        if not self.comm:
            pl.semaphore_wait(bar, 1)
            return
        hail("x")
        hail("y")
        pl.when(self.z < 3)(lambda: hail("u"))
        pl.when(self.z > 0)(lambda: hail("d"))
        pl.when((self.z == 0) | (self.z == 3))(lambda: pl.semaphore_wait(bar, 4))
        pl.when((self.z > 0) & (self.z < 3))(lambda: pl.semaphore_wait(bar, 5))


def wait_bytes(ref, sem):
    pltpu.make_async_copy(ref, ref, sem).wait()


class Gather:
    def __init__(self, pc, wall, routes, zs, fs, ts, ss):
        self.pc, self.wall, self.routes = pc, wall, routes
        self.zs, self.fs, self.ts, self.ss = zs, fs, ts, ss

    def copy(self, ref, d, rsem):
        return pltpu.make_async_remote_copy(
            src_ref=ref,
            dst_ref=ref,
            send_sem=self.ss.at["xyud".index(d)],
            recv_sem=rsem,
            device_id=self.pc.dev(d),
            device_id_type=MESH,
        )

    def block(self, p, zz):
        return self.wall.at[p, zz, self.pc.y, self.pc.x]

    def pair(self, p, zz, d1):
        if d1 == "x":
            return self.wall.at[p, zz, self.pc.y]
        return self.wall.at[p, zz, :, self.pc.x]

    def beside(self, p, zz, d):
        if d == "x":
            return self.wall.at[p, zz, self.pc.y, 1 - self.pc.x]
        return self.wall.at[p, zz, 1 - self.pc.y, self.pc.x]

    def part(self, p, zz):
        kind, d1, _ = self.routes[p]
        return self.block(p, zz) if kind == "Z" else self.pair(p, zz, d1)

    def pass_on(self, p, zz, way):
        cond = self.pc.z < 3 if way == "u" else self.pc.z > 0
        pl.when(cond)(lambda: self.copy(self.part(p, zz), way, self.zs.at[p, zz]).start())

    def to_second(self, p, zz):
        _, d1, d2 = self.routes[p]
        self.copy(self.pair(p, zz, d1), d2, self.ts.at[p]).start()

    def open(self, p):
        kind, d1, d2 = self.routes[p]
        z = self.pc.z
        if kind == "Z":
            self.pass_on(p, z, "u")
            self.pass_on(p, z, "d")
            self.copy(self.block(p, z), d1, self.fs.at[p, z]).start()
        else:
            self.copy(self.block(p, z), d1, self.fs.at[p, 0]).start()

    def first(self, p, zz):
        _, d1, _ = self.routes[p]
        sem = self.fs.at[p, zz] if self.routes[p][0] == "Z" else self.fs.at[p, 0]
        wait_bytes(self.beside(p, zz, d1), sem)

    def step(self, p, dist):
        kind, d1, d2 = self.routes[p]
        z = self.pc.z

        def along(src, way):
            wait_bytes(self.part(p, src), self.zs.at[p, src])
            self.pass_on(p, src, way)
            if kind == "Z":
                self.copy(self.block(p, src), d1, self.fs.at[p, src]).start()
            else:
                self.to_second(p, src)

        def arrived(src):
            self.first(p, src)
            self.to_second(p, src)

        if kind == "P" and dist == 0:
            self.first(p, z)
            self.pass_on(p, z, "u")
            self.pass_on(p, z, "d")
            self.to_second(p, z)
            return
        if 1 <= dist <= 3:
            pl.when(z - dist >= 0)(lambda: along(z - dist, "u"))
            pl.when(z + dist <= 3)(lambda: along(z + dist, "d"))
        if kind == "Z":
            if dist == 1:
                arrived(z)
            elif dist > 1:
                pl.when(z - dist + 1 >= 0)(lambda: arrived(z - dist + 1))
                pl.when(z + dist - 1 <= 3)(lambda: arrived(z + dist - 1))

    def close(self, p):
        d2 = self.routes[p][2]
        if d2 == "y":
            wait_bytes(self.wall.at[p, :, 1 - self.pc.y], self.ts.at[p])
        else:
            wait_bytes(self.wall.at[p, :, :, 1 - self.pc.x], self.ts.at[p])

    def drain(self, n, sem):
        while n >= 16:
            wait_bytes(self.wall.at[0], sem)
            n -= 16
        while n >= 4:
            wait_bytes(self.wall.at[0, 0], sem)
            n -= 4
        while n:
            wait_bytes(self.wall.at[0, 0, 0, 0], sem)
            n -= 1

    def finish(self):
        sent = {"x": 0, "y": 0, "z": 0}
        for kind, d1, d2 in self.routes:
            sent[d1] += 4 if kind == "Z" else 1
            sent[d2] += 8
            sent["z"] += 1 if kind == "Z" else 2
        self.drain(sent["x"], self.ss.at[0])
        self.drain(sent["y"], self.ss.at[1])
        for k in range(3):
            pl.when(self.pc.z == k)(lambda: self.drain(sent["z"] * (k + 1), self.ss.at[2]))
            pl.when(self.pc.z == k + 1)(lambda: self.drain(sent["z"] * (3 - k), self.ss.at[3]))


class Scatter:
    def __init__(self, pc, sums, routes, first, second, line, single, last, s1, s2, sz, s3, ss):
        self.pc, self.sums, self.routes = pc, sums, routes
        self.r1, self.r2, self.rz, self.rzz, self.r3 = first, second, line, single, last
        self.s1, self.s2, self.sz, self.s3, self.ss = s1, s2, sz, s3, ss
        self.rank = [sum(r[0] == "Z" for r in routes[:p]) for p in range(len(routes))]

    def copy(self, src, dst, d, rsem):
        return pltpu.make_async_remote_copy(
            src_ref=src,
            dst_ref=dst,
            send_sem=self.ss.at["xyud".index(d)],
            recv_sem=rsem,
            device_id=self.pc.dev(d),
            device_id_type=MESH,
        )

    def pair(self, p, t, d, other):
        pc = self.pc
        if d == "y":
            return self.sums.at[p, t, (1 - pc.y) if other else pc.y]
        return self.sums.at[p, t, :, (1 - pc.x) if other else pc.x]

    def one(self, p, t, flip=None):
        pc = self.pc
        return self.sums.at[p, t, (1 - pc.y) if flip == "y" else pc.y, (1 - pc.x) if flip == "x" else pc.x]

    def each(self, dist, fn):
        z = self.pc.z
        if dist == 0:
            fn(z, None)
            return
        pl.when(z + dist <= 3)(lambda: fn(z + dist, "u"))
        pl.when(z - dist >= 0)(lambda: fn(z - dist, "d"))

    def add(self, dst, *others):
        total = dst[...]
        for o in others:
            total = total + o[...]
        dst[...] = total

    def open(self, p):
        d2 = self.routes[p][2]
        for dist in (3, 2, 1, 0):
            self.each(
                dist,
                lambda t, _: self.copy(self.pair(p, t, d2, True), self.r1.at[p, t], d2, self.s1.at[p, t]).start(),
            )

    def across(self, p):
        _, d1, d2 = self.routes[p]

        def go(t, _):
            wait_bytes(self.r1.at[p, t], self.s1.at[p, t])
            self.add(self.pair(p, t, d2, False), self.r1.at[p, t])
            self.copy(self.one(p, t, d1), self.r2.at[self.rank[p], t], d1, self.s2.at[self.rank[p], t]).start()

        for dist in (3, 2, 1, 0):
            self.each(dist, go)

    def step(self, p, dist, done):
        kind, d1, d2 = self.routes[p]
        z = self.pc.z
        if kind == "Z":
            view = lambda t: self.one(p, t)
            slot = lambda i: self.rzz.at[self.rank[p], i]
        else:
            view = lambda t: self.pair(p, t, d2, False)
            slot = lambda i: self.rz.at[p - self.rank[p], i]

        def go(t, way):
            if kind == "Z":
                wait_bytes(self.r2.at[self.rank[p], t], self.s2.at[self.rank[p], t])
                mine = self.r2.at[self.rank[p], t]
            else:
                wait_bytes(self.r1.at[p, t], self.s1.at[p, t])
                mine = self.r1.at[p, t]

            def arrival(i):
                wait_bytes(slot(i), self.sz.at[p, i])
                return slot(i)

            if way == "u":
                pl.when(z > 0)(lambda: self.add(view(t), mine, arrival(t + 1)))
                pl.when(z == 0)(lambda: self.add(view(t), mine))
                self.copy(view(t), slot(t + 1), "u", self.sz.at[p, t + 1]).start()
            elif way == "d":
                pl.when(z < 3)(lambda: self.add(view(t), mine, arrival(t)))
                pl.when(z == 3)(lambda: self.add(view(t), mine))
                self.copy(view(t), slot(t), "d", self.sz.at[p, t]).start()
            else:
                pl.when(z == 0)(lambda: self.add(view(z), mine, arrival(z)))
                pl.when(z == 3)(lambda: self.add(view(z), mine, arrival(z + 1)))
                pl.when((z > 0) & (z < 3))(lambda: self.add(view(z), mine, arrival(z), arrival(z + 1)))
                if kind == "Z":
                    done(p, self.one(p, z)[...].astype(f32))
                else:
                    self.copy(self.one(p, z, d1), self.r3.at[p - self.rank[p]], d1, self.s3.at[p]).start()

        self.each(dist, go)

    def close(self, p, done):
        if self.routes[p][0] == "P":
            wait_bytes(self.r3.at[p - self.rank[p]], self.s3.at[p])
            done(p, self.one(p, self.pc.z)[...].astype(f32) + self.r3[p - self.rank[p]].astype(f32))

    def drain(self, n, sem):
        while n >= 16:
            wait_bytes(self.sums.at[0], sem)
            n -= 16
        while n >= 4:
            wait_bytes(self.sums.at[0, 0], sem)
            n -= 4
        while n:
            wait_bytes(self.sums.at[0, 0, 0, 0], sem)
            n -= 1

    def finish(self):
        sent = {"x": 0, "y": 0, "z": 0}
        for kind, d1, d2 in self.routes:
            sent[d1] += 4 if kind == "Z" else 1
            sent[d2] += 8
            sent["z"] += 1 if kind == "Z" else 2
        self.drain(sent["x"], self.ss.at[0])
        self.drain(sent["y"], self.ss.at[1])
        for k in range(3):
            pl.when(self.pc.z == k)(lambda: self.drain(sent["z"] * (3 - k), self.ss.at[2]))
            pl.when(self.pc.z == k + 1)(lambda: self.drain(sent["z"] * (k + 1), self.ss.at[3]))


def row_tile(i):
    return pl.ds(pl.multiple_of(i * PAD, 16), PAD)


def loop(count, body):
    def run(i, carry):
        body(i)
        return carry

    lax.fori_loop(0, count, run, 0)


def tensor_copy(pc, src, dst, send, recv):
    return pltpu.make_async_remote_copy(
        src_ref=src, dst_ref=dst, send_sem=send, recv_sem=recv, device_id=pc.dev("c"), device_id_type=MESH
    )


LATE = (
    ((0, 0), (0, 1), (1, 0), (1, 1)),
    ((2, 0), (2, 1), (2, 2), (0, 2)),
    ((1, 2), (0, 3), (1, 3), (2, 3)),
)

FORWARD_ROUTES = (
    ("Z", "y", "x"),
    ("P", "x", "y"),
    ("Z", "y", "x"),
    ("P", "x", "y"),
    ("P", "y", "x"),
    ("Z", "x", "y"),
    ("P", "y", "x"),
    ("Z", "x", "y"),
    ("P", "y", "x"),
    ("P", "x", "y"),
    ("P", "x", "y"),
    ("P", "y", "x"),
)
FORWARD_PLAN = {
    "small0": (21,),
    "small1": (40, 1,),
    "small2": (10, 22, 2, 11, 30,),
    "small4": (51, 3, 12, 23, 31,),
    "norm0": (13, 100,),
    "norm1": (4, 90, 32,),
    "turn_g": (71,),
    "wait_h": (24,),
    "turn_h1": (52, 110, 60,),
    "attend2": (72,),
    "attend3": (41,),
    "attend4": (80, 33, 53,),
    "attend6": (42,),
    "attend7": (73, 61, 91,),
    "need3": (43,),
    "own3": (54, 74,),
    "mid1": (62, 101,),
    "need4": (63, 81,),
    "need5": (92,),
    "need7": (82,),
    "turn_h2": (111, 93, 102,),
    "grad1": (83,),
    "grad3": (112,),
    "need8": (103,),
    "need9": (113,),
}
BACKWARD_ROUTES = (
    ("P", "x", "y"),
    ("P", "x", "y"),
    ("P", "y", "x"),
    ("Z", "y", "x"),
    ("P", "x", "y"),
    ("P", "y", "x"),
    ("Z", "y", "x"),
    ("Z", "x", "y"),
    ("P", "y", "x"),
    ("P", "x", "y"),
    ("P", "y", "x"),
    ("Z", "x", "y"),
)
BACKWARD_PLAN = {
    "layer": (3,),
    "tile7": (23, 2,),
    "tile12": (22,),
    "tile15": (13, 1,),
    "mid1": (21,),
    "grad5": (12,),
    "grad7": (43, 34,),
    "turn": (53,),
    "out": (42,),
    "attend0": (52, 33,),
    "attend1": (11,),
    "attend3": (51,),
    "attend6": (32,),
    "attend7": (41,),
    "attend8": (83, 31,),
    "attend11": (93, 64, 82, 40,),
    "attend12": (20, 92,),
    "attend13": (0,),
    "attend14": (103, 63,),
    "grad11": (81,),
    "back0": (10, 91, 74, 102, 30,),
    "back3": (62,),
    "vectors": (73,),
    "small3": (90, 101,),
    "small2": (114, 72,),
    "small1": (50, 113, 61, 5,),
    "small0": (15, 25, 80, 112, 100, 71,),
    "small_end": (95, 45, 111, 55,),
    "end": (70, 105, 85, 60, 110,),
}


def forward_kernel(comm, *refs):
    if comm:
        x_ref, go_ref, live, mask, wq, wo, w1, w2, sml = refs[:9]
        wall_o = refs[9]
        refs = refs[10:]
    else:
        x_ref, go_ref, live, mask, wall_i, smalls_in = refs[:6]
        refs = refs[6:]
    (
        h1t_o, h2t_o, g_o, q_o, k_o, v_o, o_o, lse_o, x2_o, fac_o, dw_o, outp_o, outc_o, vec,
        wall, smalls, hb, xp, h1, g, gT, hT, q, k, v, o, lse, x2, proj, precv, act, fac, dw, acc,
        lsem, osem, tsem, zs, fs, ts, ss, vzs, vfs, vts, vss,
    ) = refs
    pc = Place(comm)
    c = pc.c
    pc.greet()
    big = Gather(pc, wall, FORWARD_ROUTES, zs, fs, ts, ss)
    outs = {}

    def emit(src, dst, i):
        outs[i] = pltpu.make_async_copy(src, dst, osem.at[i])
        outs[i].start()

    def at(name):
        if comm:
            for code in FORWARD_PLAN.get(name, ()):
                big.step(code // 10, code % 10)

    def need(p):
        if comm:
            big.close(p)
            emit(wall.at[p], wall_o.at[p], 20 + p)

    def weight(p):
        return wall[p].reshape(D, COLS)

    if comm:
        smalls[0, pc.z, pc.y, pc.x] = sml[...]
        small = Gather(pc, smalls, [("P", "x", "y")], vzs, vfs, vts, vss)
        small.open(0)
        for i in range(3):
            wall[i, pc.z, pc.y, pc.x] = wq[i]
        wall[3, pc.z, pc.y, pc.x] = wo[...]
        for i in range(4):
            wall[4 + i, pc.z, pc.y, pc.x] = w1[:, i * COLS : (i + 1) * COLS]
            wall[8 + i, pc.z, pc.y, pc.x] = w2[:, i * COLS : (i + 1) * COLS]
        for p in range(PIECES):
            big.open(p)
    else:
        whole = pltpu.make_async_copy(wall_i, wall, lsem)
        whole.start()

    gcopies = []
    for i in range(2):
        rows = go_ref[i].astype(f32) * live[i].astype(f32)
        start = pl.multiple_of((2 * i + c) * PAD, 16)
        g[pl.ds(start + HALF - 4, PAD - HALF + 4)] = jnp.zeros((PAD - HALF + 4, D), bf16)
        g[pl.ds(start, HALF)] = rows.astype(bf16)
        part = g.at[row_tile(2 * i + c)]
        cp = tensor_copy(pc, part, part, tsem.at[0, i], tsem.at[1, i])
        cp.start()
        gcopies.append(cp)
        xp[i, pl.ds(HALF - 4, PAD - HALF + 4)] = jnp.zeros((PAD - HALF + 4, D), bf16)
        xp[i, pl.ds(0, HALF)] = x_ref[i]

    if comm:
        for dist in range(4):
            at(f"small{dist}")
            small.step(0, dist)
        at("small4")
        small.close(0)
        small.finish()
        blocks = [smalls[0, r // 4, (r // 2) % 2, r % 2] for r in range(GROUP)]
    else:
        blocks = [smalls_in[r] for r in range(GROUP)]
        whole.wait()
    for r in range(GROUP):
        vec[:, r * 64 : (r + 1) * 64] = blocks[r][0:8, 0:64].astype(f32)
    for r in range(GROUP // 2):
        both = jnp.where(c == 0, blocks[r][8:10].astype(f32), blocks[r + GROUP // 2][8:10].astype(f32))
        for i in range(2):
            hb[:, r * 256 + i * 128 : r * 256 + (i + 1) * 128] = both[i : i + 1]

    hcopies = []
    for i in range(2):
        at(f"norm{i}")
        normed, _ = normalize(xp[i].astype(f32))
        h1[row_tile(2 * i + c)] = (normed * vec[0:1] + vec[2:3]).astype(bf16)
        part = h1.at[row_tile(2 * i + c)]
        cp = tensor_copy(pc, part, part, tsem.at[2, i], tsem.at[3, i])
        cp.start()
        hcopies.append(cp)
    for cp in gcopies:
        cp.wait()
    emit(g, g_o, 0)

    def transpose_into(dst, src):
        def body(i):
            cols = pl.ds(pl.multiple_of(i * 128, 128), 128)
            dst[cols, :] = src[:, cols].T

        loop(D // 128, body)

    at("turn_g")
    transpose_into(gT, g)
    at("wait_h")
    for cp in hcopies:
        cp.wait()
    at("turn_h1")
    transpose_into(hT, h1)
    emit(hT, h1t_o, 1)

    qcol = pl.ds(pl.multiple_of(c * COLS, COLS), COLS)
    for p in range(3):
        at(f"need{p}")
        need(p)
        dst = (q, k, v)[p]

        def project(i):
            out = matmul(h1[row_tile(i)], weight(p))
            if p == 0:
                out = (out + vec[3:4, qcol]) * (HEAD_DIM**-0.5)
            elif p == 2:
                out = out + vec[4:5, qcol]
            dst[row_tile(i)] = out.astype(bf16)

        loop(4, project)
        emit(dst, (q_o, k_o, v_o)[p], 2 + p)

    lane = lax.broadcasted_iota(jnp.int32, (1, 128), 1)

    def attend(n):
        img, pair = n // 4, n % 4
        for j in range(8):
            pl.when(n == j)(lambda: at(f"attend{j}"))
        rows = pl.ds(pl.multiple_of(img * SEQ, 16), SEQ)
        cols = pl.ds(pl.multiple_of(pair * 128, 128), 128)
        qb, kb, vb = q[rows, cols], k[rows, cols], v[rows, cols]
        bias = mask[img, 0:1, :]
        mixed = []
        totals = lse[rows]
        for h in range(2):
            mine = (lane >= 64 * h) & (lane < 64 * h + 64)
            s = matmul_nt(jnp.where(mine, qb, jnp.zeros_like(qb)), kb) + bias
            top = jnp.max(s, axis=-1, keepdims=True)
            e = jnp.exp(s - top)
            total = jnp.sum(e, axis=-1, keepdims=True)
            mixed.append(matmul(e.astype(bf16), vb) / total)
            totals = jnp.where(lane == 2 * pair + h, top + jnp.log(total), totals)
        lse[rows] = totals
        o[rows, cols] = jnp.where(lane < 64, mixed[0], mixed[1]).astype(bf16)

    lse[...] = jnp.zeros_like(lse)
    loop(8, attend)
    emit(o, o_o, 5)

    h2 = h1
    at("need3")
    need(3)
    pcopies = []
    for i in range(2):
        other = row_tile(2 * i + 1 - c)
        proj[other] = matmul_nt(o[other], weight(3)).astype(bf16)
        cp = tensor_copy(pc, proj.at[other], precv.at[row_tile(i)], tsem.at[4, i], tsem.at[5, i])
        cp.start()
        pcopies.append(cp)
    at("own3")
    for i in range(2):
        own = row_tile(2 * i + c)
        proj[own] = matmul_nt(o[own], weight(3)).astype(bf16)
    for i in range(2):
        turned = lse[pl.ds(i * SEQ, SEQ)].T
        for h in range(8):
            lse_o[i, h] = turned[h : h + 1]
    for i in range(2):
        at(f"mid{i}")
        pcopies[i].wait()
        own = row_tile(2 * i + c)
        mid = xp[i].astype(f32) + proj[own].astype(f32) + precv[row_tile(i)].astype(f32) + vec[5:6]
        x2[row_tile(i)] = mid
        normed, _ = normalize(mid)
        h2[own] = (normed * vec[1:2] + vec[6:7]).astype(bf16)
        part = h2.at[own]
        cp = tensor_copy(pc, part, part, tsem.at[6, i], tsem.at[7, i])
        cp.start()
        hcopies[i] = cp
    emit(x2, x2_o, 6)

    def mine_first(i):
        return (i % 2) * 2 + jnp.where(i < 2, c, 1 - c)

    for j in range(4):
        at(f"need{4 + j}")
        need(4 + j)
        if j > 1:
            outs.pop(7 + j - 2).wait()

        def up(i):
            rows = row_tile(mine_first(i))
            u = matmul(h2[rows], weight(4 + j)) + hb[:, j * COLS : (j + 1) * COLS]
            gate = 1.0 / (1.0 + jnp.exp(-1.702 * u))
            act[j, rows] = (u * gate).astype(bf16)
            fac[j % 2, rows] = (gate + 1.702 * u * gate * (1.0 - gate)).astype(bf16)

        lax.fori_loop(0, 2, lambda i, z: (up(i), z)[1], 0)
        at(f"half{j}")
        if j == 0:
            for cp in hcopies:
                cp.wait()
        lax.fori_loop(2, 4, lambda i, z: (up(i), z)[1], 0)
        emit(fac.at[j % 2], fac_o.at[j], 7 + j)
    at("turn_h2")
    outs.pop(1).wait()
    transpose_into(hT, h2)
    emit(hT, h2t_o, 1)
    for j in range(4):
        at(f"grad{j}")
        if j > 1:
            outs.pop(11 + j - 2).wait()

        def weight_grad(i):
            rows = pl.ds(pl.multiple_of(i * 256, 256), 256)
            dw[j % 2, i] = matmul(gT[rows, :], act[j]).astype(bf16).reshape(2, 2, 64, COLS)

        loop(4, weight_grad)
        emit(dw.at[j % 2], dw_o.at[j], 11 + j)
    for j in range(4):
        at(f"need{8 + j}")
        need(8 + j)

        def down(i):
            rows = row_tile(i)
            out = matmul_nt(act[j, rows], weight(8 + j))
            if j > 0:
                out = out + acc[rows]
            acc[rows] = out

        if j < 3:
            loop(4, down)
            continue
        for i in range(2):
            down(2 * i + c)
            out = (acc[row_tile(2 * i + c)] + vec[7:8]).astype(bf16)
            for half in range(2):
                proj[pl.ds(half * SEQ + i * PAD, PAD), 0:COLS] = out[:, half * COLS : (half + 1) * COLS]
            down(2 * i + 1 - c)
            out = acc[row_tile(2 * i + 1 - c)].astype(bf16)
            for half in range(2):
                proj[pl.ds(half * SEQ + i * PAD, PAD), COLS:] = out[:, half * COLS : (half + 1) * COLS]
    emit(proj.at[:, pl.ds(0, COLS)], outc_o, 15)
    emit(proj.at[:, pl.ds(COLS, COLS)], outp_o, 16)
    for cp in outs.values():
        cp.wait()
    if comm:
        big.finish()


def forward_call(comm, args):
    B = lambda *s: pltpu.VMEM(s, bf16)
    F = lambda *s: pltpu.VMEM(s, f32)
    S = lambda *s: pltpu.SemaphoreType.DMA(s)
    A = pl.BlockSpec(memory_space=pl.ANY)
    V = pl.BlockSpec(memory_space=pltpu.VMEM)
    M = pl.BlockSpec(memory_space=pltpu.SMEM)
    sh = jax.ShapeDtypeStruct
    outs = [
        sh((D, ROWS), bf16), sh((D, ROWS), bf16), sh((ROWS, D), bf16),
        sh((ROWS, COLS), bf16), sh((ROWS, COLS), bf16), sh((ROWS, COLS), bf16), sh((ROWS, COLS), bf16),
        sh((2, 8, 1, SEQ), f32), sh((2 * PAD, D), f32), sh((4, ROWS, COLS), bf16), sh((4, 4, 2, 2, 64, COLS), bf16),
        sh((ROWS, COLS), bf16), sh((ROWS, COLS), bf16), sh((8, D), f32),
    ]
    ospecs = [A] * 7 + [V] + [A] * 5 + [V]
    if comm:
        outs = [sh((PIECES, 4, 2, 2, 64, COLS), bf16)] + outs
        ospecs = [A] + ospecs
        ispecs = [V, V, M, V, V, V, V, V, V]
    else:
        ispecs = [V, V, M, V, A, V]
    scratch = [
        B(PIECES, 4, 2, 2, 64, COLS), B(1, 4, 2, 2, 16, 128), F(1, 4 * COLS), B(2, PAD, D), B(ROWS, D), B(ROWS, D),
        B(D, ROWS), B(D, ROWS), B(ROWS, COLS), B(ROWS, COLS), B(ROWS, COLS), B(ROWS, COLS),
        F(2 * SEQ, 128), F(2 * PAD, D), B(ROWS, D), B(2 * PAD, D), B(4, ROWS, COLS), B(2, ROWS, COLS),
        B(2, 4, 2, 2, 64, COLS), F(ROWS, D),
        pltpu.SemaphoreType.DMA, S(32), S(8, 2), S(PIECES, 4), S(PIECES, 4), S(PIECES), S(4),
        S(1, 4), S(1, 4), S(1), S(4),
    ]
    return pl.pallas_call(
        functools.partial(forward_kernel, comm),
        out_shape=outs,
        in_specs=ispecs,
        out_specs=ospecs,
        scratch_shapes=scratch,
        name="forward",
        compiler_params=pltpu.CompilerParams(
            collective_id=0, has_side_effects=True, vmem_limit_bytes=62 * 2**20
        ),
    )(*args)


def backward_kernel(comm, *refs):
    x_ref, mask, vec, lse, wall, h1t_i, h2t_i, g_i, q_i, k_i, v_i, o_i, x2_i, fac_i, dw_i, outp_i, outc_i = refs[:17]
    layer_o, input_o = refs[17:19]
    refs = refs[19:]
    if comm:
        gqkv, gout, gfc1, gfc2, gvec, gfc = refs[:6]
        refs = refs[6:]
    else:
        sums_o, vs_o, fcs_o = refs[:3]
        refs = refs[3:]
    (
        sums, r1, r2, rz, rzz, r3, x2, drecv, dx, stage, delta, vs, fcs, vsum, v1, vz, v3, vpart,
        hT, dh2, fac, du, o, w, free,
        lsem, osem, tsem, s1, s2, sz, s3, ss, t1, tz, t3, tt,
    ) = refs
    pc = Place(comm)
    c = pc.c
    pc.greet()
    big = Scatter(pc, sums, BACKWARD_ROUTES, r1, r2, rz, rzz, r3, s1, s2, sz, s3, ss)

    def done(p, value):
        if p < 4:
            gfc2[:, p * COLS : (p + 1) * COLS] = value
        elif p < 8:
            gfc1[:, (p - 4) * COLS : (p - 3) * COLS] = value
        elif p == 8:
            gout[...] = value
        else:
            for i, (which, pair) in enumerate(LATE[p - 9]):
                gqkv[which, :, pair * 128 : (pair + 1) * 128] = value[:, i * 128 : (i + 1) * 128]

    def at(name):
        if not comm:
            return
        for code in BACKWARD_PLAN.get(name, ()):
            p, what = code // 10, code % 10
            if what == 4:
                big.across(p)
            elif what == 5:
                big.close(p, done)
            else:
                big.step(p, what, done)

    def opened(p):
        if comm:
            big.open(p)

    def fetch(src, dst, i):
        cp = pltpu.make_async_copy(src, dst, lsem.at[i])
        cp.start()
        return cp

    def weight(slot):
        return w[slot].reshape(D, COLS)

    grads = fetch(dw_i, sums.at[pl.ds(0, 4)], 0)
    gcopy = fetch(g_i, dx, 1)
    fcopy = [fetch(fac_i.at[j], fac.at[j], 2 + j) for j in range(2)]
    wcopy = [fetch(wall.at[8], w.at[0], 4), fetch(wall.at[4], w.at[1], 5), fetch(wall.at[9], w.at[2], 6), fetch(wall.at[5], w.at[3], 7)]
    ocopies = []
    for i in range(2):
        cp = tensor_copy(pc, outp_i.at[:, row_tile(i)], drecv.at[:, row_tile(i)], tsem.at[0, i], tsem.at[1, i])
        cp.start()
        ocopies.append(cp)
    x2copy = fetch(x2_i, x2, 8)
    ocopy = fetch(outc_i, o, 9)
    hcopy = fetch(h2t_i, hT, 10)
    vs[...] = jnp.zeros_like(vs)

    def weight_grad(p, right):
        def body(i):
            rows = pl.ds(pl.multiple_of(i * 256, 256), 256)
            sums[p, i] = matmul(hT[rows, :], right().reshape(ROWS, COLS)).astype(bf16).reshape(2, 2, 64, COLS)

        loop(4, body)
        opened(p)

    grads.wait()
    for p in range(4):
        opened(p)
    gcopy.wait()
    sent = []
    for j in range(4):
        fcopy[j % 2].wait()
        wcopy[2 * (j % 2)].wait()
        wcopy[2 * (j % 2) + 1].wait()

        def tile(n, inner=True):
            if inner:
                for m in range(4):
                    pl.when(n == m)(lambda: at(f"tile{4 * j + m}"))
            i = (n % 2) * 2 + jnp.where(n < 2, 1 - c, c)
            rows = row_tile(i)
            da = matmul(dx[rows], weight(2 * (j % 2)))
            du[j, rows] = (da * fac[j % 2, rows].astype(f32)).astype(bf16)
            part = matmul_nt(du[j, rows], weight(2 * (j % 2) + 1))
            if j == 0:
                dh2[rows] = part
            else:
                dh2[rows] += part

        if j < 3:
            loop(4, tile)
        else:
            lax.fori_loop(0, 2, lambda n, z: (tile(n), z)[1], 0)
            pl.semaphore_wait(free, 1)
            for i in range(2):
                for half in range(2):
                    cols = slice(half * COLS, (half + 1) * COLS)
                    o[half, row_tile(i)] = dh2[row_tile(2 * i + 1 - c), cols].astype(bf16)
                cp = tensor_copy(pc, o.at[:, row_tile(i)], drecv.at[:, row_tile(i)], tsem.at[2, i], tsem.at[3, i])
                cp.start()
                sent.append(cp)
            lax.fori_loop(2, 4, lambda n, z: (tile(n), z)[1], 0)
        fcs[:, j * COLS : (j + 1) * COLS] = column_sums(du.at[j])
        if j < 2:
            fcopy[j] = fetch(fac_i.at[j + 2], fac.at[j], 2 + j)
            wcopy[2 * j] = fetch(wall.at[10 + j], w.at[2 * j], 4 + 2 * j)
            wcopy[2 * j + 1] = fetch(wall.at[6 + j], w.at[2 * j + 1], 5 + 2 * j)
        elif j == 2:
            wcopy[0] = fetch(wall.at[0], w.at[0], 4)
            wcopy[1] = fetch(wall.at[1], w.at[1], 5)
        else:
            wcopy[2] = fetch(wall.at[2], w.at[2], 6)
            wcopy[3] = fetch(wall.at[3], w.at[3], 7)
        if j == 0:
            at("layer")
            x2copy.wait()
            ocopy.wait()
            for i in range(2):
                ocopies[i].wait()
                for half in range(2):
                    cols = slice(half * COLS, (half + 1) * COLS)
                    total = (
                        x2[row_tile(i), cols]
                        + o[half, row_tile(i)].astype(f32)
                        + drecv[half, row_tile(i)].astype(f32)
                    )
                    stage[i, :, cols] = total[0:HALF].astype(bf16)
            lcopy = pltpu.make_async_copy(stage, layer_o, osem.at[0])
            lcopy.start()
            pl.semaphore_signal(free, inc=1, device_id=pc.dev("c"), device_id_type=MESH)

    def received(i):
        return jnp.concatenate([drecv[0, row_tile(i)], drecv[1, row_tile(i)]], axis=1).astype(f32)

    at("grad4")
    hcopy.wait()
    weight_grad(4, lambda: du[0])
    copies = []
    for i in range(2):
        at(f"mid{i}")
        sent[i].wait()
        own = row_tile(2 * i + c)
        up = dh2[own] + received(i)
        normed, inverse = normalize(x2[row_tile(i)])
        grad = dx[own].astype(f32)
        total = grad + norm_backward(up, normed, inverse, vec[1:2])
        low = total.astype(bf16)
        x2[row_tile(i)] = total
        dx[own] = low
        cp = tensor_copy(pc, dx.at[own], dx.at[own], tsem.at[4, i], tsem.at[5, i])
        cp.start()
        copies.append(cp)
        vs[5:6] += jnp.sum(up * normed, axis=0, keepdims=True)
        vs[6:7] += jnp.sum(up, axis=0, keepdims=True)
        vs[4:5] += jnp.sum(low.astype(f32), axis=0, keepdims=True)
        vs[7:8] += jnp.sum(grad, axis=0, keepdims=True)
    lcopy.wait()
    xcopy = fetch(x_ref, stage, 8)
    ocopy = fetch(o_i, o, 9)
    for j in range(1, 4):
        at(f"grad{4 + j}")
        weight_grad(4 + j, lambda: du[j])
        if j == 1:
            qcopy = fetch(q_i, du.at[0], 2)
            kcopy = fetch(k_i, du.at[1], 3)
        elif j == 2:
            vcopy = fetch(v_i, du.at[2], 10)
    q, k, v, do = (du.at[i] for i in range(4))
    at("turn")
    for cp in copies:
        cp.wait()

    def turn(i):
        cols = pl.ds(pl.multiple_of(i * 128, 128), 128)
        hT[cols, :] = dx[:, cols].T

    loop(D // 128, turn)
    ocopy.wait()
    weight_grad(8, lambda: o[...])
    hcopy = fetch(h1t_i, hT, 0)
    at("out")
    wcopy[3].wait()

    def out_back(i):
        do[row_tile(i)] = matmul(dx[row_tile(i)], weight(3)).astype(bf16)

    loop(4, out_back)
    at("delta")
    pick = lax.broadcasted_iota(jnp.int32, (8, COLS), 0) == lax.broadcasted_iota(jnp.int32, (8, COLS), 1) // HEAD_DIM
    pick = pick.astype(f32).astype(bf16)
    mcol = dh2.at[:, pl.ds(0, 128)]
    for i in range(2):
        rows = pl.ds(i * SEQ, SEQ)
        prod = do[rows].astype(f32) * o[i].astype(f32)
        high = prod.astype(bf16)
        low = (prod - high.astype(f32)).astype(bf16)
        part = matmul_nt(pick, high) + matmul_nt(pick, low)
        for h in range(8):
            delta[i, h] = part[h : h + 1]
        mcol[rows] = jnp.broadcast_to(mask[i, 0:1], (128, SEQ)).T
    for cp in (qcopy, kcopy, vcopy):
        cp.wait()
    lane = lax.broadcasted_iota(jnp.int32, (1, 128), 1)

    def late_grad(i):
        def right():
            blocks = [(q, k, v)[which][:, pair * 128 : (pair + 1) * 128] for which, pair in LATE[i]]
            return jnp.concatenate(blocks, axis=1)

        weight_grad(9 + i, right)

    def attend(n):
        img, head = n // 2 % 2, 2 * (n // 4) + n % 2

        @pl.when(n == 8)
        def _():
            hcopy.wait()
            at("grad9")
            late_grad(0)

        @pl.when(n == 12)
        def _():
            at("grad10")
            late_grad(1)

        for j in range(16):
            pl.when(n == j)(lambda: at(f"attend{j}"))
        rows = pl.ds(pl.multiple_of(img * SEQ, 16), SEQ)
        cols = pl.ds(pl.multiple_of(head // 2 * 128, 128), 128)
        first = 64 * (head % 2)
        mine = (lane >= first) & (lane < first + 64)
        qb, gb = q[rows, cols], do[rows, cols]
        qm = jnp.where(mine, qb, jnp.zeros_like(qb))
        gm = jnp.where(mine, gb, jnp.zeros_like(gb))
        dq = None
        for t in range(2):
            part = pl.ds(pl.multiple_of(img * SEQ + t * PAD, 16), PAD)
            kb, vb = k[part, cols], v[part, cols]
            p = jnp.exp(matmul_nt(kb, qm) + mcol[part, 0:1] - lse[img, head])
            dp = matmul_nt(vb, gm)
            ds = (p * (dp - delta[img, head])).astype(bf16)
            dv = matmul(p.astype(bf16), gm)
            dk = matmul(ds, qm)
            dqt = matmul_tn(ds, kb)
            dq = dqt if dq is None else dq + dqt
            k[part, cols] = jnp.where(mine, dk.astype(bf16), kb)
            v[part, cols] = jnp.where(mine, dv.astype(bf16), vb)
        q[rows, cols] = jnp.where(mine, (dq * (HEAD_DIM**-0.5)).astype(bf16), qb)

    loop(16, attend)
    at("grad11")
    late_grad(2)
    for i in range(3):
        wcopy[i].wait()

    def back(t):
        rows = row_tile(t)
        total = matmul_nt(q[rows], weight(0))
        total += matmul_nt(k[rows], weight(1))
        total += matmul_nt(v[rows], weight(2))
        return total

    sent = []
    for i in range(2):
        at(f"back{i}")
        part = back(2 * i + 1 - c).astype(bf16)
        for half in range(2):
            o[half, row_tile(i)] = part[:, half * COLS : (half + 1) * COLS]
        cp = tensor_copy(pc, o.at[:, row_tile(i)], drecv.at[:, row_tile(i)], tsem.at[6, i], tsem.at[7, i])
        cp.start()
        sent.append(cp)
    xcopy.wait()
    here = pl.ds(pl.multiple_of(c * COLS, COLS), COLS)
    vs[2:3, here] = column_sums(q)
    vs[3:4, here] = column_sums(v)
    for i in range(2):
        at(f"back{2 + i}")
        up = back(2 * i + c)
        sent[i].wait()
        up = (up + received(i))[0:HALF]
        normed, inverse = normalize(stage[i].astype(f32))
        total = x2[row_tile(i)][0:HALF] + norm_backward(up, normed, inverse, vec[0:1])
        stage[i] = total.astype(bf16)
        vs[0:1] += jnp.sum(up * normed, axis=0, keepdims=True)
        vs[1:2] += jnp.sum(up, axis=0, keepdims=True)
    icopy = pltpu.make_async_copy(stage, input_o, osem.at[1])
    icopy.start()
    if comm:
        at("vectors")
        vsum[...] = jnp.zeros_like(vsum)
        for r in range(GROUP):
            vsum[0, r // 4, (r // 2) % 2, r % 2, 0:8, 0:64] = vs[:, r * 64 : (r + 1) * 64]
        for r in range(GROUP // 2):
            for half in range(2):
                row = fcs[:, (2 * r + half) * 128 : (2 * r + half + 1) * 128]
                for side in range(2):
                    to = r + side * (GROUP // 2)
                    value = jnp.where(c == side, row, jnp.zeros_like(row))
                    vsum[0, to // 4, (to // 2) % 2, to % 2, 8 + half : 9 + half, :] = value
        small = Scatter(pc, vsum, [("P", "x", "y")], v1, None, vz, None, v3, t1, None, tz, t3, tt)
        small.open(0)
        for dist in (3, 2, 1, 0):
            at(f"small{dist}")
            small.step(0, dist, None)

        def keep(p, value):
            vpart[0] = value

        at("small_end")
        small.close(0, keep)
        cp = tensor_copy(pc, vpart.at[0], vpart.at[1], tsem.at[8, 0], tsem.at[9, 0])
        cp.start()
        at("end")
        cp.wait()
        total = vpart[0] + vpart[1]
        gvec[...] = jnp.where(c == 0, total[0:8, 0:32], total[0:8, 32:64])
        gfc[...] = jnp.where(c == 0, total[8:9], total[9:10])
        small.finish()
        big.finish()
    else:
        pairs = ((sums, sums_o), (vs, vs_o), (fcs, fcs_o))
        copies = [pltpu.make_async_copy(a, b, osem.at[2 + i]) for i, (a, b) in enumerate(pairs)]
        for cp in copies:
            cp.start()
        for cp in copies:
            cp.wait()
    icopy.wait()


def backward_call(comm, args):
    B = lambda *s: pltpu.VMEM(s, bf16)
    F = lambda *s: pltpu.VMEM(s, f32)
    S = lambda *s: pltpu.SemaphoreType.DMA(s)
    A = pl.BlockSpec(memory_space=pl.ANY)
    V = pl.BlockSpec(memory_space=pltpu.VMEM)
    sh = jax.ShapeDtypeStruct
    outs = [sh((2, HALF, D), bf16), sh((2, HALF, D), bf16)]
    ospecs = [A, A]
    if comm:
        outs += [
            sh((3, 64, COLS), f32), sh((64, COLS), f32), sh((64, 4 * COLS), f32), sh((64, 4 * COLS), f32),
            sh((8, 32), f32), sh((1, 128), f32),
        ]
        ospecs += [V] * 6
    else:
        outs += [sh((PIECES, 4, 2, 2, 64, COLS), bf16), sh((8, D), f32), sh((1, 4 * COLS), f32)]
        ospecs += [A] * 3
    ispecs = [A, V, V, V] + [A] * 13
    one = (4, 2, 2, 64, COLS)
    scratch = [
        B(PIECES, *one), B(PIECES, 4, 2, 64, COLS), B(4, 4, 64, COLS), B(8, 5, 2, 64, COLS), B(4, 5, 64, COLS),
        B(8, 64, COLS),
        F(2 * PAD, D), B(2, SEQ, COLS), B(ROWS, D), B(2, HALF, D), F(2, 8, 1, SEQ), F(8, D), F(1, 4 * COLS),
        F(1, 4, 2, 2, 16, 128), F(1, 4, 2, 16, 128), F(1, 5, 2, 16, 128), F(1, 16, 128), F(2, 16, 128),
        B(D, ROWS), F(ROWS, D), B(2, ROWS, COLS), B(4, ROWS, COLS), B(2, SEQ, COLS), B(4, *one),
        pltpu.SemaphoreType.REGULAR, S(11), S(5), S(10, 2), S(PIECES, 4), S(4, 4), S(PIECES, 5), S(PIECES), S(4), S(1, 4), S(1, 5), S(1), S(4),
    ]
    return pl.pallas_call(
        functools.partial(backward_kernel, comm),
        out_shape=outs,
        in_specs=ispecs,
        out_specs=ospecs,
        scratch_shapes=scratch,
        name="backward",
        compiler_params=pltpu.CompilerParams(
            collective_id=1, has_side_effects=True, vmem_limit_bytes=63 * 2**20
        ),
    )(*args)


def split_cols(m):
    return jnp.transpose(m.reshape(m.shape[0], m.shape[1] // COLS, COLS), (1, 0, 2))


def shards(layer_in, out_grad, key_valid, image_live, w_qkv, w_out, w_fc1, w_fc2, norm_gains, bias_rows, fc_bias):
    comm = lax.axis_size("dp") == GROUP
    valid = jnp.pad(key_valid.reshape(2, 2, HALF), ((0, 0), (0, 0), (0, PAD - HALF))).reshape(2, 1, SEQ)
    mask = jnp.broadcast_to(jnp.where(valid > 0, 0.0, -1e9).astype(f32), (2, 8, SEQ))
    rows = jnp.concatenate([norm_gains, bias_rows], axis=0)
    if comm:
        low = jnp.pad(rows, ((0, 8), (0, 64)))
        small = lax.dynamic_update_slice(low, fc_bias.reshape(2, 128), (8, 0))
        made = forward_call(True, (layer_in, out_grad, image_live, mask, w_qkv, w_out.T, w_fc1, w_fc2.T, small))
        wall, made = made[0], made[1:]
    else:
        local = jnp.concatenate([w_qkv, w_out.T[None], split_cols(w_fc1), split_cols(w_fc2.T)], axis=0)
        wall = lax.all_gather(local, "dp", axis=1, tiled=True).reshape(PIECES, 4, 2, 2, 64, COLS)
        rows = lax.all_gather(rows, "dp", axis=1, tiled=True)
        hidden = lax.all_gather(fc_bias, "dp", axis=0, tiled=True)
        small = jnp.pad(jnp.transpose(rows.reshape(8, GROUP, 64), (1, 0, 2)), ((0, 0), (0, 8), (0, 64)))
        small = lax.dynamic_update_slice(small, hidden.reshape(GROUP, 2, 128), (0, 8, 0))
        made = forward_call(False, (layer_in, out_grad, image_live, mask, wall, small))
    h1t, h2t, g, q, k, v, o, lse, x2, fac, dw, outp, outc, vec = made
    o, outp, outc = (m.reshape(2, SEQ, COLS) for m in (o, outp, outc))
    back = backward_call(
        comm, (layer_in, mask, vec, lse, wall, h1t, h2t, g, q, k, v, o, x2, fac, dw, outp, outc)
    )
    layer_out, input_grad = back[:2]
    if comm:
        gqkv, gout, gfc1, gfc2, gvec, gfc = back[2:]
        return (layer_out, input_grad, gqkv, gout.T, gfc1, gfc2.T, gvec, gfc.reshape(128))
    sums, vs, fcs = back[2:]
    mine = lax.psum_scatter(sums.reshape(PIECES, D, COLS), "dp", scatter_dimension=1, tiled=True).astype(f32)
    down = jnp.transpose(mine[0:4], (0, 2, 1)).reshape(4 * COLS, -1)
    up = jnp.transpose(mine[4:8], (1, 0, 2)).reshape(-1, 4 * COLS)
    vector = lax.psum_scatter(vs, ("dp", "tensor"), scatter_dimension=1, tiled=True)
    whole = lax.dynamic_update_slice(jnp.zeros((FF,), f32), fcs[0], (lax.axis_index("tensor") * 4 * COLS,))
    hidden = lax.psum_scatter(whole, ("dp", "tensor"), scatter_dimension=0, tiled=True)
    blocks = {
        key: mine[9 + i][:, j * 128 : (j + 1) * 128] for i, keys in enumerate(LATE) for j, key in enumerate(keys)
    }
    qkv = jnp.stack([jnp.concatenate([blocks[(which, pair)] for pair in range(4)], axis=1) for which in range(3)])
    return (layer_out, input_grad, qkv, mine[8].T, up, down, vector, hidden)


def solution(mesh):
    return jax.shard_map(
        shards,
        mesh=mesh,
        in_specs=(
            P("dp", "tensor", None),
            P("dp", "tensor", None),
            P("dp", None),
            P("dp"),
            P(None, "dp", "tensor"),
            P("tensor", "dp"),
            P("dp", "tensor"),
            P("tensor", "dp"),
            P(None, "dp"),
            P(None, "dp"),
            P("dp"),
        ),
        out_specs=(
            P("dp", "tensor", None),
            P("dp", "tensor", None),
            P(None, "dp", "tensor"),
            P("tensor", "dp"),
            P("dp", "tensor"),
            P("tensor", "dp"),
            P(None, ("dp", "tensor")),
            P(("dp", "tensor")),
        ),
        check_vma=False,
    )
```

```python
import functools

import jax
import jax.numpy as jnp
from jax import lax
from jax.experimental import pallas as pl
from jax.experimental.pallas import tpu as pltpu
from jax.sharding import PartitionSpec as P

D = 1024
HEAD_DIM = 64
FF = 4096
EPSILON = 1e-05
MESH = pl.DeviceIdType.MESH
bf16 = jnp.bfloat16
f32 = jnp.float32

PIECES = 12
COLS = 512
HALF = 292
PAD = 304
SEQ = 2 * PAD
ROWS = 4 * PAD
GROUP = 16


def matmul(a, b):
    return lax.dot_general(a, b, (((1,), (0,)), ((), ())), preferred_element_type=f32)


def matmul_nt(a, b):
    return lax.dot_general(a, b, (((1,), (1,)), ((), ())), preferred_element_type=f32)


def matmul_tn(a, b):
    return lax.dot_general(a, b, (((0,), (0,)), ((), ())), preferred_element_type=f32)


def column_sums(ref):
    return matmul(jnp.ones((8, ref.shape[0]), bf16), ref[...])[0:1]


def normalize(values):
    centred = values - jnp.mean(values, axis=-1, keepdims=True)
    inverse = lax.rsqrt(jnp.mean(centred * centred, axis=-1, keepdims=True) + EPSILON)
    return centred * inverse, inverse


def norm_backward(upstream, normed, inverse, gain_row):
    scaled = upstream * gain_row
    return inverse * (
        scaled
        - jnp.mean(scaled, axis=-1, keepdims=True)
        - normed * jnp.mean(scaled * normed, axis=-1, keepdims=True)
    )


class Place:
    def __init__(self, comm):
        self.comm = comm
        self.dp = lax.axis_index("dp")
        self.c = lax.axis_index("tensor")
        self.z = self.dp // 4
        self.y = (self.dp // 2) % 2
        self.x = self.dp % 2

    def dev(self, d):
        if d == "x":
            t = self.dp + 1 - 2 * self.x
        elif d == "y":
            t = self.dp + 2 - 4 * self.y
        elif d == "u":
            t = self.dp + 4
        elif d == "d":
            t = self.dp - 4
        else:
            return (self.dp, 1 - self.c)
        return (t, self.c)

    def greet(self):
        bar = pltpu.get_barrier_semaphore()

        def hail(d):
            pl.semaphore_signal(bar, inc=1, device_id=self.dev(d), device_id_type=MESH)

        hail("c")
        if not self.comm:
            pl.semaphore_wait(bar, 1)
            return
        hail("x")
        hail("y")
        pl.when(self.z < 3)(lambda: hail("u"))
        pl.when(self.z > 0)(lambda: hail("d"))
        pl.when((self.z == 0) | (self.z == 3))(lambda: pl.semaphore_wait(bar, 4))
        pl.when((self.z > 0) & (self.z < 3))(lambda: pl.semaphore_wait(bar, 5))


def wait_bytes(ref, sem):
    pltpu.make_async_copy(ref, ref, sem).wait()


class Gather:
    def __init__(self, pc, wall, routes, zs, fs, ts, ss):
        self.pc, self.wall, self.routes = pc, wall, routes
        self.zs, self.fs, self.ts, self.ss = zs, fs, ts, ss

    def copy(self, ref, d, rsem):
        return pltpu.make_async_remote_copy(
            src_ref=ref,
            dst_ref=ref,
            send_sem=self.ss.at["xyud".index(d)],
            recv_sem=rsem,
            device_id=self.pc.dev(d),
            device_id_type=MESH,
        )

    def block(self, p, zz):
        return self.wall.at[p, zz, self.pc.y, self.pc.x]

    def pair(self, p, zz, d1):
        if d1 == "x":
            return self.wall.at[p, zz, self.pc.y]
        return self.wall.at[p, zz, :, self.pc.x]

    def beside(self, p, zz, d):
        if d == "x":
            return self.wall.at[p, zz, self.pc.y, 1 - self.pc.x]
        return self.wall.at[p, zz, 1 - self.pc.y, self.pc.x]

    def part(self, p, zz):
        kind, d1, _ = self.routes[p]
        return self.block(p, zz) if kind == "Z" else self.pair(p, zz, d1)

    def pass_on(self, p, zz, way):
        cond = self.pc.z < 3 if way == "u" else self.pc.z > 0
        pl.when(cond)(lambda: self.copy(self.part(p, zz), way, self.zs.at[p, zz]).start())

    def to_second(self, p, zz):
        _, d1, d2 = self.routes[p]
        self.copy(self.pair(p, zz, d1), d2, self.ts.at[p]).start()

    def open(self, p):
        kind, d1, d2 = self.routes[p]
        z = self.pc.z
        if kind == "Z":
            self.pass_on(p, z, "u")
            self.pass_on(p, z, "d")
            self.copy(self.block(p, z), d1, self.fs.at[p, z]).start()
        else:
            self.copy(self.block(p, z), d1, self.fs.at[p, 0]).start()

    def first(self, p, zz):
        _, d1, _ = self.routes[p]
        sem = self.fs.at[p, zz] if self.routes[p][0] == "Z" else self.fs.at[p, 0]
        wait_bytes(self.beside(p, zz, d1), sem)

    def step(self, p, dist):
        kind, d1, d2 = self.routes[p]
        z = self.pc.z

        def along(src, way):
            wait_bytes(self.part(p, src), self.zs.at[p, src])
            self.pass_on(p, src, way)
            if kind == "Z":
                self.copy(self.block(p, src), d1, self.fs.at[p, src]).start()
            else:
                self.to_second(p, src)

        def arrived(src):
            self.first(p, src)
            self.to_second(p, src)

        if kind == "P" and dist == 0:
            self.first(p, z)
            self.pass_on(p, z, "u")
            self.pass_on(p, z, "d")
            self.to_second(p, z)
            return
        if 1 <= dist <= 3:
            pl.when(z - dist >= 0)(lambda: along(z - dist, "u"))
            pl.when(z + dist <= 3)(lambda: along(z + dist, "d"))
        if kind == "Z":
            if dist == 1:
                arrived(z)
            elif dist > 1:
                pl.when(z - dist + 1 >= 0)(lambda: arrived(z - dist + 1))
                pl.when(z + dist - 1 <= 3)(lambda: arrived(z + dist - 1))

    def close(self, p):
        d2 = self.routes[p][2]
        if d2 == "y":
            wait_bytes(self.wall.at[p, :, 1 - self.pc.y], self.ts.at[p])
        else:
            wait_bytes(self.wall.at[p, :, :, 1 - self.pc.x], self.ts.at[p])

    def drain(self, n, sem):
        while n >= 16:
            wait_bytes(self.wall.at[0], sem)
            n -= 16
        while n >= 4:
            wait_bytes(self.wall.at[0, 0], sem)
            n -= 4
        while n:
            wait_bytes(self.wall.at[0, 0, 0, 0], sem)
            n -= 1

    def finish(self):
        sent = {"x": 0, "y": 0, "z": 0}
        for kind, d1, d2 in self.routes:
            sent[d1] += 4 if kind == "Z" else 1
            sent[d2] += 8
            sent["z"] += 1 if kind == "Z" else 2
        self.drain(sent["x"], self.ss.at[0])
        self.drain(sent["y"], self.ss.at[1])
        for k in range(3):
            pl.when(self.pc.z == k)(lambda: self.drain(sent["z"] * (k + 1), self.ss.at[2]))
            pl.when(self.pc.z == k + 1)(lambda: self.drain(sent["z"] * (3 - k), self.ss.at[3]))


class Scatter:
    def __init__(self, pc, sums, routes, first, second, line, single, last, s1, s2, sz, s3, ss):
        self.pc, self.sums, self.routes = pc, sums, routes
        self.r1, self.r2, self.rz, self.rzz, self.r3 = first, second, line, single, last
        self.s1, self.s2, self.sz, self.s3, self.ss = s1, s2, sz, s3, ss
        self.rank = [sum(r[0] == "Z" for r in routes[:p]) for p in range(len(routes))]

    def copy(self, src, dst, d, rsem):
        return pltpu.make_async_remote_copy(
            src_ref=src,
            dst_ref=dst,
            send_sem=self.ss.at["xyud".index(d)],
            recv_sem=rsem,
            device_id=self.pc.dev(d),
            device_id_type=MESH,
        )

    def pair(self, p, t, d, other):
        pc = self.pc
        if d == "y":
            return self.sums.at[p, t, (1 - pc.y) if other else pc.y]
        return self.sums.at[p, t, :, (1 - pc.x) if other else pc.x]

    def one(self, p, t, flip=None):
        pc = self.pc
        return self.sums.at[p, t, (1 - pc.y) if flip == "y" else pc.y, (1 - pc.x) if flip == "x" else pc.x]

    def each(self, dist, fn):
        z = self.pc.z
        if dist == 0:
            fn(z, None)
            return
        pl.when(z + dist <= 3)(lambda: fn(z + dist, "u"))
        pl.when(z - dist >= 0)(lambda: fn(z - dist, "d"))

    def add(self, dst, *others):
        total = dst[...]
        for o in others:
            total = total + o[...]
        dst[...] = total

    def open(self, p):
        d2 = self.routes[p][2]
        for dist in (3, 2, 1, 0):
            self.each(
                dist,
                lambda t, _: self.copy(self.pair(p, t, d2, True), self.r1.at[p, t], d2, self.s1.at[p, t]).start(),
            )

    def across(self, p):
        _, d1, d2 = self.routes[p]

        def go(t, _):
            wait_bytes(self.r1.at[p, t], self.s1.at[p, t])
            self.add(self.pair(p, t, d2, False), self.r1.at[p, t])
            self.copy(self.one(p, t, d1), self.r2.at[self.rank[p], t], d1, self.s2.at[self.rank[p], t]).start()

        for dist in (3, 2, 1, 0):
            self.each(dist, go)

    def step(self, p, dist, done):
        kind, d1, d2 = self.routes[p]
        z = self.pc.z
        if kind == "Z":
            view = lambda t: self.one(p, t)
            slot = lambda i: self.rzz.at[self.rank[p], i]
        else:
            view = lambda t: self.pair(p, t, d2, False)
            slot = lambda i: self.rz.at[p - self.rank[p], i]

        def go(t, way):
            if kind == "Z":
                wait_bytes(self.r2.at[self.rank[p], t], self.s2.at[self.rank[p], t])
                mine = self.r2.at[self.rank[p], t]
            else:
                wait_bytes(self.r1.at[p, t], self.s1.at[p, t])
                mine = self.r1.at[p, t]

            def arrival(i):
                wait_bytes(slot(i), self.sz.at[p, i])
                return slot(i)

            if way == "u":
                pl.when(z > 0)(lambda: self.add(view(t), mine, arrival(t + 1)))
                pl.when(z == 0)(lambda: self.add(view(t), mine))
                self.copy(view(t), slot(t + 1), "u", self.sz.at[p, t + 1]).start()
            elif way == "d":
                pl.when(z < 3)(lambda: self.add(view(t), mine, arrival(t)))
                pl.when(z == 3)(lambda: self.add(view(t), mine))
                self.copy(view(t), slot(t), "d", self.sz.at[p, t]).start()
            else:
                pl.when(z == 0)(lambda: self.add(view(z), mine, arrival(z)))
                pl.when(z == 3)(lambda: self.add(view(z), mine, arrival(z + 1)))
                pl.when((z > 0) & (z < 3))(lambda: self.add(view(z), mine, arrival(z), arrival(z + 1)))
                if kind == "Z":
                    done(p, self.one(p, z)[...].astype(f32))
                else:
                    self.copy(self.one(p, z, d1), self.r3.at[p - self.rank[p]], d1, self.s3.at[p]).start()

        self.each(dist, go)

    def close(self, p, done):
        if self.routes[p][0] == "P":
            wait_bytes(self.r3.at[p - self.rank[p]], self.s3.at[p])
            done(p, self.one(p, self.pc.z)[...].astype(f32) + self.r3[p - self.rank[p]].astype(f32))

    def drain(self, n, sem):
        while n >= 16:
            wait_bytes(self.sums.at[0], sem)
            n -= 16
        while n >= 4:
            wait_bytes(self.sums.at[0, 0], sem)
            n -= 4
        while n:
            wait_bytes(self.sums.at[0, 0, 0, 0], sem)
            n -= 1

    def finish(self):
        sent = {"x": 0, "y": 0, "z": 0}
        for kind, d1, d2 in self.routes:
            sent[d1] += 4 if kind == "Z" else 1
            sent[d2] += 8
            sent["z"] += 1 if kind == "Z" else 2
        self.drain(sent["x"], self.ss.at[0])
        self.drain(sent["y"], self.ss.at[1])
        for k in range(3):
            pl.when(self.pc.z == k)(lambda: self.drain(sent["z"] * (3 - k), self.ss.at[2]))
            pl.when(self.pc.z == k + 1)(lambda: self.drain(sent["z"] * (k + 1), self.ss.at[3]))


def row_tile(i):
    return pl.ds(pl.multiple_of(i * PAD, 16), PAD)


def loop(count, body):
    def run(i, carry):
        body(i)
        return carry

    lax.fori_loop(0, count, run, 0)


def tensor_copy(pc, src, dst, send, recv):
    return pltpu.make_async_remote_copy(
        src_ref=src, dst_ref=dst, send_sem=send, recv_sem=recv, device_id=pc.dev("c"), device_id_type=MESH
    )


LATE = (
    ((0, 0), (0, 1), (1, 0), (1, 1)),
    ((2, 0), (2, 1), (2, 2), (0, 2)),
    ((1, 2), (0, 3), (1, 3), (2, 3)),
)

FORWARD_ROUTES = (
    ("Z", "y", "x"),
    ("P", "x", "y"),
    ("P", "y", "x"),
    ("Z", "y", "x"),
    ("Z", "x", "y"),
    ("P", "x", "y"),
    ("P", "y", "x"),
    ("P", "x", "y"),
    ("Z", "x", "y"),
    ("P", "y", "x"),
    ("P", "x", "y"),
    ("P", "y", "x"),
)
FORWARD_PLAN = {
    "small1": (20,),
    "small3": (1,),
    "small4": (10,),
    "norm1": (21, 2, 41, 11,),
    "turn_g": (3, 22, 31, 12, 4, 50, 23, 32,),
    "turn_h1": (60, 13, 100, 70, 42, 51,),
    "attend0": (33,),
    "attend2": (90,),
    "attend3": (81, 34, 52,),
    "attend5": (43,),
    "attend6": (71,),
    "need3": (44, 53, 61,),
    "own3": (72,),
    "mid0": (62,),
    "mid1": (110,),
    "need4": (63,),
    "half0": (82, 73, 91,),
    "half2": (83, 101,),
    "need7": (92,),
    "grad1": (84, 111, 93,),
    "grad2": (102,),
    "need8": (112, 103,),
    "need9": (113,),
}
BACKWARD_ROUTES = (
    ("P", "x", "y"),
    ("P", "x", "y"),
    ("P", "y", "x"),
    ("Z", "y", "x"),
    ("P", "x", "y"),
    ("P", "y", "x"),
    ("Z", "y", "x"),
    ("Z", "x", "y"),
    ("P", "y", "x"),
    ("P", "x", "y"),
    ("P", "y", "x"),
    ("Z", "x", "y"),
)
BACKWARD_PLAN = {
    "layer": (3,),
    "tile7": (23, 2,),
    "tile12": (22,),
    "tile15": (13, 1,),
    "mid1": (21,),
    "grad5": (12,),
    "grad7": (43, 34,),
    "turn": (53,),
    "out": (42,),
    "attend0": (52, 33,),
    "attend1": (11,),
    "attend3": (51,),
    "attend6": (32,),
    "attend7": (41,),
    "attend8": (83, 31,),
    "attend11": (93, 64, 82, 40,),
    "attend12": (20, 92,),
    "attend13": (0,),
    "attend14": (103, 63,),
    "grad11": (81,),
    "back0": (10, 91, 74, 102, 30,),
    "back3": (62,),
    "vectors": (73,),
    "small3": (90, 101,),
    "small2": (114, 72,),
    "small1": (50, 113, 61, 5,),
    "small0": (15, 25, 80, 112, 100, 71,),
    "small_end": (95, 45, 111, 55,),
    "end": (70, 105, 85, 60, 110,),
    "start": (6, 26,),
    "tile3": (16, 36,),
}


def forward_kernel(comm, *refs):
    if comm:
        x_ref, go_ref, live, kept, wq, wo, w1, w2, gains, shifts, hidden = refs[:11]
        wall_o = refs[11]
        refs = refs[12:]
    else:
        x_ref, go_ref, live, kept, wall_i, smalls_in = refs[:6]
        refs = refs[6:]
    (
        h1t_o, h2t_o, g_o, q_o, k_o, v_o, o_o, lse_o, x2_o, fac_o, dw_o, outp_o, outc_o, vec, mask,
        wall, smalls, pack, hb, xp, h1, g, gT, hT, q, k, v, o, lse, x2, proj, precv, act, fac, dw, acc,
        lsem, osem, tsem, zs, fs, ts, ss, vzs, vfs, vts, vss,
    ) = refs
    pc = Place(comm)
    c = pc.c
    pc.greet()
    big = Gather(pc, wall, FORWARD_ROUTES, zs, fs, ts, ss)
    outs = {}

    def emit(src, dst, i):
        outs[i] = pltpu.make_async_copy(src, dst, osem.at[i])
        outs[i].start()

    def at(name):
        if comm:
            for code in FORWARD_PLAN.get(name, ()):
                big.step(code // 10, code % 10)

    def need(p):
        if comm:
            big.close(p)
            emit(wall.at[p], wall_o.at[p], 20 + p)

    def weight(p):
        return wall[p].reshape(D, COLS)

    if comm:
        pack[...] = jnp.zeros_like(pack)
        pack[0:2, 0:64] = gains[...].astype(f32)
        pack[2:8, 0:64] = shifts[...].astype(f32)
        pack[8:10] = hidden[...].astype(f32)
        smalls[0, pc.z, pc.y, pc.x] = pack[...].astype(bf16)
        small = Gather(pc, smalls, [("P", "x", "y")], vzs, vfs, vts, vss)
        small.open(0)
        for i in range(3):
            wall[i, pc.z, pc.y, pc.x] = wq[i]
        wall[3, pc.z, pc.y, pc.x] = wo[...]
        for i in range(4):
            wall[4 + i, pc.z, pc.y, pc.x] = w1[:, i * COLS : (i + 1) * COLS]
            wall[8 + i, pc.z, pc.y, pc.x] = w2[:, i * COLS : (i + 1) * COLS]
        for p in range(PIECES):
            big.open(p)
    else:
        whole = pltpu.make_async_copy(wall_i, wall, lsem)
        whole.start()

    mask[...] = jnp.full_like(mask, -1e9)
    for i in range(2):
        row = jnp.where(kept[i : i + 1] > 0, 0.0, -1e9)
        for half in range(2):
            mask[i, 0:1, half * PAD : half * PAD + HALF] = row[:, half * HALF : (half + 1) * HALF]

    gcopies = []
    for i in range(2):
        rows = go_ref[i].astype(f32) * live[i].astype(f32)
        start = pl.multiple_of((2 * i + c) * PAD, 16)
        g[pl.ds(start + HALF - 4, PAD - HALF + 4)] = jnp.zeros((PAD - HALF + 4, D), bf16)
        g[pl.ds(start, HALF)] = rows.astype(bf16)
        part = g.at[row_tile(2 * i + c)]
        cp = tensor_copy(pc, part, part, tsem.at[0, i], tsem.at[1, i])
        cp.start()
        gcopies.append(cp)
        xp[i, pl.ds(HALF - 4, PAD - HALF + 4)] = jnp.zeros((PAD - HALF + 4, D), bf16)
        xp[i, pl.ds(0, HALF)] = x_ref[i]

    if comm:
        for dist in range(4):
            at(f"small{dist}")
            small.step(0, dist)
        at("small4")
        small.close(0)
        small.finish()
        blocks = [smalls[0, r // 4, (r // 2) % 2, r % 2] for r in range(GROUP)]
    else:
        blocks = [smalls_in[r] for r in range(GROUP)]
        whole.wait()
    for r in range(GROUP):
        vec[:, r * 64 : (r + 1) * 64] = blocks[r][0:8, 0:64].astype(f32)
    for r in range(GROUP // 2):
        both = jnp.where(c == 0, blocks[r][8:10].astype(f32), blocks[r + GROUP // 2][8:10].astype(f32))
        for i in range(2):
            hb[:, r * 256 + i * 128 : r * 256 + (i + 1) * 128] = both[i : i + 1]

    hcopies = []
    for i in range(2):
        at(f"norm{i}")
        normed, _ = normalize(xp[i].astype(f32))
        h1[row_tile(2 * i + c)] = (normed * vec[0:1] + vec[2:3]).astype(bf16)
        part = h1.at[row_tile(2 * i + c)]
        cp = tensor_copy(pc, part, part, tsem.at[2, i], tsem.at[3, i])
        cp.start()
        hcopies.append(cp)
    for cp in gcopies:
        cp.wait()
    emit(g, g_o, 0)

    def transpose_into(dst, src):
        def body(i):
            cols = pl.ds(pl.multiple_of(i * 128, 128), 128)
            dst[cols, :] = src[:, cols].T

        loop(D // 128, body)

    at("turn_g")
    transpose_into(gT, g)
    at("wait_h")
    for cp in hcopies:
        cp.wait()
    at("turn_h1")
    transpose_into(hT, h1)
    emit(hT, h1t_o, 1)

    qcol = pl.ds(pl.multiple_of(c * COLS, COLS), COLS)
    for p in range(3):
        at(f"need{p}")
        need(p)
        dst = (q, k, v)[p]

        def project(i):
            out = matmul(h1[row_tile(i)], weight(p))
            if p == 0:
                out = (out + vec[3:4, qcol]) * (HEAD_DIM**-0.5)
            elif p == 2:
                out = out + vec[4:5, qcol]
            dst[row_tile(i)] = out.astype(bf16)

        loop(4, project)
        emit(dst, (q_o, k_o, v_o)[p], 2 + p)

    lane = lax.broadcasted_iota(jnp.int32, (1, 128), 1)

    def attend(n):
        img, pair = n // 4, n % 4
        for j in range(8):
            pl.when(n == j)(lambda: at(f"attend{j}"))
        rows = pl.ds(pl.multiple_of(img * SEQ, 16), SEQ)
        cols = pl.ds(pl.multiple_of(pair * 128, 128), 128)
        qb, kb, vb = q[rows, cols], k[rows, cols], v[rows, cols]
        bias = mask[img, 0:1, :]
        mixed = []
        totals = lse[rows]
        for h in range(2):
            mine = (lane >= 64 * h) & (lane < 64 * h + 64)
            s = matmul_nt(jnp.where(mine, qb, jnp.zeros_like(qb)), kb) + bias
            top = jnp.max(s, axis=-1, keepdims=True)
            e = jnp.exp(s - top)
            total = jnp.sum(e, axis=-1, keepdims=True)
            mixed.append(matmul(e.astype(bf16), vb) / total)
            totals = jnp.where(lane == 2 * pair + h, top + jnp.log(total), totals)
        lse[rows] = totals
        o[rows, cols] = jnp.where(lane < 64, mixed[0], mixed[1]).astype(bf16)

    lse[...] = jnp.zeros_like(lse)
    loop(8, attend)
    emit(o, o_o, 5)

    h2 = h1
    at("need3")
    need(3)
    pcopies = []
    for i in range(2):
        other = row_tile(2 * i + 1 - c)
        proj[other] = matmul_nt(o[other], weight(3)).astype(bf16)
        cp = tensor_copy(pc, proj.at[other], precv.at[row_tile(i)], tsem.at[4, i], tsem.at[5, i])
        cp.start()
        pcopies.append(cp)
    at("own3")
    for i in range(2):
        own = row_tile(2 * i + c)
        proj[own] = matmul_nt(o[own], weight(3)).astype(bf16)
    for i in range(2):
        turned = lse[pl.ds(i * SEQ, SEQ)].T
        for h in range(8):
            lse_o[i, h] = turned[h : h + 1]
    for i in range(2):
        at(f"mid{i}")
        pcopies[i].wait()
        own = row_tile(2 * i + c)
        mid = xp[i].astype(f32) + proj[own].astype(f32) + precv[row_tile(i)].astype(f32) + vec[5:6]
        x2[row_tile(i)] = mid
        normed, _ = normalize(mid)
        h2[own] = (normed * vec[1:2] + vec[6:7]).astype(bf16)
        part = h2.at[own]
        cp = tensor_copy(pc, part, part, tsem.at[6, i], tsem.at[7, i])
        cp.start()
        hcopies[i] = cp
    emit(x2, x2_o, 6)

    def mine_first(i):
        return (i % 2) * 2 + jnp.where(i < 2, c, 1 - c)

    for j in range(4):
        at(f"need{4 + j}")
        need(4 + j)
        if j > 1:
            outs.pop(7 + j - 2).wait()

        def up(i):
            rows = row_tile(mine_first(i))
            u = matmul(h2[rows], weight(4 + j)) + hb[:, j * COLS : (j + 1) * COLS]
            gate = 1.0 / (1.0 + jnp.exp(-1.702 * u))
            act[j, rows] = (u * gate).astype(bf16)
            fac[j % 2, rows] = (gate + 1.702 * u * gate * (1.0 - gate)).astype(bf16)

        lax.fori_loop(0, 2, lambda i, z: (up(i), z)[1], 0)
        at(f"half{j}")
        if j == 0:
            for cp in hcopies:
                cp.wait()
        lax.fori_loop(2, 4, lambda i, z: (up(i), z)[1], 0)
        emit(fac.at[j % 2], fac_o.at[j], 7 + j)
    at("turn_h2")
    outs.pop(1).wait()
    transpose_into(hT, h2)
    emit(hT, h2t_o, 1)
    for j in range(4):
        at(f"grad{j}")
        if j > 1:
            outs.pop(11 + j - 2).wait()

        def weight_grad(i):
            rows = pl.ds(pl.multiple_of(i * 256, 256), 256)
            dw[j % 2, i] = matmul(gT[rows, :], act[j]).astype(bf16).reshape(2, 2, 64, COLS)

        loop(4, weight_grad)
        emit(dw.at[j % 2], dw_o.at[j], 11 + j)
    for j in range(4):
        at(f"need{8 + j}")
        need(8 + j)

        def down(i):
            rows = row_tile(i)
            out = matmul_nt(act[j, rows], weight(8 + j))
            if j > 0:
                out = out + acc[rows]
            acc[rows] = out

        if j < 3:
            loop(4, down)
            continue
        for i in range(2):
            down(2 * i + c)
            out = (acc[row_tile(2 * i + c)] + vec[7:8]).astype(bf16)
            for half in range(2):
                proj[pl.ds(half * SEQ + i * PAD, PAD), 0:COLS] = out[:, half * COLS : (half + 1) * COLS]
            down(2 * i + 1 - c)
            out = acc[row_tile(2 * i + 1 - c)].astype(bf16)
            for half in range(2):
                proj[pl.ds(half * SEQ + i * PAD, PAD), COLS:] = out[:, half * COLS : (half + 1) * COLS]
    emit(proj.at[:, pl.ds(0, COLS)], outc_o, 15)
    emit(proj.at[:, pl.ds(COLS, COLS)], outp_o, 16)
    for cp in outs.values():
        cp.wait()
    if comm:
        big.finish()


def forward_call(comm, args):
    B = lambda *s: pltpu.VMEM(s, bf16)
    F = lambda *s: pltpu.VMEM(s, f32)
    S = lambda *s: pltpu.SemaphoreType.DMA(s)
    A = pl.BlockSpec(memory_space=pl.ANY)
    V = pl.BlockSpec(memory_space=pltpu.VMEM)
    M = pl.BlockSpec(memory_space=pltpu.SMEM)
    sh = jax.ShapeDtypeStruct
    outs = [
        sh((D, ROWS), bf16), sh((D, ROWS), bf16), sh((ROWS, D), bf16),
        sh((ROWS, COLS), bf16), sh((ROWS, COLS), bf16), sh((ROWS, COLS), bf16), sh((ROWS, COLS), bf16),
        sh((2, 8, 1, SEQ), f32), sh((2 * PAD, D), f32), sh((4, ROWS, COLS), bf16), sh((4, 4, 2, 2, 64, COLS), bf16),
        sh((ROWS, COLS), bf16), sh((ROWS, COLS), bf16), sh((8, D), f32), sh((2, 8, SEQ), f32),
    ]
    ospecs = [A] * 7 + [V] + [A] * 5 + [V] * 2
    if comm:
        outs = [sh((PIECES, 4, 2, 2, 64, COLS), bf16)] + outs
        ospecs = [A] + ospecs
        ispecs = [V, V, M] + [V] * 8
    else:
        ispecs = [V, V, M, V, A, V]
    scratch = [
        B(PIECES, 4, 2, 2, 64, COLS), B(1, 4, 2, 2, 16, 128), F(16, 128), F(1, 4 * COLS), B(2, PAD, D), B(ROWS, D), B(ROWS, D),
        B(D, ROWS), B(D, ROWS), B(ROWS, COLS), B(ROWS, COLS), B(ROWS, COLS), B(ROWS, COLS),
        F(2 * SEQ, 128), F(2 * PAD, D), B(ROWS, D), B(2 * PAD, D), B(4, ROWS, COLS), B(2, ROWS, COLS),
        B(2, 4, 2, 2, 64, COLS), F(ROWS, D),
        pltpu.SemaphoreType.DMA, S(32), S(8, 2), S(PIECES, 4), S(PIECES, 4), S(PIECES), S(4),
        S(1, 4), S(1, 4), S(1), S(4),
    ]
    return pl.pallas_call(
        functools.partial(forward_kernel, comm),
        out_shape=outs,
        in_specs=ispecs,
        out_specs=ospecs,
        scratch_shapes=scratch,
        name="forward",
        compiler_params=pltpu.CompilerParams(
            collective_id=0, has_side_effects=True, vmem_limit_bytes=62 * 2**20
        ),
    )(*args)


def backward_kernel(comm, *refs):
    x_ref, mask, vec, lse, wall, h1t_i, h2t_i, g_i, q_i, k_i, v_i, o_i, x2_i, fac_i, dw_i, outp_i, outc_i = refs[:17]
    layer_o, input_o = refs[17:19]
    refs = refs[19:]
    if comm:
        gqkv, gout, gfc1, gfc2, gvec, gfc = refs[:6]
        refs = refs[6:]
    else:
        sums_o, vs_o, fcs_o = refs[:3]
        refs = refs[3:]
    (
        sums, r1, r2, rz, rzz, r3, x2, drecv, dx, stage, delta, vs, fcs, vsum, v1, vz, v3, vpart,
        hT, dh2, fac, du, o, w, free,
        lsem, osem, tsem, s1, s2, sz, s3, ss, t1, tz, t3, tt,
    ) = refs
    pc = Place(comm)
    c = pc.c
    pc.greet()
    big = Scatter(pc, sums, BACKWARD_ROUTES, r1, r2, rz, rzz, r3, s1, s2, sz, s3, ss)

    def done(p, value):
        if p < 4:
            gfc2[:, p * COLS : (p + 1) * COLS] = value
        elif p < 8:
            gfc1[:, (p - 4) * COLS : (p - 3) * COLS] = value
        elif p == 8:
            gout[...] = value
        else:
            for i, (which, pair) in enumerate(LATE[p - 9]):
                gqkv[which, :, pair * 128 : (pair + 1) * 128] = value[:, i * 128 : (i + 1) * 128]

    def at(name):
        if not comm:
            return
        for code in BACKWARD_PLAN.get(name, ()):
            p, what = code // 10, code % 10
            if what == 6:
                grads[p].wait()
                big.open(p)
            elif what == 4:
                big.across(p)
            elif what == 5:
                big.close(p, done)
            else:
                big.step(p, what, done)

    def opened(p):
        if comm:
            big.open(p)

    def fetch(src, dst, i):
        cp = pltpu.make_async_copy(src, dst, lsem.at[i])
        cp.start()
        return cp

    def weight(slot):
        return w[slot].reshape(D, COLS)

    grads = [fetch(dw_i.at[j], sums.at[j], (0, 11, 12, 13)[j]) for j in range(4)]
    gcopy = fetch(g_i, dx, 1)
    fcopy = [fetch(fac_i.at[j], fac.at[j], 2 + j) for j in range(2)]
    wcopy = [fetch(wall.at[8], w.at[0], 4), fetch(wall.at[4], w.at[1], 5), fetch(wall.at[9], w.at[2], 6), fetch(wall.at[5], w.at[3], 7)]
    ocopies = []
    for i in range(2):
        cp = tensor_copy(pc, outp_i.at[:, row_tile(i)], drecv.at[:, row_tile(i)], tsem.at[0, i], tsem.at[1, i])
        cp.start()
        ocopies.append(cp)
    x2copy = fetch(x2_i, x2, 8)
    ocopy = fetch(outc_i, o, 9)
    hcopy = fetch(h2t_i, hT, 10)
    vs[...] = jnp.zeros_like(vs)

    def weight_grad(p, right):
        def body(i):
            rows = pl.ds(pl.multiple_of(i * 256, 256), 256)
            sums[p, i] = matmul(hT[rows, :], right().reshape(ROWS, COLS)).astype(bf16).reshape(2, 2, 64, COLS)

        loop(4, body)
        opened(p)

    at("start")
    if not comm:
        for cp in grads:
            cp.wait()
    gcopy.wait()
    sent = []
    for j in range(4):
        fcopy[j % 2].wait()
        wcopy[2 * (j % 2)].wait()
        wcopy[2 * (j % 2) + 1].wait()

        def tile(n, inner=True):
            if inner:
                for m in range(4):
                    pl.when(n == m)(lambda: at(f"tile{4 * j + m}"))
            i = (n % 2) * 2 + jnp.where(n < 2, 1 - c, c)
            rows = row_tile(i)
            da = matmul(dx[rows], weight(2 * (j % 2)))
            du[j, rows] = (da * fac[j % 2, rows].astype(f32)).astype(bf16)
            part = matmul_nt(du[j, rows], weight(2 * (j % 2) + 1))
            if j == 0:
                dh2[rows] = part
            else:
                dh2[rows] += part

        if j < 3:
            loop(4, tile)
        else:
            lax.fori_loop(0, 2, lambda n, z: (tile(n), z)[1], 0)
            pl.semaphore_wait(free, 1)
            for i in range(2):
                for half in range(2):
                    cols = slice(half * COLS, (half + 1) * COLS)
                    o[half, row_tile(i)] = dh2[row_tile(2 * i + 1 - c), cols].astype(bf16)
                cp = tensor_copy(pc, o.at[:, row_tile(i)], drecv.at[:, row_tile(i)], tsem.at[2, i], tsem.at[3, i])
                cp.start()
                sent.append(cp)
            lax.fori_loop(2, 4, lambda n, z: (tile(n), z)[1], 0)
        fcs[:, j * COLS : (j + 1) * COLS] = column_sums(du.at[j])
        if j < 2:
            fcopy[j] = fetch(fac_i.at[j + 2], fac.at[j], 2 + j)
            wcopy[2 * j] = fetch(wall.at[10 + j], w.at[2 * j], 4 + 2 * j)
            wcopy[2 * j + 1] = fetch(wall.at[6 + j], w.at[2 * j + 1], 5 + 2 * j)
        elif j == 2:
            wcopy[0] = fetch(wall.at[0], w.at[0], 4)
            wcopy[1] = fetch(wall.at[1], w.at[1], 5)
        else:
            wcopy[2] = fetch(wall.at[2], w.at[2], 6)
            wcopy[3] = fetch(wall.at[3], w.at[3], 7)
        if j == 0:
            at("layer")
            x2copy.wait()
            ocopy.wait()
            for i in range(2):
                ocopies[i].wait()
                for half in range(2):
                    cols = slice(half * COLS, (half + 1) * COLS)
                    total = (
                        x2[row_tile(i), cols]
                        + o[half, row_tile(i)].astype(f32)
                        + drecv[half, row_tile(i)].astype(f32)
                    )
                    stage[i, :, cols] = total[0:HALF].astype(bf16)
            lcopy = pltpu.make_async_copy(stage, layer_o, osem.at[0])
            lcopy.start()
            pl.semaphore_signal(free, inc=1, device_id=pc.dev("c"), device_id_type=MESH)

    def received(i):
        return jnp.concatenate([drecv[0, row_tile(i)], drecv[1, row_tile(i)]], axis=1).astype(f32)

    at("grad4")
    hcopy.wait()
    weight_grad(4, lambda: du[0])
    copies = []
    for i in range(2):
        at(f"mid{i}")
        sent[i].wait()
        own = row_tile(2 * i + c)
        up = dh2[own] + received(i)
        normed, inverse = normalize(x2[row_tile(i)])
        grad = dx[own].astype(f32)
        total = grad + norm_backward(up, normed, inverse, vec[1:2])
        low = total.astype(bf16)
        x2[row_tile(i)] = total
        dx[own] = low
        cp = tensor_copy(pc, dx.at[own], dx.at[own], tsem.at[4, i], tsem.at[5, i])
        cp.start()
        copies.append(cp)
        vs[5:6] += jnp.sum(up * normed, axis=0, keepdims=True)
        vs[6:7] += jnp.sum(up, axis=0, keepdims=True)
        vs[4:5] += jnp.sum(low.astype(f32), axis=0, keepdims=True)
        vs[7:8] += jnp.sum(grad, axis=0, keepdims=True)
    lcopy.wait()
    xcopy = fetch(x_ref, stage, 8)
    ocopy = fetch(o_i, o, 9)
    for j in range(1, 4):
        at(f"grad{4 + j}")
        weight_grad(4 + j, lambda: du[j])
        if j == 1:
            qcopy = fetch(q_i, du.at[0], 2)
            kcopy = fetch(k_i, du.at[1], 3)
        elif j == 2:
            vcopy = fetch(v_i, du.at[2], 10)
    q, k, v, do = (du.at[i] for i in range(4))
    at("turn")
    for cp in copies:
        cp.wait()

    def turn(i):
        cols = pl.ds(pl.multiple_of(i * 128, 128), 128)
        hT[cols, :] = dx[:, cols].T

    loop(D // 128, turn)
    ocopy.wait()
    weight_grad(8, lambda: o[...])
    hcopy = fetch(h1t_i, hT, 0)
    at("out")
    wcopy[3].wait()

    def out_back(i):
        do[row_tile(i)] = matmul(dx[row_tile(i)], weight(3)).astype(bf16)

    loop(4, out_back)
    at("delta")
    pick = lax.broadcasted_iota(jnp.int32, (8, COLS), 0) == lax.broadcasted_iota(jnp.int32, (8, COLS), 1) // HEAD_DIM
    pick = pick.astype(f32).astype(bf16)
    mcol = dh2.at[:, pl.ds(0, 128)]
    for i in range(2):
        rows = pl.ds(i * SEQ, SEQ)
        prod = do[rows].astype(f32) * o[i].astype(f32)
        high = prod.astype(bf16)
        low = (prod - high.astype(f32)).astype(bf16)
        part = matmul_nt(pick, high) + matmul_nt(pick, low)
        for h in range(8):
            delta[i, h] = part[h : h + 1]
        mcol[rows] = jnp.broadcast_to(mask[i, 0:1], (128, SEQ)).T
    for cp in (qcopy, kcopy, vcopy):
        cp.wait()
    lane = lax.broadcasted_iota(jnp.int32, (1, 128), 1)

    def late_grad(i):
        def right():
            blocks = [(q, k, v)[which][:, pair * 128 : (pair + 1) * 128] for which, pair in LATE[i]]
            return jnp.concatenate(blocks, axis=1)

        weight_grad(9 + i, right)

    def attend(n):
        img, head = n // 2 % 2, 2 * (n // 4) + n % 2

        @pl.when(n == 8)
        def _():
            hcopy.wait()
            at("grad9")
            late_grad(0)

        @pl.when(n == 12)
        def _():
            at("grad10")
            late_grad(1)

        for j in range(16):
            pl.when(n == j)(lambda: at(f"attend{j}"))
        rows = pl.ds(pl.multiple_of(img * SEQ, 16), SEQ)
        cols = pl.ds(pl.multiple_of(head // 2 * 128, 128), 128)
        first = 64 * (head % 2)
        mine = (lane >= first) & (lane < first + 64)
        qb, gb = q[rows, cols], do[rows, cols]
        qm = jnp.where(mine, qb, jnp.zeros_like(qb))
        gm = jnp.where(mine, gb, jnp.zeros_like(gb))
        dq = None
        for t in range(2):
            part = pl.ds(pl.multiple_of(img * SEQ + t * PAD, 16), PAD)
            kb, vb = k[part, cols], v[part, cols]
            p = jnp.exp(matmul_nt(kb, qm) + mcol[part, 0:1] - lse[img, head])
            dp = matmul_nt(vb, gm)
            ds = (p * (dp - delta[img, head])).astype(bf16)
            dv = matmul(p.astype(bf16), gm)
            dk = matmul(ds, qm)
            dqt = matmul_tn(ds, kb)
            dq = dqt if dq is None else dq + dqt
            k[part, cols] = jnp.where(mine, dk.astype(bf16), kb)
            v[part, cols] = jnp.where(mine, dv.astype(bf16), vb)
        q[rows, cols] = jnp.where(mine, (dq * (HEAD_DIM**-0.5)).astype(bf16), qb)

    loop(16, attend)
    at("grad11")
    late_grad(2)
    for i in range(3):
        wcopy[i].wait()

    def back(t):
        rows = row_tile(t)
        total = matmul_nt(q[rows], weight(0))
        total += matmul_nt(k[rows], weight(1))
        total += matmul_nt(v[rows], weight(2))
        return total

    sent = []
    for i in range(2):
        at(f"back{i}")
        part = back(2 * i + 1 - c).astype(bf16)
        for half in range(2):
            o[half, row_tile(i)] = part[:, half * COLS : (half + 1) * COLS]
        cp = tensor_copy(pc, o.at[:, row_tile(i)], drecv.at[:, row_tile(i)], tsem.at[6, i], tsem.at[7, i])
        cp.start()
        sent.append(cp)
    xcopy.wait()
    here = pl.ds(pl.multiple_of(c * COLS, COLS), COLS)
    vs[2:3, here] = column_sums(q)
    vs[3:4, here] = column_sums(v)
    for i in range(2):
        at(f"back{2 + i}")
        up = back(2 * i + c)
        sent[i].wait()
        up = (up + received(i))[0:HALF]
        normed, inverse = normalize(stage[i].astype(f32))
        total = x2[row_tile(i)][0:HALF] + norm_backward(up, normed, inverse, vec[0:1])
        stage[i] = total.astype(bf16)
        vs[0:1] += jnp.sum(up * normed, axis=0, keepdims=True)
        vs[1:2] += jnp.sum(up, axis=0, keepdims=True)
    icopy = pltpu.make_async_copy(stage, input_o, osem.at[1])
    icopy.start()
    if comm:
        at("vectors")
        vsum[...] = jnp.zeros_like(vsum)
        for r in range(GROUP):
            vsum[0, r // 4, (r // 2) % 2, r % 2, 0:8, 0:64] = vs[:, r * 64 : (r + 1) * 64]
        for r in range(GROUP // 2):
            for half in range(2):
                row = fcs[:, (2 * r + half) * 128 : (2 * r + half + 1) * 128]
                for side in range(2):
                    to = r + side * (GROUP // 2)
                    value = jnp.where(c == side, row, jnp.zeros_like(row))
                    vsum[0, to // 4, (to // 2) % 2, to % 2, 8 + half : 9 + half, :] = value
        small = Scatter(pc, vsum, [("P", "x", "y")], v1, None, vz, None, v3, t1, None, tz, t3, tt)
        small.open(0)
        for dist in (3, 2, 1, 0):
            at(f"small{dist}")
            small.step(0, dist, None)

        def keep(p, value):
            vpart[0] = value

        at("small_end")
        small.close(0, keep)
        cp = tensor_copy(pc, vpart.at[0], vpart.at[1], tsem.at[8, 0], tsem.at[9, 0])
        cp.start()
        at("end")
        cp.wait()
        total = vpart[0] + vpart[1]
        gvec[...] = jnp.where(c == 0, total[0:8, 0:32], total[0:8, 32:64])
        gfc[...] = jnp.where(c == 0, total[8:9], total[9:10])
        small.finish()
        big.finish()
    else:
        pairs = ((sums, sums_o), (vs, vs_o), (fcs, fcs_o))
        copies = [pltpu.make_async_copy(a, b, osem.at[2 + i]) for i, (a, b) in enumerate(pairs)]
        for cp in copies:
            cp.start()
        for cp in copies:
            cp.wait()
    icopy.wait()


def backward_call(comm, args):
    B = lambda *s: pltpu.VMEM(s, bf16)
    F = lambda *s: pltpu.VMEM(s, f32)
    S = lambda *s: pltpu.SemaphoreType.DMA(s)
    A = pl.BlockSpec(memory_space=pl.ANY)
    V = pl.BlockSpec(memory_space=pltpu.VMEM)
    sh = jax.ShapeDtypeStruct
    outs = [sh((2, HALF, D), bf16), sh((2, HALF, D), bf16)]
    ospecs = [A, A]
    if comm:
        outs += [
            sh((3, 64, COLS), f32), sh((64, COLS), f32), sh((64, 4 * COLS), f32), sh((64, 4 * COLS), f32),
            sh((8, 32), f32), sh((1, 128), f32),
        ]
        ospecs += [V] * 6
    else:
        outs += [sh((PIECES, 4, 2, 2, 64, COLS), bf16), sh((8, D), f32), sh((1, 4 * COLS), f32)]
        ospecs += [A] * 3
    ispecs = [A, V, V, V] + [A] * 13
    one = (4, 2, 2, 64, COLS)
    scratch = [
        B(PIECES, *one), B(PIECES, 4, 2, 64, COLS), B(4, 4, 64, COLS), B(8, 5, 2, 64, COLS), B(4, 5, 64, COLS),
        B(8, 64, COLS),
        F(2 * PAD, D), B(2, SEQ, COLS), B(ROWS, D), B(2, HALF, D), F(2, 8, 1, SEQ), F(8, D), F(1, 4 * COLS),
        F(1, 4, 2, 2, 16, 128), F(1, 4, 2, 16, 128), F(1, 5, 2, 16, 128), F(1, 16, 128), F(2, 16, 128),
        B(D, ROWS), F(ROWS, D), B(2, ROWS, COLS), B(4, ROWS, COLS), B(2, SEQ, COLS), B(4, *one),
        pltpu.SemaphoreType.REGULAR, S(14), S(5), S(10, 2), S(PIECES, 4), S(4, 4), S(PIECES, 5), S(PIECES), S(4), S(1, 4), S(1, 5), S(1), S(4),
    ]
    return pl.pallas_call(
        functools.partial(backward_kernel, comm),
        out_shape=outs,
        in_specs=ispecs,
        out_specs=ospecs,
        scratch_shapes=scratch,
        name="backward",
        compiler_params=pltpu.CompilerParams(
            collective_id=1, has_side_effects=True, vmem_limit_bytes=63 * 2**20
        ),
    )(*args)


def split_cols(m):
    return jnp.transpose(m.reshape(m.shape[0], m.shape[1] // COLS, COLS), (1, 0, 2))


def shards(layer_in, out_grad, key_valid, image_live, w_qkv, w_out, w_fc1, w_fc2, norm_gains, bias_rows, fc_bias):
    comm = lax.axis_size("dp") == GROUP
    if comm:
        small = (norm_gains, bias_rows, fc_bias.reshape(2, 128))
        made = forward_call(
            True, (layer_in, out_grad, image_live, key_valid, w_qkv, w_out.T, w_fc1, w_fc2.T) + small
        )
        wall, made = made[0], made[1:]
    else:
        local = jnp.concatenate([w_qkv, w_out.T[None], split_cols(w_fc1), split_cols(w_fc2.T)], axis=0)
        wall = lax.all_gather(local, "dp", axis=1, tiled=True).reshape(PIECES, 4, 2, 2, 64, COLS)
        rows = lax.all_gather(jnp.concatenate([norm_gains, bias_rows], axis=0), "dp", axis=1, tiled=True)
        hidden = lax.all_gather(fc_bias, "dp", axis=0, tiled=True)
        small = jnp.pad(jnp.transpose(rows.reshape(8, GROUP, 64), (1, 0, 2)), ((0, 0), (0, 8), (0, 64)))
        small = lax.dynamic_update_slice(small, hidden.reshape(GROUP, 2, 128), (0, 8, 0))
        made = forward_call(False, (layer_in, out_grad, image_live, key_valid, wall, small))
    h1t, h2t, g, q, k, v, o, lse, x2, fac, dw, outp, outc, vec, mask = made
    o, outp, outc = (m.reshape(2, SEQ, COLS) for m in (o, outp, outc))
    back = backward_call(
        comm, (layer_in, mask, vec, lse, wall, h1t, h2t, g, q, k, v, o, x2, fac, dw, outp, outc)
    )
    layer_out, input_grad = back[:2]
    if comm:
        gqkv, gout, gfc1, gfc2, gvec, gfc = back[2:]
        return (layer_out, input_grad, gqkv, gout.T, gfc1, gfc2.T, gvec, gfc.reshape(128))
    sums, vs, fcs = back[2:]
    mine = lax.psum_scatter(sums.reshape(PIECES, D, COLS), "dp", scatter_dimension=1, tiled=True).astype(f32)
    down = jnp.transpose(mine[0:4], (0, 2, 1)).reshape(4 * COLS, -1)
    up = jnp.transpose(mine[4:8], (1, 0, 2)).reshape(-1, 4 * COLS)
    vector = lax.psum_scatter(vs, ("dp", "tensor"), scatter_dimension=1, tiled=True)
    whole = lax.dynamic_update_slice(jnp.zeros((FF,), f32), fcs[0], (lax.axis_index("tensor") * 4 * COLS,))
    hidden = lax.psum_scatter(whole, ("dp", "tensor"), scatter_dimension=0, tiled=True)
    blocks = {
        key: mine[9 + i][:, j * 128 : (j + 1) * 128] for i, keys in enumerate(LATE) for j, key in enumerate(keys)
    }
    qkv = jnp.stack([jnp.concatenate([blocks[(which, pair)] for pair in range(4)], axis=1) for which in range(3)])
    return (layer_out, input_grad, qkv, mine[8].T, up, down, vector, hidden)


def solution(mesh):
    return jax.shard_map(
        shards,
        mesh=mesh,
        in_specs=(
            P("dp", "tensor", None),
            P("dp", "tensor", None),
            P("dp", None),
            P("dp"),
            P(None, "dp", "tensor"),
            P("tensor", "dp"),
            P("dp", "tensor"),
            P("tensor", "dp"),
            P(None, "dp"),
            P(None, "dp"),
            P("dp"),
        ),
        out_specs=(
            P("dp", "tensor", None),
            P("dp", "tensor", None),
            P(None, "dp", "tensor"),
            P("tensor", "dp"),
            P("dp", "tensor"),
            P("tensor", "dp"),
            P(None, ("dp", "tensor")),
            P(("dp", "tensor")),
        ),
        check_vma=False,
    )
```

```python
import functools

import jax
import jax.numpy as jnp
from jax import lax
from jax.experimental import pallas as pl
from jax.experimental.pallas import tpu as pltpu
from jax.sharding import PartitionSpec as P

D = 1024
HEAD_DIM = 64
FF = 4096
EPSILON = 1e-05
MESH = pl.DeviceIdType.MESH
bf16 = jnp.bfloat16
f32 = jnp.float32

PIECES = 12
COLS = 512
HALF = 292
PAD = 304
SEQ = 2 * PAD
ROWS = 4 * PAD
GROUP = 16


def matmul(a, b):
    return lax.dot_general(a, b, (((1,), (0,)), ((), ())), preferred_element_type=f32)


def matmul_nt(a, b):
    return lax.dot_general(a, b, (((1,), (1,)), ((), ())), preferred_element_type=f32)


def matmul_tn(a, b):
    return lax.dot_general(a, b, (((0,), (0,)), ((), ())), preferred_element_type=f32)


def column_sums(ref):
    return matmul(jnp.ones((8, ref.shape[0]), bf16), ref[...])[0:1]


def normalize(values):
    centred = values - jnp.mean(values, axis=-1, keepdims=True)
    inverse = lax.rsqrt(jnp.mean(centred * centred, axis=-1, keepdims=True) + EPSILON)
    return centred * inverse, inverse


def norm_backward(upstream, normed, inverse, gain_row):
    scaled = upstream * gain_row
    return inverse * (
        scaled
        - jnp.mean(scaled, axis=-1, keepdims=True)
        - normed * jnp.mean(scaled * normed, axis=-1, keepdims=True)
    )


class Place:
    def __init__(self, comm):
        self.comm = comm
        self.dp = lax.axis_index("dp")
        self.c = lax.axis_index("tensor")
        self.z = self.dp // 4
        self.y = (self.dp // 2) % 2
        self.x = self.dp % 2

    def dev(self, d):
        if d == "x":
            t = self.dp + 1 - 2 * self.x
        elif d == "y":
            t = self.dp + 2 - 4 * self.y
        elif d == "u":
            t = self.dp + 4
        elif d == "d":
            t = self.dp - 4
        else:
            return (self.dp, 1 - self.c)
        return (t, self.c)

    def greet(self):
        bar = pltpu.get_barrier_semaphore()

        def hail(d):
            pl.semaphore_signal(bar, inc=1, device_id=self.dev(d), device_id_type=MESH)

        hail("c")
        if not self.comm:
            pl.semaphore_wait(bar, 1)
            return
        hail("x")
        hail("y")
        pl.when(self.z < 3)(lambda: hail("u"))
        pl.when(self.z > 0)(lambda: hail("d"))
        pl.when((self.z == 0) | (self.z == 3))(lambda: pl.semaphore_wait(bar, 4))
        pl.when((self.z > 0) & (self.z < 3))(lambda: pl.semaphore_wait(bar, 5))


def wait_bytes(ref, sem):
    pltpu.make_async_copy(ref, ref, sem).wait()


class Gather:
    def __init__(self, pc, wall, routes, zs, fs, ts, ss):
        self.pc, self.wall, self.routes = pc, wall, routes
        self.zs, self.fs, self.ts, self.ss = zs, fs, ts, ss

    def copy(self, ref, d, rsem):
        return pltpu.make_async_remote_copy(
            src_ref=ref,
            dst_ref=ref,
            send_sem=self.ss.at["xyud".index(d)],
            recv_sem=rsem,
            device_id=self.pc.dev(d),
            device_id_type=MESH,
        )

    def block(self, p, zz):
        return self.wall.at[p, zz, self.pc.y, self.pc.x]

    def pair(self, p, zz, d1):
        if d1 == "x":
            return self.wall.at[p, zz, self.pc.y]
        return self.wall.at[p, zz, :, self.pc.x]

    def beside(self, p, zz, d):
        if d == "x":
            return self.wall.at[p, zz, self.pc.y, 1 - self.pc.x]
        return self.wall.at[p, zz, 1 - self.pc.y, self.pc.x]

    def part(self, p, zz):
        kind, d1, _ = self.routes[p]
        return self.block(p, zz) if kind == "Z" else self.pair(p, zz, d1)

    def pass_on(self, p, zz, way):
        cond = self.pc.z < 3 if way == "u" else self.pc.z > 0
        pl.when(cond)(lambda: self.copy(self.part(p, zz), way, self.zs.at[p, zz]).start())

    def to_second(self, p, zz):
        _, d1, d2 = self.routes[p]
        self.copy(self.pair(p, zz, d1), d2, self.ts.at[p]).start()

    def open(self, p):
        kind, d1, d2 = self.routes[p]
        z = self.pc.z
        if kind == "Z":
            self.pass_on(p, z, "u")
            self.pass_on(p, z, "d")
            self.copy(self.block(p, z), d1, self.fs.at[p, z]).start()
        else:
            self.copy(self.block(p, z), d1, self.fs.at[p, 0]).start()

    def first(self, p, zz):
        _, d1, _ = self.routes[p]
        sem = self.fs.at[p, zz] if self.routes[p][0] == "Z" else self.fs.at[p, 0]
        wait_bytes(self.beside(p, zz, d1), sem)

    def step(self, p, dist):
        kind, d1, d2 = self.routes[p]
        z = self.pc.z

        def along(src, way):
            wait_bytes(self.part(p, src), self.zs.at[p, src])
            self.pass_on(p, src, way)
            if kind == "Z":
                self.copy(self.block(p, src), d1, self.fs.at[p, src]).start()
            else:
                self.to_second(p, src)

        def arrived(src):
            self.first(p, src)
            self.to_second(p, src)

        if kind == "P" and dist == 0:
            self.first(p, z)
            self.pass_on(p, z, "u")
            self.pass_on(p, z, "d")
            self.to_second(p, z)
            return
        if 1 <= dist <= 3:
            pl.when(z - dist >= 0)(lambda: along(z - dist, "u"))
            pl.when(z + dist <= 3)(lambda: along(z + dist, "d"))
        if kind == "Z":
            if dist == 1:
                arrived(z)
            elif dist > 1:
                pl.when(z - dist + 1 >= 0)(lambda: arrived(z - dist + 1))
                pl.when(z + dist - 1 <= 3)(lambda: arrived(z + dist - 1))

    def close(self, p):
        d2 = self.routes[p][2]
        if d2 == "y":
            wait_bytes(self.wall.at[p, :, 1 - self.pc.y], self.ts.at[p])
        else:
            wait_bytes(self.wall.at[p, :, :, 1 - self.pc.x], self.ts.at[p])

    def drain(self, n, sem):
        while n >= 16:
            wait_bytes(self.wall.at[0], sem)
            n -= 16
        while n >= 4:
            wait_bytes(self.wall.at[0, 0], sem)
            n -= 4
        while n:
            wait_bytes(self.wall.at[0, 0, 0, 0], sem)
            n -= 1

    def finish(self):
        sent = {"x": 0, "y": 0, "z": 0}
        for kind, d1, d2 in self.routes:
            sent[d1] += 4 if kind == "Z" else 1
            sent[d2] += 8
            sent["z"] += 1 if kind == "Z" else 2
        self.drain(sent["x"], self.ss.at[0])
        self.drain(sent["y"], self.ss.at[1])
        for k in range(3):
            pl.when(self.pc.z == k)(lambda: self.drain(sent["z"] * (k + 1), self.ss.at[2]))
            pl.when(self.pc.z == k + 1)(lambda: self.drain(sent["z"] * (3 - k), self.ss.at[3]))


class Scatter:
    def __init__(self, pc, sums, routes, first, second, line, single, last, s1, s2, sz, s3, ss):
        self.pc, self.sums, self.routes = pc, sums, routes
        self.r1, self.r2, self.rz, self.rzz, self.r3 = first, second, line, single, last
        self.s1, self.s2, self.sz, self.s3, self.ss = s1, s2, sz, s3, ss
        self.rank = [sum(r[0] == "Z" for r in routes[:p]) for p in range(len(routes))]

    def copy(self, src, dst, d, rsem):
        return pltpu.make_async_remote_copy(
            src_ref=src,
            dst_ref=dst,
            send_sem=self.ss.at["xyud".index(d)],
            recv_sem=rsem,
            device_id=self.pc.dev(d),
            device_id_type=MESH,
        )

    def pair(self, p, t, d, other):
        pc = self.pc
        if d == "y":
            return self.sums.at[p, t, (1 - pc.y) if other else pc.y]
        return self.sums.at[p, t, :, (1 - pc.x) if other else pc.x]

    def one(self, p, t, flip=None):
        pc = self.pc
        return self.sums.at[p, t, (1 - pc.y) if flip == "y" else pc.y, (1 - pc.x) if flip == "x" else pc.x]

    def each(self, dist, fn):
        z = self.pc.z
        if dist == 0:
            fn(z, None)
            return
        pl.when(z + dist <= 3)(lambda: fn(z + dist, "u"))
        pl.when(z - dist >= 0)(lambda: fn(z - dist, "d"))

    def add(self, dst, *others):
        total = dst[...]
        for o in others:
            total = total + o[...]
        dst[...] = total

    def open(self, p):
        d2 = self.routes[p][2]
        for dist in (3, 2, 1, 0):
            self.each(
                dist,
                lambda t, _: self.copy(self.pair(p, t, d2, True), self.r1.at[p, t], d2, self.s1.at[p, t]).start(),
            )

    def across(self, p):
        _, d1, d2 = self.routes[p]

        def go(t, _):
            wait_bytes(self.r1.at[p, t], self.s1.at[p, t])
            self.add(self.pair(p, t, d2, False), self.r1.at[p, t])
            self.copy(self.one(p, t, d1), self.r2.at[self.rank[p], t], d1, self.s2.at[self.rank[p], t]).start()

        for dist in (3, 2, 1, 0):
            self.each(dist, go)

    def step(self, p, dist, done):
        kind, d1, d2 = self.routes[p]
        z = self.pc.z
        if kind == "Z":
            view = lambda t: self.one(p, t)
            slot = lambda i: self.rzz.at[self.rank[p], i]
        else:
            view = lambda t: self.pair(p, t, d2, False)
            slot = lambda i: self.rz.at[p - self.rank[p], i]

        def go(t, way):
            if kind == "Z":
                wait_bytes(self.r2.at[self.rank[p], t], self.s2.at[self.rank[p], t])
                mine = self.r2.at[self.rank[p], t]
            else:
                wait_bytes(self.r1.at[p, t], self.s1.at[p, t])
                mine = self.r1.at[p, t]

            def arrival(i):
                wait_bytes(slot(i), self.sz.at[p, i])
                return slot(i)

            if way == "u":
                pl.when(z > 0)(lambda: self.add(view(t), mine, arrival(t + 1)))
                pl.when(z == 0)(lambda: self.add(view(t), mine))
                self.copy(view(t), slot(t + 1), "u", self.sz.at[p, t + 1]).start()
            elif way == "d":
                pl.when(z < 3)(lambda: self.add(view(t), mine, arrival(t)))
                pl.when(z == 3)(lambda: self.add(view(t), mine))
                self.copy(view(t), slot(t), "d", self.sz.at[p, t]).start()
            else:
                pl.when(z == 0)(lambda: self.add(view(z), mine, arrival(z)))
                pl.when(z == 3)(lambda: self.add(view(z), mine, arrival(z + 1)))
                pl.when((z > 0) & (z < 3))(lambda: self.add(view(z), mine, arrival(z), arrival(z + 1)))
                if kind == "Z":
                    done(p, self.one(p, z)[...].astype(f32))
                else:
                    self.copy(self.one(p, z, d1), self.r3.at[p - self.rank[p]], d1, self.s3.at[p]).start()

        self.each(dist, go)

    def close(self, p, done):
        if self.routes[p][0] == "P":
            wait_bytes(self.r3.at[p - self.rank[p]], self.s3.at[p])
            done(p, self.one(p, self.pc.z)[...].astype(f32) + self.r3[p - self.rank[p]].astype(f32))

    def drain(self, n, sem):
        while n >= 16:
            wait_bytes(self.sums.at[0], sem)
            n -= 16
        while n >= 4:
            wait_bytes(self.sums.at[0, 0], sem)
            n -= 4
        while n:
            wait_bytes(self.sums.at[0, 0, 0, 0], sem)
            n -= 1

    def finish(self):
        sent = {"x": 0, "y": 0, "z": 0}
        for kind, d1, d2 in self.routes:
            sent[d1] += 4 if kind == "Z" else 1
            sent[d2] += 8
            sent["z"] += 1 if kind == "Z" else 2
        self.drain(sent["x"], self.ss.at[0])
        self.drain(sent["y"], self.ss.at[1])
        for k in range(3):
            pl.when(self.pc.z == k)(lambda: self.drain(sent["z"] * (3 - k), self.ss.at[2]))
            pl.when(self.pc.z == k + 1)(lambda: self.drain(sent["z"] * (k + 1), self.ss.at[3]))


def row_tile(i):
    return pl.ds(pl.multiple_of(i * PAD, 16), PAD)


def loop(count, body):
    def run(i, carry):
        body(i)
        return carry

    lax.fori_loop(0, count, run, 0)


def tensor_copy(pc, src, dst, send, recv):
    return pltpu.make_async_remote_copy(
        src_ref=src, dst_ref=dst, send_sem=send, recv_sem=recv, device_id=pc.dev("c"), device_id_type=MESH
    )


LATE = (
    ((0, 0), (0, 1), (1, 0), (1, 1)),
    ((2, 0), (2, 1), (2, 2), (0, 2)),
    ((1, 2), (0, 3), (1, 3), (2, 3)),
)

FORWARD_ROUTES = (
    ("Z", "y", "x"),
    ("P", "x", "y"),
    ("P", "y", "x"),
    ("Z", "y", "x"),
    ("Z", "x", "y"),
    ("P", "x", "y"),
    ("P", "y", "x"),
    ("P", "x", "y"),
    ("Z", "x", "y"),
    ("P", "y", "x"),
    ("P", "x", "y"),
    ("P", "y", "x"),
)
FORWARD_PLAN = {
    "small1": (20,),
    "small3": (1,),
    "small4": (10,),
    "norm1": (21, 2, 41, 11,),
    "turn_g": (3, 22, 31, 12, 4, 50, 23, 32,),
    "turn_h1": (60, 13, 100, 70, 42, 51,),
    "attend0": (33,),
    "attend2": (90,),
    "attend3": (81, 34, 52,),
    "attend5": (43,),
    "attend6": (71,),
    "need3": (44, 53, 61,),
    "own3": (72,),
    "mid0": (62,),
    "mid1": (110,),
    "need4": (63,),
    "half0": (82, 73, 91,),
    "half2": (83, 101,),
    "need7": (92,),
    "grad1": (84, 111, 93,),
    "grad2": (102,),
    "need8": (112, 103,),
    "need9": (113,),
}
BACKWARD_ROUTES = (
    ("P", "x", "y"),
    ("P", "x", "y"),
    ("P", "y", "x"),
    ("Z", "y", "x"),
    ("P", "x", "y"),
    ("P", "y", "x"),
    ("Z", "y", "x"),
    ("Z", "x", "y"),
    ("P", "y", "x"),
    ("P", "x", "y"),
    ("P", "y", "x"),
    ("Z", "x", "y"),
)
BACKWARD_PLAN = {
    "layer": (3,),
    "tile7": (23, 2,),
    "tile12": (22,),
    "tile15": (13, 1,),
    "mid1": (21,),
    "grad5": (12,),
    "grad7": (43, 34,),
    "turn": (53,),
    "out": (42,),
    "attend0": (52, 33,),
    "attend1": (11,),
    "attend3": (51,),
    "attend6": (32,),
    "attend7": (41,),
    "attend8": (83, 31,),
    "attend11": (93, 64, 82, 40,),
    "attend12": (20, 92,),
    "attend13": (0,),
    "attend14": (103, 63,),
    "grad11": (81,),
    "back0": (10, 91, 74, 102, 30,),
    "back3": (62,),
    "vectors": (73,),
    "small3": (90, 101,),
    "small2": (114, 72,),
    "small1": (50, 113, 61, 5,),
    "small0": (15, 25, 80, 112, 100, 71,),
    "small_end": (95, 45, 111, 55,),
    "end": (70, 105, 85, 60, 110,),
    "start": (6, 26,),
    "tile3": (16, 36,),
}


def forward_kernel(comm, *refs):
    if comm:
        x_in, go_in, live, kept, wq, wo, w1, w2, gains, shifts, hidden = refs[:11]
        wall_o = refs[11]
        refs = refs[12:]
    else:
        x_in, go_in, live, kept, wall_i, smalls_in = refs[:6]
        refs = refs[6:]
    (
        h1t_o, h2t_o, g_o, q_o, k_o, v_o, o_o, lse_o, x2_o, fac_o, dw_o, outp_o, outc_o, vec, mask,
        wall, smalls, pack, hb, xp, h1, g, gT, hT, q, k, v, o, lse, x2, proj, precv, act, fac, dw, acc,
        x_ref, go_ref, isem,
        lsem, osem, tsem, zs, fs, ts, ss, vzs, vfs, vts, vss,
    ) = refs
    pc = Place(comm)
    c = pc.c
    icopies = [pltpu.make_async_copy(a, b, isem.at[i]) for i, (a, b) in enumerate(((go_in, go_ref), (x_in, x_ref)))]
    for cp in icopies:
        cp.start()
    pc.greet()
    big = Gather(pc, wall, FORWARD_ROUTES, zs, fs, ts, ss)
    outs = {}

    def emit(src, dst, i):
        outs[i] = pltpu.make_async_copy(src, dst, osem.at[i])
        outs[i].start()

    def at(name):
        if comm:
            for code in FORWARD_PLAN.get(name, ()):
                big.step(code // 10, code % 10)

    def need(p):
        if comm:
            big.close(p)
            emit(wall.at[p], wall_o.at[p], 20 + p)

    def weight(p):
        return wall[p].reshape(D, COLS)

    if comm:
        pack[...] = jnp.zeros_like(pack)
        pack[0:2, 0:64] = gains[...].astype(f32)
        pack[2:8, 0:64] = shifts[...].astype(f32)
        pack[8:10] = hidden[...].astype(f32)
        smalls[0, pc.z, pc.y, pc.x] = pack[...].astype(bf16)
        small = Gather(pc, smalls, [("P", "x", "y")], vzs, vfs, vts, vss)
        small.open(0)
        for i in range(3):
            wall[i, pc.z, pc.y, pc.x] = wq[i]
        wall[3, pc.z, pc.y, pc.x] = wo[...]
        for i in range(4):
            wall[4 + i, pc.z, pc.y, pc.x] = w1[:, i * COLS : (i + 1) * COLS]
            wall[8 + i, pc.z, pc.y, pc.x] = w2[:, i * COLS : (i + 1) * COLS]
        for p in range(PIECES):
            big.open(p)
    else:
        whole = pltpu.make_async_copy(wall_i, wall, lsem)
        whole.start()

    mask[...] = jnp.full_like(mask, -1e9)
    for i in range(2):
        row = jnp.where(kept[i : i + 1] > 0, 0.0, -1e9)
        for half in range(2):
            mask[i, 0:1, half * PAD : half * PAD + HALF] = row[:, half * HALF : (half + 1) * HALF]

    for cp in icopies:
        cp.wait()
    gcopies = []
    for i in range(2):
        rows = go_ref[i].astype(f32) * live[i].astype(f32)
        start = pl.multiple_of((2 * i + c) * PAD, 16)
        g[pl.ds(start + HALF - 4, PAD - HALF + 4)] = jnp.zeros((PAD - HALF + 4, D), bf16)
        g[pl.ds(start, HALF)] = rows.astype(bf16)
        part = g.at[row_tile(2 * i + c)]
        cp = tensor_copy(pc, part, part, tsem.at[0, i], tsem.at[1, i])
        cp.start()
        gcopies.append(cp)
        xp[i, pl.ds(HALF - 4, PAD - HALF + 4)] = jnp.zeros((PAD - HALF + 4, D), bf16)
        xp[i, pl.ds(0, HALF)] = x_ref[i]

    if comm:
        for dist in range(4):
            at(f"small{dist}")
            small.step(0, dist)
        at("small4")
        small.close(0)
        small.finish()
        blocks = [smalls[0, r // 4, (r // 2) % 2, r % 2] for r in range(GROUP)]
    else:
        blocks = [smalls_in[r] for r in range(GROUP)]
        whole.wait()
    for r in range(GROUP):
        vec[:, r * 64 : (r + 1) * 64] = blocks[r][0:8, 0:64].astype(f32)
    for r in range(GROUP // 2):
        both = jnp.where(c == 0, blocks[r][8:10].astype(f32), blocks[r + GROUP // 2][8:10].astype(f32))
        for i in range(2):
            hb[:, r * 256 + i * 128 : r * 256 + (i + 1) * 128] = both[i : i + 1]

    hcopies = []
    for i in range(2):
        at(f"norm{i}")
        normed, _ = normalize(xp[i].astype(f32))
        h1[row_tile(2 * i + c)] = (normed * vec[0:1] + vec[2:3]).astype(bf16)
        part = h1.at[row_tile(2 * i + c)]
        cp = tensor_copy(pc, part, part, tsem.at[2, i], tsem.at[3, i])
        cp.start()
        hcopies.append(cp)
    for cp in gcopies:
        cp.wait()
    emit(g, g_o, 0)

    def transpose_into(dst, src):
        def body(i):
            cols = pl.ds(pl.multiple_of(i * 128, 128), 128)
            dst[cols, :] = src[:, cols].T

        loop(D // 128, body)

    at("turn_g")
    transpose_into(gT, g)
    at("wait_h")
    for cp in hcopies:
        cp.wait()
    at("turn_h1")
    transpose_into(hT, h1)
    emit(hT, h1t_o, 1)

    qcol = pl.ds(pl.multiple_of(c * COLS, COLS), COLS)
    for p in range(3):
        at(f"need{p}")
        need(p)
        dst = (q, k, v)[p]

        def project(i):
            out = matmul(h1[row_tile(i)], weight(p))
            if p == 0:
                out = (out + vec[3:4, qcol]) * (HEAD_DIM**-0.5)
            elif p == 2:
                out = out + vec[4:5, qcol]
            dst[row_tile(i)] = out.astype(bf16)

        loop(4, project)
        emit(dst, (q_o, k_o, v_o)[p], 2 + p)

    lane = lax.broadcasted_iota(jnp.int32, (1, 128), 1)

    def attend(n):
        img, pair = n // 4, n % 4
        for j in range(8):
            pl.when(n == j)(lambda: at(f"attend{j}"))
        rows = pl.ds(pl.multiple_of(img * SEQ, 16), SEQ)
        cols = pl.ds(pl.multiple_of(pair * 128, 128), 128)
        qb, kb, vb = q[rows, cols], k[rows, cols], v[rows, cols]
        bias = mask[img, 0:1, :]
        mixed = []
        totals = lse[rows]
        for h in range(2):
            mine = (lane >= 64 * h) & (lane < 64 * h + 64)
            s = matmul_nt(jnp.where(mine, qb, jnp.zeros_like(qb)), kb) + bias
            top = jnp.max(s, axis=-1, keepdims=True)
            e = jnp.exp(s - top)
            total = jnp.sum(e, axis=-1, keepdims=True)
            mixed.append(matmul(e.astype(bf16), vb) / total)
            totals = jnp.where(lane == 2 * pair + h, top + jnp.log(total), totals)
        lse[rows] = totals
        o[rows, cols] = jnp.where(lane < 64, mixed[0], mixed[1]).astype(bf16)

    lse[...] = jnp.zeros_like(lse)
    loop(8, attend)
    emit(o, o_o, 5)

    h2 = h1
    at("need3")
    need(3)
    pcopies = []
    for i in range(2):
        other = row_tile(2 * i + 1 - c)
        proj[other] = matmul_nt(o[other], weight(3)).astype(bf16)
        cp = tensor_copy(pc, proj.at[other], precv.at[row_tile(i)], tsem.at[4, i], tsem.at[5, i])
        cp.start()
        pcopies.append(cp)
    at("own3")
    for i in range(2):
        own = row_tile(2 * i + c)
        proj[own] = matmul_nt(o[own], weight(3)).astype(bf16)
    for i in range(2):
        turned = lse[pl.ds(i * SEQ, SEQ)].T
        for h in range(8):
            lse_o[i, h] = turned[h : h + 1]
    for i in range(2):
        at(f"mid{i}")
        pcopies[i].wait()
        own = row_tile(2 * i + c)
        mid = xp[i].astype(f32) + proj[own].astype(f32) + precv[row_tile(i)].astype(f32) + vec[5:6]
        x2[row_tile(i)] = mid
        normed, _ = normalize(mid)
        h2[own] = (normed * vec[1:2] + vec[6:7]).astype(bf16)
        part = h2.at[own]
        cp = tensor_copy(pc, part, part, tsem.at[6, i], tsem.at[7, i])
        cp.start()
        hcopies[i] = cp
    emit(x2, x2_o, 6)

    def mine_first(i):
        return (i % 2) * 2 + jnp.where(i < 2, c, 1 - c)

    for j in range(4):
        at(f"need{4 + j}")
        need(4 + j)
        if j > 1:
            outs.pop(7 + j - 2).wait()

        def up(i):
            rows = row_tile(mine_first(i))
            u = matmul(h2[rows], weight(4 + j)) + hb[:, j * COLS : (j + 1) * COLS]
            gate = 1.0 / (1.0 + jnp.exp(-1.702 * u))
            act[j, rows] = (u * gate).astype(bf16)
            fac[j % 2, rows] = (gate + 1.702 * u * gate * (1.0 - gate)).astype(bf16)

        lax.fori_loop(0, 2, lambda i, z: (up(i), z)[1], 0)
        at(f"half{j}")
        if j == 0:
            for cp in hcopies:
                cp.wait()
        lax.fori_loop(2, 4, lambda i, z: (up(i), z)[1], 0)
        emit(fac.at[j % 2], fac_o.at[j], 7 + j)
    at("turn_h2")
    outs.pop(1).wait()
    transpose_into(hT, h2)
    emit(hT, h2t_o, 1)
    for j in range(4):
        at(f"grad{j}")
        if j > 1:
            outs.pop(11 + j - 2).wait()

        def weight_grad(i):
            rows = pl.ds(pl.multiple_of(i * 256, 256), 256)
            dw[j % 2, i] = matmul(gT[rows, :], act[j]).astype(bf16).reshape(2, 2, 64, COLS)

        loop(4, weight_grad)
        emit(dw.at[j % 2], dw_o.at[j], 11 + j)
    for j in range(4):
        at(f"need{8 + j}")
        need(8 + j)

        def down(i):
            rows = row_tile(i)
            out = matmul_nt(act[j, rows], weight(8 + j))
            if j > 0:
                out = out + acc[rows]
            acc[rows] = out

        if j < 3:
            loop(4, down)
            continue
        for i in range(2):
            down(2 * i + c)
            out = (acc[row_tile(2 * i + c)] + vec[7:8]).astype(bf16)
            for half in range(2):
                proj[pl.ds(half * SEQ + i * PAD, PAD), 0:COLS] = out[:, half * COLS : (half + 1) * COLS]
            down(2 * i + 1 - c)
            out = acc[row_tile(2 * i + 1 - c)].astype(bf16)
            for half in range(2):
                proj[pl.ds(half * SEQ + i * PAD, PAD), COLS:] = out[:, half * COLS : (half + 1) * COLS]
    emit(proj.at[:, pl.ds(0, COLS)], outc_o, 15)
    emit(proj.at[:, pl.ds(COLS, COLS)], outp_o, 16)
    for cp in outs.values():
        cp.wait()
    if comm:
        big.finish()


def forward_call(comm, args):
    B = lambda *s: pltpu.VMEM(s, bf16)
    F = lambda *s: pltpu.VMEM(s, f32)
    S = lambda *s: pltpu.SemaphoreType.DMA(s)
    A = pl.BlockSpec(memory_space=pl.ANY)
    V = pl.BlockSpec(memory_space=pltpu.VMEM)
    M = pl.BlockSpec(memory_space=pltpu.SMEM)
    sh = jax.ShapeDtypeStruct
    outs = [
        sh((D, ROWS), bf16), sh((D, ROWS), bf16), sh((ROWS, D), bf16),
        sh((ROWS, COLS), bf16), sh((ROWS, COLS), bf16), sh((ROWS, COLS), bf16), sh((ROWS, COLS), bf16),
        sh((2, 8, 1, SEQ), f32), sh((2 * PAD, D), f32), sh((4, ROWS, COLS), bf16), sh((4, 4, 2, 2, 64, COLS), bf16),
        sh((ROWS, COLS), bf16), sh((ROWS, COLS), bf16), sh((8, D), f32), sh((2, 8, SEQ), f32),
    ]
    ospecs = [A] * 7 + [V] + [A] * 5 + [V] * 2
    if comm:
        outs = [sh((PIECES, 4, 2, 2, 64, COLS), bf16)] + outs
        ospecs = [A] + ospecs
        ispecs = [A, A, M] + [V] * 8
    else:
        ispecs = [A, A, M, V, A, V]
    scratch = [
        B(PIECES, 4, 2, 2, 64, COLS), B(1, 4, 2, 2, 16, 128), F(16, 128), F(1, 4 * COLS), B(2, PAD, D), B(ROWS, D), B(ROWS, D),
        B(D, ROWS), B(D, ROWS), B(ROWS, COLS), B(ROWS, COLS), B(ROWS, COLS), B(ROWS, COLS),
        F(2 * SEQ, 128), F(2 * PAD, D), B(ROWS, D), B(2 * PAD, D), B(4, ROWS, COLS), B(2, ROWS, COLS),
        B(2, 4, 2, 2, 64, COLS), F(ROWS, D),
        B(2, HALF, D), B(2, HALF, D), S(2),
        pltpu.SemaphoreType.DMA, S(32), S(8, 2), S(PIECES, 4), S(PIECES, 4), S(PIECES), S(4),
        S(1, 4), S(1, 4), S(1), S(4),
    ]
    return pl.pallas_call(
        functools.partial(forward_kernel, comm),
        out_shape=outs,
        in_specs=ispecs,
        out_specs=ospecs,
        scratch_shapes=scratch,
        name="forward",
        compiler_params=pltpu.CompilerParams(
            collective_id=0, has_side_effects=True, vmem_limit_bytes=62 * 2**20
        ),
    )(*args)


def backward_kernel(comm, *refs):
    x_ref, mask, vec, lse, wall, h1t_i, h2t_i, g_i, q_i, k_i, v_i, o_i, x2_i, fac_i, dw_i, outp_i, outc_i = refs[:17]
    layer_o, input_o = refs[17:19]
    refs = refs[19:]
    if comm:
        gqkv, gout, gfc1, gfc2, gvec, gfc = refs[:6]
        refs = refs[6:]
    else:
        sums_o, vs_o, fcs_o = refs[:3]
        refs = refs[3:]
    (
        sums, r1, r2, rz, rzz, r3, x2, drecv, dx, stage, delta, vs, fcs, vsum, v1, vz, v3, vpart,
        hT, dh2, fac, du, o, w, free,
        lsem, osem, tsem, s1, s2, sz, s3, ss, t1, tz, t3, tt,
    ) = refs
    pc = Place(comm)
    c = pc.c
    pc.greet()
    big = Scatter(pc, sums, BACKWARD_ROUTES, r1, r2, rz, rzz, r3, s1, s2, sz, s3, ss)

    def done(p, value):
        if p < 4:
            gfc2[:, p * COLS : (p + 1) * COLS] = value
        elif p < 8:
            gfc1[:, (p - 4) * COLS : (p - 3) * COLS] = value
        elif p == 8:
            gout[...] = value
        else:
            for i, (which, pair) in enumerate(LATE[p - 9]):
                gqkv[which, :, pair * 128 : (pair + 1) * 128] = value[:, i * 128 : (i + 1) * 128]

    def at(name):
        if not comm:
            return
        for code in BACKWARD_PLAN.get(name, ()):
            p, what = code // 10, code % 10
            if what == 6:
                grads[p].wait()
                big.open(p)
            elif what == 4:
                big.across(p)
            elif what == 5:
                big.close(p, done)
            else:
                big.step(p, what, done)

    def opened(p):
        if comm:
            big.open(p)

    def fetch(src, dst, i):
        cp = pltpu.make_async_copy(src, dst, lsem.at[i])
        cp.start()
        return cp

    def weight(slot):
        return w[slot].reshape(D, COLS)

    grads = [fetch(dw_i.at[j], sums.at[j], (0, 11, 12, 13)[j]) for j in range(4)]
    gcopy = fetch(g_i, dx, 1)
    fcopy = [fetch(fac_i.at[j], fac.at[j], 2 + j) for j in range(2)]
    wcopy = [fetch(wall.at[8], w.at[0], 4), fetch(wall.at[4], w.at[1], 5), fetch(wall.at[9], w.at[2], 6), fetch(wall.at[5], w.at[3], 7)]
    ocopies = []
    for i in range(2):
        cp = tensor_copy(pc, outp_i.at[:, row_tile(i)], drecv.at[:, row_tile(i)], tsem.at[0, i], tsem.at[1, i])
        cp.start()
        ocopies.append(cp)
    x2copy = fetch(x2_i, x2, 8)
    ocopy = fetch(outc_i, o, 9)
    hcopy = fetch(h2t_i, hT, 10)
    vs[...] = jnp.zeros_like(vs)

    def weight_grad(p, right):
        def body(i):
            rows = pl.ds(pl.multiple_of(i * 256, 256), 256)
            sums[p, i] = matmul(hT[rows, :], right().reshape(ROWS, COLS)).astype(bf16).reshape(2, 2, 64, COLS)

        loop(4, body)
        opened(p)

    at("start")
    if not comm:
        for cp in grads:
            cp.wait()
    gcopy.wait()
    sent = []
    for j in range(4):
        fcopy[j % 2].wait()
        wcopy[2 * (j % 2)].wait()
        wcopy[2 * (j % 2) + 1].wait()

        def tile(n, inner=True):
            if inner:
                for m in range(4):
                    pl.when(n == m)(lambda: at(f"tile{4 * j + m}"))
            i = (n % 2) * 2 + jnp.where(n < 2, 1 - c, c)
            rows = row_tile(i)
            da = matmul(dx[rows], weight(2 * (j % 2)))
            du[j, rows] = (da * fac[j % 2, rows].astype(f32)).astype(bf16)
            part = matmul_nt(du[j, rows], weight(2 * (j % 2) + 1))
            if j == 0:
                dh2[rows] = part
            else:
                dh2[rows] += part

        if j < 3:
            loop(4, tile)
        else:
            lax.fori_loop(0, 2, lambda n, z: (tile(n), z)[1], 0)
            pl.semaphore_wait(free, 1)
            for i in range(2):
                for half in range(2):
                    cols = slice(half * COLS, (half + 1) * COLS)
                    o[half, row_tile(i)] = dh2[row_tile(2 * i + 1 - c), cols].astype(bf16)
                cp = tensor_copy(pc, o.at[:, row_tile(i)], drecv.at[:, row_tile(i)], tsem.at[2, i], tsem.at[3, i])
                cp.start()
                sent.append(cp)
            lax.fori_loop(2, 4, lambda n, z: (tile(n), z)[1], 0)
        fcs[:, j * COLS : (j + 1) * COLS] = column_sums(du.at[j])
        if j < 2:
            fcopy[j] = fetch(fac_i.at[j + 2], fac.at[j], 2 + j)
            wcopy[2 * j] = fetch(wall.at[10 + j], w.at[2 * j], 4 + 2 * j)
            wcopy[2 * j + 1] = fetch(wall.at[6 + j], w.at[2 * j + 1], 5 + 2 * j)
        elif j == 2:
            wcopy[0] = fetch(wall.at[0], w.at[0], 4)
            wcopy[1] = fetch(wall.at[1], w.at[1], 5)
        else:
            wcopy[2] = fetch(wall.at[2], w.at[2], 6)
            wcopy[3] = fetch(wall.at[3], w.at[3], 7)
        if j == 0:
            at("layer")
            x2copy.wait()
            ocopy.wait()
            for i in range(2):
                ocopies[i].wait()
                for half in range(2):
                    cols = slice(half * COLS, (half + 1) * COLS)
                    total = (
                        x2[row_tile(i), cols]
                        + o[half, row_tile(i)].astype(f32)
                        + drecv[half, row_tile(i)].astype(f32)
                    )
                    stage[i, :, cols] = total[0:HALF].astype(bf16)
            lcopy = pltpu.make_async_copy(stage, layer_o, osem.at[0])
            lcopy.start()
            pl.semaphore_signal(free, inc=1, device_id=pc.dev("c"), device_id_type=MESH)

    def received(i):
        return jnp.concatenate([drecv[0, row_tile(i)], drecv[1, row_tile(i)]], axis=1).astype(f32)

    at("grad4")
    hcopy.wait()
    weight_grad(4, lambda: du[0])
    copies = []
    for i in range(2):
        at(f"mid{i}")
        sent[i].wait()
        own = row_tile(2 * i + c)
        up = dh2[own] + received(i)
        normed, inverse = normalize(x2[row_tile(i)])
        grad = dx[own].astype(f32)
        total = grad + norm_backward(up, normed, inverse, vec[1:2])
        low = total.astype(bf16)
        x2[row_tile(i)] = total
        dx[own] = low
        cp = tensor_copy(pc, dx.at[own], dx.at[own], tsem.at[4, i], tsem.at[5, i])
        cp.start()
        copies.append(cp)
        vs[5:6] += jnp.sum(up * normed, axis=0, keepdims=True)
        vs[6:7] += jnp.sum(up, axis=0, keepdims=True)
        vs[4:5] += jnp.sum(low.astype(f32), axis=0, keepdims=True)
        vs[7:8] += jnp.sum(grad, axis=0, keepdims=True)
    lcopy.wait()
    xcopy = fetch(x_ref, stage, 8)
    ocopy = fetch(o_i, o, 9)
    for j in range(1, 4):
        at(f"grad{4 + j}")
        weight_grad(4 + j, lambda: du[j])
        if j == 1:
            qcopy = fetch(q_i, du.at[0], 2)
            kcopy = fetch(k_i, du.at[1], 3)
        elif j == 2:
            vcopy = fetch(v_i, du.at[2], 10)
    q, k, v, do = (du.at[i] for i in range(4))
    at("turn")
    for cp in copies:
        cp.wait()

    def turn(i):
        cols = pl.ds(pl.multiple_of(i * 128, 128), 128)
        hT[cols, :] = dx[:, cols].T

    loop(D // 128, turn)
    ocopy.wait()
    weight_grad(8, lambda: o[...])
    hcopy = fetch(h1t_i, hT, 0)
    at("out")
    wcopy[3].wait()

    def out_back(i):
        do[row_tile(i)] = matmul(dx[row_tile(i)], weight(3)).astype(bf16)

    loop(4, out_back)
    at("delta")
    pick = lax.broadcasted_iota(jnp.int32, (8, COLS), 0) == lax.broadcasted_iota(jnp.int32, (8, COLS), 1) // HEAD_DIM
    pick = pick.astype(f32).astype(bf16)
    mcol = dh2.at[:, pl.ds(0, 128)]
    for i in range(2):
        rows = pl.ds(i * SEQ, SEQ)
        prod = do[rows].astype(f32) * o[i].astype(f32)
        high = prod.astype(bf16)
        low = (prod - high.astype(f32)).astype(bf16)
        part = matmul_nt(pick, high) + matmul_nt(pick, low)
        for h in range(8):
            delta[i, h] = part[h : h + 1]
        mcol[rows] = jnp.broadcast_to(mask[i, 0:1], (128, SEQ)).T
    for cp in (qcopy, kcopy, vcopy):
        cp.wait()
    lane = lax.broadcasted_iota(jnp.int32, (1, 128), 1)

    def late_grad(i):
        def right():
            blocks = [(q, k, v)[which][:, pair * 128 : (pair + 1) * 128] for which, pair in LATE[i]]
            return jnp.concatenate(blocks, axis=1)

        weight_grad(9 + i, right)

    def attend(n):
        img, head = n // 2 % 2, 2 * (n // 4) + n % 2

        @pl.when(n == 8)
        def _():
            hcopy.wait()
            at("grad9")
            late_grad(0)

        @pl.when(n == 12)
        def _():
            at("grad10")
            late_grad(1)

        for j in range(16):
            pl.when(n == j)(lambda: at(f"attend{j}"))
        rows = pl.ds(pl.multiple_of(img * SEQ, 16), SEQ)
        cols = pl.ds(pl.multiple_of(head // 2 * 128, 128), 128)
        first = 64 * (head % 2)
        mine = (lane >= first) & (lane < first + 64)
        qb, gb = q[rows, cols], do[rows, cols]
        qm = jnp.where(mine, qb, jnp.zeros_like(qb))
        gm = jnp.where(mine, gb, jnp.zeros_like(gb))
        dq = None
        for t in range(2):
            part = pl.ds(pl.multiple_of(img * SEQ + t * PAD, 16), PAD)
            kb, vb = k[part, cols], v[part, cols]
            p = jnp.exp(matmul_nt(kb, qm) + mcol[part, 0:1] - lse[img, head])
            dp = matmul_nt(vb, gm)
            ds = (p * (dp - delta[img, head])).astype(bf16)
            dv = matmul(p.astype(bf16), gm)
            dk = matmul(ds, qm)
            dqt = matmul_tn(ds, kb)
            dq = dqt if dq is None else dq + dqt
            k[part, cols] = jnp.where(mine, dk.astype(bf16), kb)
            v[part, cols] = jnp.where(mine, dv.astype(bf16), vb)
        q[rows, cols] = jnp.where(mine, (dq * (HEAD_DIM**-0.5)).astype(bf16), qb)

    loop(16, attend)
    at("grad11")
    late_grad(2)
    for i in range(3):
        wcopy[i].wait()

    def back(t):
        rows = row_tile(t)
        total = matmul_nt(q[rows], weight(0))
        total += matmul_nt(k[rows], weight(1))
        total += matmul_nt(v[rows], weight(2))
        return total

    sent = []
    for i in range(2):
        at(f"back{i}")
        part = back(2 * i + 1 - c).astype(bf16)
        for half in range(2):
            o[half, row_tile(i)] = part[:, half * COLS : (half + 1) * COLS]
        cp = tensor_copy(pc, o.at[:, row_tile(i)], drecv.at[:, row_tile(i)], tsem.at[6, i], tsem.at[7, i])
        cp.start()
        sent.append(cp)
    xcopy.wait()
    here = pl.ds(pl.multiple_of(c * COLS, COLS), COLS)
    vs[2:3, here] = column_sums(q)
    vs[3:4, here] = column_sums(v)
    for i in range(2):
        at(f"back{2 + i}")
        up = back(2 * i + c)
        sent[i].wait()
        up = (up + received(i))[0:HALF]
        normed, inverse = normalize(stage[i].astype(f32))
        total = x2[row_tile(i)][0:HALF] + norm_backward(up, normed, inverse, vec[0:1])
        stage[i] = total.astype(bf16)
        vs[0:1] += jnp.sum(up * normed, axis=0, keepdims=True)
        vs[1:2] += jnp.sum(up, axis=0, keepdims=True)
    icopy = pltpu.make_async_copy(stage, input_o, osem.at[1])
    icopy.start()
    if comm:
        at("vectors")
        vsum[...] = jnp.zeros_like(vsum)
        for r in range(GROUP):
            vsum[0, r // 4, (r // 2) % 2, r % 2, 0:8, 0:64] = vs[:, r * 64 : (r + 1) * 64]
        for r in range(GROUP // 2):
            for half in range(2):
                row = fcs[:, (2 * r + half) * 128 : (2 * r + half + 1) * 128]
                for side in range(2):
                    to = r + side * (GROUP // 2)
                    value = jnp.where(c == side, row, jnp.zeros_like(row))
                    vsum[0, to // 4, (to // 2) % 2, to % 2, 8 + half : 9 + half, :] = value
        small = Scatter(pc, vsum, [("P", "x", "y")], v1, None, vz, None, v3, t1, None, tz, t3, tt)
        small.open(0)
        for dist in (3, 2, 1, 0):
            at(f"small{dist}")
            small.step(0, dist, None)

        def keep(p, value):
            vpart[0] = value

        at("small_end")
        small.close(0, keep)
        cp = tensor_copy(pc, vpart.at[0], vpart.at[1], tsem.at[8, 0], tsem.at[9, 0])
        cp.start()
        at("end")
        cp.wait()
        total = vpart[0] + vpart[1]
        gvec[...] = jnp.where(c == 0, total[0:8, 0:32], total[0:8, 32:64])
        gfc[...] = jnp.where(c == 0, total[8:9], total[9:10])
        small.finish()
        big.finish()
    else:
        pairs = ((sums, sums_o), (vs, vs_o), (fcs, fcs_o))
        copies = [pltpu.make_async_copy(a, b, osem.at[2 + i]) for i, (a, b) in enumerate(pairs)]
        for cp in copies:
            cp.start()
        for cp in copies:
            cp.wait()
    icopy.wait()


def backward_call(comm, args):
    B = lambda *s: pltpu.VMEM(s, bf16)
    F = lambda *s: pltpu.VMEM(s, f32)
    S = lambda *s: pltpu.SemaphoreType.DMA(s)
    A = pl.BlockSpec(memory_space=pl.ANY)
    V = pl.BlockSpec(memory_space=pltpu.VMEM)
    sh = jax.ShapeDtypeStruct
    outs = [sh((2, HALF, D), bf16), sh((2, HALF, D), bf16)]
    ospecs = [A, A]
    if comm:
        outs += [
            sh((3, 64, COLS), f32), sh((64, COLS), f32), sh((64, 4 * COLS), f32), sh((64, 4 * COLS), f32),
            sh((8, 32), f32), sh((1, 128), f32),
        ]
        ospecs += [V] * 6
    else:
        outs += [sh((PIECES, 4, 2, 2, 64, COLS), bf16), sh((8, D), f32), sh((1, 4 * COLS), f32)]
        ospecs += [A] * 3
    ispecs = [A, V, V, V] + [A] * 13
    one = (4, 2, 2, 64, COLS)
    scratch = [
        B(PIECES, *one), B(PIECES, 4, 2, 64, COLS), B(4, 4, 64, COLS), B(8, 5, 2, 64, COLS), B(4, 5, 64, COLS),
        B(8, 64, COLS),
        F(2 * PAD, D), B(2, SEQ, COLS), B(ROWS, D), B(2, HALF, D), F(2, 8, 1, SEQ), F(8, D), F(1, 4 * COLS),
        F(1, 4, 2, 2, 16, 128), F(1, 4, 2, 16, 128), F(1, 5, 2, 16, 128), F(1, 16, 128), F(2, 16, 128),
        B(D, ROWS), F(ROWS, D), B(2, ROWS, COLS), B(4, ROWS, COLS), B(2, SEQ, COLS), B(4, *one),
        pltpu.SemaphoreType.REGULAR, S(14), S(5), S(10, 2), S(PIECES, 4), S(4, 4), S(PIECES, 5), S(PIECES), S(4), S(1, 4), S(1, 5), S(1), S(4),
    ]
    return pl.pallas_call(
        functools.partial(backward_kernel, comm),
        out_shape=outs,
        in_specs=ispecs,
        out_specs=ospecs,
        scratch_shapes=scratch,
        name="backward",
        compiler_params=pltpu.CompilerParams(
            collective_id=1, has_side_effects=True, vmem_limit_bytes=63 * 2**20
        ),
    )(*args)


def split_cols(m):
    return jnp.transpose(m.reshape(m.shape[0], m.shape[1] // COLS, COLS), (1, 0, 2))


def shards(layer_in, out_grad, key_valid, image_live, w_qkv, w_out, w_fc1, w_fc2, norm_gains, bias_rows, fc_bias):
    comm = lax.axis_size("dp") == GROUP
    if comm:
        small = (norm_gains, bias_rows, fc_bias.reshape(2, 128))
        made = forward_call(
            True, (layer_in, out_grad, image_live, key_valid, w_qkv, w_out.T, w_fc1, w_fc2.T) + small
        )
        wall, made = made[0], made[1:]
    else:
        local = jnp.concatenate([w_qkv, w_out.T[None], split_cols(w_fc1), split_cols(w_fc2.T)], axis=0)
        wall = lax.all_gather(local, "dp", axis=1, tiled=True).reshape(PIECES, 4, 2, 2, 64, COLS)
        rows = lax.all_gather(jnp.concatenate([norm_gains, bias_rows], axis=0), "dp", axis=1, tiled=True)
        hidden = lax.all_gather(fc_bias, "dp", axis=0, tiled=True)
        small = jnp.pad(jnp.transpose(rows.reshape(8, GROUP, 64), (1, 0, 2)), ((0, 0), (0, 8), (0, 64)))
        small = lax.dynamic_update_slice(small, hidden.reshape(GROUP, 2, 128), (0, 8, 0))
        made = forward_call(False, (layer_in, out_grad, image_live, key_valid, wall, small))
    h1t, h2t, g, q, k, v, o, lse, x2, fac, dw, outp, outc, vec, mask = made
    o, outp, outc = (m.reshape(2, SEQ, COLS) for m in (o, outp, outc))
    back = backward_call(
        comm, (layer_in, mask, vec, lse, wall, h1t, h2t, g, q, k, v, o, x2, fac, dw, outp, outc)
    )
    layer_out, input_grad = back[:2]
    if comm:
        gqkv, gout, gfc1, gfc2, gvec, gfc = back[2:]
        return (layer_out, input_grad, gqkv, gout.T, gfc1, gfc2.T, gvec, gfc.reshape(128))
    sums, vs, fcs = back[2:]
    mine = lax.psum_scatter(sums.reshape(PIECES, D, COLS), "dp", scatter_dimension=1, tiled=True).astype(f32)
    down = jnp.transpose(mine[0:4], (0, 2, 1)).reshape(4 * COLS, -1)
    up = jnp.transpose(mine[4:8], (1, 0, 2)).reshape(-1, 4 * COLS)
    vector = lax.psum_scatter(vs, ("dp", "tensor"), scatter_dimension=1, tiled=True)
    whole = lax.dynamic_update_slice(jnp.zeros((FF,), f32), fcs[0], (lax.axis_index("tensor") * 4 * COLS,))
    hidden = lax.psum_scatter(whole, ("dp", "tensor"), scatter_dimension=0, tiled=True)
    blocks = {
        key: mine[9 + i][:, j * 128 : (j + 1) * 128] for i, keys in enumerate(LATE) for j, key in enumerate(keys)
    }
    qkv = jnp.stack([jnp.concatenate([blocks[(which, pair)] for pair in range(4)], axis=1) for which in range(3)])
    return (layer_out, input_grad, qkv, mine[8].T, up, down, vector, hidden)


def solution(mesh):
    return jax.shard_map(
        shards,
        mesh=mesh,
        in_specs=(
            P("dp", "tensor", None),
            P("dp", "tensor", None),
            P("dp", None),
            P("dp"),
            P(None, "dp", "tensor"),
            P("tensor", "dp"),
            P("dp", "tensor"),
            P("tensor", "dp"),
            P(None, "dp"),
            P(None, "dp"),
            P("dp"),
        ),
        out_specs=(
            P("dp", "tensor", None),
            P("dp", "tensor", None),
            P(None, "dp", "tensor"),
            P("tensor", "dp"),
            P("dp", "tensor"),
            P("tensor", "dp"),
            P(None, ("dp", "tensor")),
            P(("dp", "tensor")),
        ),
        check_vma=False,
    )
```
